512 devices in a mesh: fsdp: 32 (over z, y_hi), grp: 2 (over core), slab: 8 (over x, y_lo).
Axes of the slice: x: 4, y: 4 (y_hi: 2, y_lo: 2; y = y_hi * 2 + y_lo), z: 16, core: 2. Of those that a mesh axis runs over, the one named last changes fastest.
Arguments:
- hidden: bfloat16 [64, 64, 64, 3072], P(('fsdp', 'grp'), 'slab'), may hold values from -6 to 6
- modulation: bfloat16 [64, 2, 3072], P(('fsdp', 'grp')), may hold values from -3 to 3
- noisy: bfloat16 [64, 64, 64, 64], P(('fsdp', 'grp'), 'slab'), may hold values from -6 to 6
- step_index: int32 [64], P(('fsdp', 'grp')), may hold values from 0 to 27
- proj_weight: bfloat16 [3072, 64], P('fsdp'), may hold values from -0.109375 to 0.109375
- proj_bias: float32 [64], replicated, may hold values from -3 to 3
- conv_weight: bfloat16 [3, 3, 16, 512], P(None, None, None, 'fsdp'), may hold values from -0.5 to 0.5
- conv_bias: float32 [512], replicated, may hold values from -3 to 3
- norm_gain: float32 [512], replicated, may hold values from 0.25 to 1.75
- norm_shift: float32 [512], replicated, may hold values from -3 to 3
- head_weight: bfloat16 [512, 192], P('fsdp'), may hold values from -1 to 1
- head_bias: float32 [192], replicated, may hold values from -2 to 2
- patch_weight: bfloat16 [588, 1280], P(None, 'fsdp'), may hold values from -0.25 to 0.25
- position: bfloat16 [256, 1280], P('slab'), may hold values from -3 to 3
- class_token: float32 [1280], replicated, may hold values from -6 to 6
- vit_gain: float32 [4, 1280], replicated, may hold values from 0.25 to 1.75
- vit_shift: float32 [4, 1280], replicated, may hold values from -2 to 2
- attn_in: bfloat16 [1280, 3840], P('fsdp', 'slab'), may hold values from -0.15625 to 0.15625
- attn_out: bfloat16 [1280, 1280], P('slab', 'fsdp'), may hold values from -0.625 to 0.625
- attn_out_bias: float32 [1280], replicated, may hold values from -3 to 3
- mlp_in: bfloat16 [1280, 5120], P(None, ('fsdp', 'slab')), may hold values from -0.15625 to 0.15625
- mlp_in_bias: bfloat16 [5120], P(('fsdp', 'slab')), may hold values from -3 to 3
- mlp_out: bfloat16 [5120, 1280], P(('fsdp', 'slab')), may hold values from -0.078125 to 0.078125
- mlp_out_bias: float32 [1280], replicated, may hold values from -3 to 3
- vit_proj: bfloat16 [1280, 1024], P('fsdp'), may hold values from -0.15625 to 0.15625
- text_embed: float32 [64, 1024], P(('fsdp', 'grp')), may hold values from -6 to 6
Outputs:
- proj_grad: float32 [3072, 64], P('fsdp')
- scores: float32 [64], P(('fsdp', 'grp'))
The draws below stay inside these ranges and needn't reach their ends.
All inputs are finite; a program needn't handle non-finite values.
Results may differ from the reference program's by a relative error of at most 0.023.
Values may be sent and summed in bfloat16 or wider, within the bound.
A program may use at most 128 MiB of HBM per device.

```python
import jax
import jax.numpy as jnp
from jax import lax

D = 3072
PATCH_CH = 64
LAT_CH = 16
VC = 512
GROUPS = 32
VD = 1280
HEADS = 16
HEAD_DIM = 80
VH = 5120
EMB = 1024
STEPS = 28
IMAGES = 64
TOK_SIDE = 64
GRID = 16
NT = 256


def draw_noisy(key, part):
    key = jax.random.fold_in(key, 11)
    shape = (IMAGES, TOK_SIDE, TOK_SIDE, PATCH_CH)
    rows = jnp.arange(TOK_SIDE, dtype=jnp.float32) / max(TOK_SIDE - 1, 1)
    scale = 0.4 * 8.0 ** rows
    base = jax.random.normal(key, shape, jnp.float32)
    values = jnp.clip(base * scale[None, :, None, None], -6.0, 6.0)
    return values.astype(jnp.bfloat16)


def draw_head_weight(key, part):
    key = jax.random.fold_in(key, 23)
    columns = jnp.arange(192, dtype=jnp.int32)
    inner_row = columns // 8 % 8
    edge = (inner_row == 0) | (inner_row == 7)
    factor = jnp.where(edge, 3.0, 1.0).astype(jnp.float32)
    base = jnp.clip(jax.random.normal(key, (VC, 192), jnp.float32), -5.0, 5.0)
    values = jnp.clip(base * factor[None, :] * VC ** (-0.5), -1.0, 1.0)
    return values.astype(jnp.bfloat16)


def plant(result, own_key, low, high):
    index_at = [jax.random.randint(jax.random.fold_in(own_key, axis), (), 0, length) for axis, length in enumerate(result.shape)]
    widest = result.shape.index(max(result.shape))
    neighbour = index_at[:widest] + [(index_at[widest] + 1) % result.shape[widest]] + index_at[widest + 1:]
    return result.at[tuple(index_at)].set(low).at[tuple(neighbour)].set(high)


def level_of(key, shape, split, smallest, high):
    level, own = 1.0, jax.random.fold_in(key, 6)
    for dim, parts in split:
        draws = jnp.exp(jax.random.uniform(jax.random.fold_in(own, dim), (parts,), jnp.float32, smallest / len(split), high / len(split)))
        level = level * jnp.repeat(draws, shape[dim] // parts).reshape([-1 if axis == dim else 1 for axis in range(len(shape))])
    return level


def bell_draw(key, extent, spread, bound, pieces=(), kind=jnp.bfloat16):
    level = level_of(key, extent, pieces, -0.22, 0.18) if pieces else 1.0
    values = jax.random.normal(key, extent, jnp.float32) * spread * level
    return jnp.minimum(jnp.maximum(values, -bound), bound).astype(kind)


def setup_inputs(seed: int = 0) -> dict:
    seeds = jax.random.split(jax.random.key(seed), 27)
    hidden = bell_draw(seeds[0], (IMAGES, TOK_SIDE, TOK_SIDE, D), 1.0, 6.0, ((0, 64), (1, 8)))
    modulation = bell_draw(seeds[1], (IMAGES, 2, D), 0.5, 3.0, ((0, 64),))
    noisy = draw_noisy(jax.random.fold_in(seeds[26], 71), 0)
    step_index = plant(jax.random.randint(seeds[3], (IMAGES,), 0, STEPS), jax.random.fold_in(seeds[3], 1), 0, STEPS - 1).astype(jnp.int32)
    proj_weight = bell_draw(seeds[4], (D, PATCH_CH), D ** -0.5, 0.109375, ((0, 32),))
    proj_bias = bell_draw(seeds[5], (PATCH_CH,), 0.5, 3.0, (), jnp.float32)
    conv_weight = bell_draw(seeds[6], (3, 3, LAT_CH, VC), (9 * LAT_CH) ** -0.5, 0.5, ((3, 32),))
    conv_bias = bell_draw(seeds[7], (VC,), 0.5, 3.0, (), jnp.float32)
    norm_gain = jnp.clip(1.0 + 0.15 * jax.random.normal(seeds[8], (VC,), jnp.float32), 0.25, 1.75)
    norm_shift = bell_draw(seeds[9], (VC,), 0.5, 3.0, (), jnp.float32)
    head_weight = draw_head_weight(jax.random.fold_in(seeds[26], 71), 0)
    head_bias = bell_draw(seeds[11], (192,), 0.3, 2.0, (), jnp.float32)
    patch_weight = bell_draw(seeds[12], (588, VD), 588 ** -0.5, 0.25, ((1, 32),))
    position = bell_draw(seeds[13], (NT, VD), 0.5, 3.0, ((0, 8),))
    class_token = bell_draw(seeds[14], (VD,), 1.0, 6.0, (), jnp.float32)
    vit_gain = jnp.clip(1.0 + 0.15 * jax.random.normal(seeds[15], (4, VD), jnp.float32), 0.25, 1.75)
    vit_shift = bell_draw(seeds[16], (4, VD), 0.3, 2.0, (), jnp.float32)
    attn_in = bell_draw(seeds[17], (VD, 3 * VD), VD ** -0.5, 0.15625, ((0, 32), (1, 8)))
    attn_out = bell_draw(seeds[18], (VD, VD), HEAD_DIM ** -0.5, 0.625, ((0, 8), (1, 32)))
    attn_out_bias = bell_draw(seeds[19], (VD,), 0.5, 3.0, (), jnp.float32)
    mlp_in = bell_draw(seeds[20], (VD, VH), VD ** -0.5, 0.15625, ((1, 256),))
    mlp_in_bias = bell_draw(seeds[21], (VH,), 0.5, 3.0, ((0, 256),))
    mlp_out = bell_draw(seeds[22], (VH, VD), VH ** -0.5, 0.078125, ((0, 256),))
    mlp_out_bias = bell_draw(seeds[23], (VD,), 0.5, 3.0, (), jnp.float32)
    vit_proj = bell_draw(seeds[24], (VD, EMB), VD ** -0.5, 0.15625, ((0, 32),))
    text_embed = bell_draw(seeds[25], (IMAGES, EMB), 1.0, 6.0, ((0, 64),), jnp.float32)
    return {"hidden": hidden, "modulation": modulation, "noisy": noisy, "step_index": step_index, "proj_weight": proj_weight, "proj_bias": proj_bias, "conv_weight": conv_weight, "conv_bias": conv_bias, "norm_gain": norm_gain, "norm_shift": norm_shift, "head_weight": head_weight, "head_bias": head_bias, "patch_weight": patch_weight, "position": position, "class_token": class_token, "vit_gain": vit_gain, "vit_shift": vit_shift, "attn_in": attn_in, "attn_out": attn_out, "attn_out_bias": attn_out_bias, "mlp_in": mlp_in, "mlp_in_bias": mlp_in_bias, "mlp_out": mlp_out, "mlp_out_bias": mlp_out_bias, "vit_proj": vit_proj, "text_embed": text_embed}


LAT_SCALE = 0.3611
LAT_SHIFT = 0.1159
PIX_MEAN = (0.48145466, 0.4578275, 0.40821073)
PIX_STD = (0.26862954, 0.26130258, 0.27577711)
HIGH = lax.Precision.HIGHEST

def norm_rows(values, epsilon):
    average = lax.optimization_barrier(jnp.mean(values, axis=-1, keepdims=True))
    centered = values - average
    return centered / jnp.sqrt(lax.optimization_barrier(jnp.mean(centered * centered, axis=-1, keepdims=True)) + epsilon)

def affine_norm(values, gain, shift):
    return norm_rows(values, 1e-05) * gain + shift

def exact_gelu(values):
    return jax.nn.gelu(values, approximate=False)

def flow_sigma(step_index):
    remain = 1.0 - step_index.astype(jnp.float32) / STEPS
    return 3.0 * remain / (1.0 + 2.0 * remain)

def channel_consts():
    return (jnp.array(PIX_MEAN, jnp.float32).reshape(1, 3, 1, 1), jnp.array(PIX_STD, jnp.float32).reshape(1, 3, 1, 1))

def resize_table(out_count, in_count):
    stretch = in_count / out_count
    centers = (jnp.arange(out_count, dtype=jnp.float32) + 0.5) * stretch
    places = jnp.arange(in_count, dtype=jnp.float32) + 0.5
    weights = jnp.maximum(0.0, 1.0 - jnp.abs(places[None, :] - centers[:, None]) / stretch)
    return weights / lax.optimization_barrier(jnp.sum(weights, axis=1, keepdims=True))

def tokens_to_latent(tokens):
    count, rows, cols, chans = tokens.shape
    view = tokens.reshape(count, rows, cols, chans // 4, 2, 2).transpose(0, 1, 4, 2, 5, 3)
    return view.reshape(count, rows * 2, cols * 2, chans // 4)

def latent_to_tokens(latent):
    count, rows, cols, chans = latent.shape
    view = latent.reshape(count, rows // 2, 2, cols // 2, 2, chans).transpose(0, 1, 3, 5, 2, 4)
    return view.reshape(count, rows // 2, cols // 2, chans * 4)

def cells_to_pixels(cells):
    count, rows, cols, chans = cells.shape
    view = cells.reshape(count, rows, cols, 3, 8, 8).transpose(0, 3, 1, 4, 2, 5)
    return view.reshape(count, 3, rows * 8, cols * 8)

def pixels_to_cells(pixels):
    count, chans, rows, cols = pixels.shape
    view = pixels.reshape(count, 3, rows // 8, 8, cols // 8, 8).transpose(0, 2, 4, 1, 3, 5)
    return view.reshape(count, rows // 8, cols // 8, 192)

def image_to_patches(image):
    count, chans, rows, cols = image.shape
    view = image.reshape(count, 3, rows // 14, 14, cols // 14, 14).transpose(0, 2, 4, 1, 3, 5)
    return view.reshape(count, rows // 14 * (cols // 14), 588)

def patches_to_image(patches, rows, cols):
    count = patches.shape[0]
    view = patches.reshape(count, rows // 14, cols // 14, 3, 14, 14).transpose(0, 3, 1, 4, 2, 5)
    return view.reshape(count, 3, rows, cols)

def conv_columns(padded, rows, cols):
    return jnp.concatenate([padded[:, tap // 3:tap // 3 + rows, tap % 3:tap % 3 + cols] for tap in range(9)], axis=-1)

def columns_back(d_columns, rows, cols):
    chans = d_columns.shape[-1] // 9
    total = jnp.zeros(d_columns.shape[:1] + (rows + 2, cols + 2, chans), jnp.float32)
    for tap in range(9):
        shift_row = tap // 3
        shift_col = tap % 3
        piece = d_columns[..., tap * chans:(tap + 1) * chans]
        total = total + jnp.pad(piece, ((0, 0), (shift_row, 2 - shift_row), (shift_col, 2 - shift_col), (0, 0)))
    return total

def group_view(values):
    count, rows, cols, chans = values.shape
    return values.reshape(count, rows * cols, GROUPS, chans // GROUPS)

def group_sums(conv_out):
    view = group_view(conv_out)
    return (lax.optimization_barrier(jnp.sum(view, axis=(1, 3))), lax.optimization_barrier(jnp.sum(view * view, axis=(1, 3))))

def group_apply(conv_out, totals, cells):
    average = totals[0] / cells
    inverse = 1.0 / jnp.sqrt(totals[1] / cells - average * average + 1e-06)
    normed = (group_view(conv_out) - average[:, None, :, None]) * inverse[:, None, :, None]
    return (normed.reshape(conv_out.shape), inverse)

def group_pair(d_normed, normed):
    return (lax.optimization_barrier(jnp.sum(group_view(d_normed), axis=(1, 3))), lax.optimization_barrier(jnp.sum(group_view(d_normed * normed), axis=(1, 3))))

def group_back(d_normed, normed, inverse, totals, cells):
    grads = group_view(d_normed) - totals[0][:, None, :, None] / cells
    grads = grads - group_view(normed) * (totals[1][:, None, :, None] / cells)
    return (grads * inverse[:, None, :, None]).reshape(d_normed.shape)

def match_score(embed, text):
    dots = lax.optimization_barrier(jnp.sum(embed * text, axis=-1))
    sizes = jnp.sqrt(lax.optimization_barrier(jnp.sum(embed * embed, axis=-1)) + 1e-06) * jnp.sqrt(lax.optimization_barrier(jnp.sum(text * text, axis=-1)) + 1e-06)
    return 100.0 * dots / sizes

def reference(hidden, modulation, noisy, step_index, proj_weight, proj_bias, conv_weight, conv_bias, norm_gain, norm_shift, head_weight, head_bias, patch_weight, position, class_token, vit_gain, vit_shift, attn_in, attn_out, attn_out_bias, mlp_in, mlp_in_bias, mlp_out, mlp_out_bias, vit_proj, text_embed):
    images = hidden.shape[0]
    lat_side = 2 * hidden.shape[1]
    pix_side = 8 * lat_side
    vit_side = 14 * GRID
    width_vd = patch_weight.shape[1]
    root = HEAD_DIM ** 0.5
    table = resize_table(vit_side, pix_side)
    conv_mat = conv_weight.reshape(-1, conv_weight.shape[-1])
    cells = lat_side * lat_side * (conv_weight.shape[-1] // GROUPS)
    pix_mean, pix_std = channel_consts()
    attn_view = attn_in.astype(jnp.float32).reshape(width_vd, HEADS, 3, HEAD_DIM)
    query_w = attn_view[:, :, 0]
    key_w = attn_view[:, :, 1]
    value_w = attn_view[:, :, 2]

    def one_image(carry, item):
        hid, mods, noise, index, text = item
        hid, mods, noise, index, text = (hid[None], mods[None], noise[None], index[None], text[None])
        sigma = flow_sigma(index)
        modulated = (norm_rows(hid.astype(jnp.float32), 1e-06) * (1.0 + mods[:, 1].astype(jnp.float32)[:, None, None, :]) + mods[:, 0].astype(jnp.float32)[:, None, None, :]).astype(jnp.bfloat16)
        velocity = jnp.einsum('nijd,dk->nijk', modulated.astype(jnp.float32), proj_weight.astype(jnp.float32)) + proj_bias
        clean = noise.astype(jnp.float32) - sigma[:, None, None, None] * velocity
        latent = (tokens_to_latent(clean) / LAT_SCALE + LAT_SHIFT).astype(jnp.bfloat16)
        padded = jnp.pad(latent, ((0, 0), (1, 1), (1, 1), (0, 0)))
        conv_out = jnp.einsum('nrck,ko->nrco', conv_columns(padded, lat_side, lat_side).astype(jnp.float32), conv_mat.astype(jnp.float32)) + conv_bias
        normed, inverse = group_apply(conv_out, group_sums(conv_out), cells)
        gained = normed * norm_gain + norm_shift
        active_vae, silu_back = jax.vjp(jax.nn.silu, gained)
        cell_vals = jnp.einsum('nrco,ok->nrck', active_vae.astype(jnp.bfloat16).astype(jnp.float32), head_weight.astype(jnp.float32)) + head_bias
        pixels = cells_to_pixels(cell_vals).astype(jnp.bfloat16)
        shrunk = jnp.einsum('ik,nckp->ncip', table, pixels.astype(jnp.float32), precision=HIGH)
        shrunk = jnp.einsum('ncip,jp->ncij', shrunk, table, precision=HIGH)
        image = ((shrunk + 1.0) * 0.5 - pix_mean) / pix_std
        patches = image_to_patches(image).astype(jnp.bfloat16)
        embedded = jnp.einsum('ntk,kd->ntd', patches.astype(jnp.float32), patch_weight.astype(jnp.float32)) + position.astype(jnp.float32)[None]
        pre_x, pre_back = jax.vjp(lambda values: affine_norm(values, vit_gain[0], vit_shift[0]), embedded)
        unit, unit_back = jax.vjp(lambda values: affine_norm(values, vit_gain[1], vit_shift[1]), pre_x)
        unit_b = unit.astype(jnp.bfloat16).astype(jnp.float32)
        class_pre = affine_norm(class_token[None], vit_gain[0], vit_shift[0])
        class_unit = affine_norm(class_pre, vit_gain[1], vit_shift[1]).astype(jnp.bfloat16).astype(jnp.float32)
        query = jnp.einsum('nd,dhe->nhe', class_unit, query_w).astype(jnp.bfloat16).astype(jnp.float32)
        class_key = jnp.einsum('nd,dhe->nhe', class_unit, key_w).astype(jnp.bfloat16).astype(jnp.float32)
        class_val = jnp.einsum('nd,dhe->nhe', class_unit, value_w).astype(jnp.bfloat16).astype(jnp.float32)
        keys = jnp.einsum('ntd,dhe->nthe', unit_b, key_w).astype(jnp.bfloat16).astype(jnp.float32)
        vals = jnp.einsum('ntd,dhe->nthe', unit_b, value_w).astype(jnp.bfloat16).astype(jnp.float32)
        class_logit = jnp.einsum('nhe,nhe->nh', query, class_key) / root
        token_logits = jnp.einsum('nhe,nthe->nht', query, keys) / root
        class_exp = jnp.exp(class_logit)
        token_exp = jnp.exp(token_logits)
        denominator = class_exp + lax.optimization_barrier(jnp.sum(token_exp, axis=-1))
        class_weight = class_exp / denominator
        token_weight = token_exp / denominator[..., None]
        class_rounded = class_weight.astype(jnp.bfloat16).astype(jnp.float32)
        token_rounded = token_weight.astype(jnp.bfloat16).astype(jnp.float32)
        heads = class_rounded[..., None] * class_val + jnp.einsum('nht,nthe->nhe', token_rounded, vals)
        heads_b = heads.astype(jnp.bfloat16).reshape(1, width_vd)
        block_mid = class_pre + jnp.dot(heads_b, attn_out, preferred_element_type=jnp.float32) + attn_out_bias
        mlp_input, mid_back = jax.vjp(lambda values: affine_norm(values, vit_gain[2], vit_shift[2]), block_mid)
        preact = jnp.dot(mlp_input.astype(jnp.bfloat16), mlp_in, preferred_element_type=jnp.float32) + mlp_in_bias.astype(jnp.float32)
        active, gelu_back = jax.vjp(exact_gelu, preact)
        block_out = block_mid + jnp.dot(active.astype(jnp.bfloat16), mlp_out, preferred_element_type=jnp.float32) + mlp_out_bias
        post, post_back = jax.vjp(lambda values: affine_norm(values, vit_gain[3], vit_shift[3]), block_out)
        embed = jnp.dot(post.astype(jnp.bfloat16), vit_proj, preferred_element_type=jnp.float32)
        score, score_back = jax.vjp(lambda values: match_score(values, text), embed)
        d_embed = score_back(jnp.full_like(score, -1.0 / images))[0].astype(jnp.bfloat16)
        d_post = jnp.dot(d_embed, vit_proj.T, preferred_element_type=jnp.float32)
        d_second = post_back(d_post)[0]
        d_active = jnp.dot(d_second.astype(jnp.bfloat16), mlp_out.T, preferred_element_type=jnp.float32)
        d_pre = gelu_back(d_active)[0].astype(jnp.bfloat16)
        d_input = jnp.dot(d_pre, mlp_in.T, preferred_element_type=jnp.float32)
        d_first = d_second + mid_back(d_input)[0]
        d_heads = jnp.dot(d_first.astype(jnp.bfloat16), attn_out.T, preferred_element_type=jnp.float32)
        d_heads = d_heads.astype(jnp.bfloat16).astype(jnp.float32).reshape(1, HEADS, HEAD_DIM)
        class_dots = jnp.einsum('nhe,nhe->nh', d_heads, class_val)
        token_dots = jnp.einsum('nhe,nthe->nht', d_heads, vals)
        expected = class_weight * class_dots + lax.optimization_barrier(jnp.sum(token_weight * token_dots, axis=-1))
        logit_grads = token_weight * (token_dots - expected[..., None])
        key_dir = jnp.einsum('nhe,dhe->nhd', query, key_w)
        value_dir = jnp.einsum('nhe,dhe->nhd', d_heads, value_w)
        d_unit = jnp.einsum('nht,nhd->ntd', logit_grads / root, key_dir, precision=HIGH) + jnp.einsum('nht,nhd->ntd', token_rounded, value_dir, precision=HIGH)
        d_pre_x = unit_back(d_unit)[0]
        d_embedded = pre_back(d_pre_x)[0].astype(jnp.bfloat16)
        d_patches = jnp.einsum('ntd,kd->ntk', d_embedded.astype(jnp.float32), patch_weight.astype(jnp.float32))
        d_image = patches_to_image(d_patches, vit_side, vit_side) / (2.0 * pix_std)
        folded = jnp.einsum('ncij,jp->ncip', d_image, table, precision=HIGH)
        d_pixels = jnp.einsum('ik,ncip->nckp', table, folded, precision=HIGH)
        d_cells = pixels_to_cells(d_pixels).astype(jnp.bfloat16)
        d_act = jnp.einsum('nrck,ok->nrco', d_cells.astype(jnp.float32), head_weight.astype(jnp.float32))
        d_normed = silu_back(d_act)[0] * norm_gain
        d_conv = group_back(d_normed, normed, inverse, group_pair(d_normed, normed), cells).astype(jnp.bfloat16)
        d_columns = jnp.einsum('nrco,ko->nrck', d_conv.astype(jnp.float32), conv_mat.astype(jnp.float32))
        d_latent = columns_back(d_columns, lat_side, lat_side)[:, 1:-1, 1:-1]
        d_clean = latent_to_tokens(d_latent) / LAT_SCALE
        d_velocity = (-sigma[:, None, None, None] * d_clean).astype(jnp.bfloat16)
        grad_local = jnp.einsum('nijd,nijk->dk', modulated.astype(jnp.float32), d_velocity.astype(jnp.float32))
        return (carry + grad_local, score[0])
    total, scores = lax.scan(one_image, jnp.zeros((D, PATCH_CH), jnp.float32), (hidden, modulation, noisy, step_index, text_embed))
    return (total, scores)
```

```python
import functools

import jax
import jax.numpy as jnp
import numpy as np
from jax import lax
from jax.experimental import pallas as pl
from jax.experimental.pallas import tpu as pltpu
from jax.sharding import PartitionSpec as P

GROUPS = 32
HEAD_DIM = 80
STEPS = 28
LAT_SCALE = 0.3611
LAT_SHIFT = 0.1159
PIX_MEAN = (0.48145466, 0.4578275, 0.40821073)
PIX_STD = (0.26862954, 0.26130258, 0.27577711)
HIGH = lax.Precision.HIGHEST
MESH = pl.DeviceIdType.MESH
F32 = jnp.float32
BF16 = jnp.bfloat16
ANY = pl.BlockSpec(memory_space=pl.ANY)
VMEM = pl.BlockSpec(memory_space=pltpu.VMEM)


def greet(targets):
    barrier = pltpu.get_barrier_semaphore()
    for target in targets:
        pl.semaphore_signal(barrier, inc=1, device_id=target, device_id_type=MESH)
    pl.semaphore_wait(barrier, len(targets))


def remote(source, dest, send, recv, target):
    return pltpu.make_async_remote_copy(
        src_ref=source, dst_ref=dest, send_sem=send, recv_sem=recv,
        device_id=target, device_id_type=MESH,
    )


def spread_kernel(count, swap, *refs):
    n = lax.axis_size("slab")
    ins, outs = refs[:count], refs[count : 2 * count]
    send, recv = refs[2 * count :]
    me = lax.axis_index("slab")
    peers = [lax.rem(me + d, n) for d in range(1, n)]
    greet([{"slab": p} for p in peers])
    copies = []
    for a in range(count):
        for d, p in enumerate(peers):
            source = ins[a].at[p] if swap else ins[a]
            copy = remote(source, outs[a].at[me], send.at[a, d], recv.at[a, d], {"slab": p})
            copy.start()
            copies.append(copy)
    for a in range(count):
        outs[a][me] = ins[a][me] if swap else ins[a][...]
    for copy in copies:
        copy.wait()


def slab_spread(arrays, cid, swap=False):
    n = lax.axis_size("slab")
    count = len(arrays)
    shapes = [
        jax.ShapeDtypeStruct(a.shape if swap else (n,) + a.shape, a.dtype) for a in arrays
    ]
    return pl.pallas_call(
        functools.partial(spread_kernel, count, swap),
        out_shape=shapes,
        in_specs=[VMEM] * count,
        out_specs=[VMEM] * count,
        scratch_shapes=[pltpu.SemaphoreType.DMA((count, n - 1))] * 2,
        compiler_params=pltpu.CompilerParams(collective_id=cid, has_side_effects=True),
        name=f"slab_{cid}",
    )(*arrays)


def gather_kernel(
    s_in, r_in, s_out, r_out, pair_send, pair_recv, local_sem,
    ring_send, ring_recv, slab_send, slab_recv, core_send, core_recv,
):
    nf = lax.axis_size("fsdp")
    ns = lax.axis_size("slab")
    nz = nf // 2
    f = lax.axis_index("fsdp")
    g = lax.axis_index("grp")
    s = lax.axis_index("slab")
    z, half = f // 2, lax.rem(f, 2)
    w = g * ns + s
    other = {"fsdp": z * 2 + 1 - half}
    right = {"fsdp": lax.rem(z + 1, nz) * 2 + half}
    left = {"fsdp": lax.rem(z + nz - 1, nz) * 2 + half}
    core = {"grp": 1 - g}
    peers = [lax.rem(s + d, ns) for d in range(1, ns)]
    greet([other, right, left, core] + [{"slab": p} for p in peers])
    own = [
        pltpu.make_async_copy(s_in.at[g], s_out.at[g, z, half], local_sem.at[0]),
        pltpu.make_async_copy(r_in.at[w], r_out.at[w, z, half], local_sem.at[1]),
    ]
    pair = [
        remote(s_in.at[g], s_out.at[g, z, half], pair_send.at[0], pair_recv.at[0], other),
        remote(r_in.at[w], r_out.at[w, z, half], pair_send.at[1], pair_recv.at[1], other),
    ]
    for copy in pair + own:
        copy.start()

    def ring(step, way):
        block = lax.rem(z - step + nz, nz) if way == 0 else lax.rem(z + step, nz)
        target = right if way == 0 else left
        slot = way * 8 + step
        return [
            remote(r_out.at[w, block], r_out.at[w, block], ring_send.at[0, slot], ring_recv.at[0, slot], target),
            remote(s_out.at[g, block], s_out.at[g, block], ring_send.at[1, slot], ring_recv.at[1, slot], target),
        ]

    def share(block):
        for d, p in enumerate(peers):
            remote(
                r_out.at[w, block], r_out.at[w, block], slab_send.at[d], slab_recv.at[d], {"slab": p}
            ).start()
        remote(r_out.at[w, block], r_out.at[w, block], core_send.at[0], core_recv.at[0], core).start()
        remote(s_out.at[g, block], s_out.at[g, block], core_send.at[1], core_recv.at[1], core).start()

    for copy in own:
        copy.wait()
    for copy in pair:
        copy.wait_recv()
    steps = (nz // 2, nz - 1 - nz // 2)
    sent = []
    for step in range(steps[0]):
        for way in (0, 1):
            if step < steps[way]:
                copies = ring(step, way)
                for copy in copies:
                    copy.start()
                sent += copies
        if step == 0:
            share(z)
        for way in (0, 1):
            if step < steps[way]:
                for copy in sent[-4 if steps[1] > step else -2 :][2 * way : 2 * way + 2]:
                    copy.wait_recv()
                share(lax.rem(z - step - 1 + nz, nz) if way == 0 else lax.rem(z + step + 1, nz))
    forwards = []
    for d in range(ns - 1):
        source = g * ns + lax.rem(s + ns - 1 - d, ns)
        remote(r_out.at[source], r_out.at[source], slab_send.at[d], slab_recv.at[d], core).wait_recv()
        copy = remote(r_out.at[source], r_out.at[source], core_send.at[2 + d], core_recv.at[2 + d], core)
        copy.start()
        forwards.append(copy)
    theirs = (1 - g) * ns
    for d in range(ns - 1):
        forwards[d].wait_send()
        source = theirs + lax.rem(s + ns - 1 - d, ns)
        remote(r_out.at[source], r_out.at[source], core_send.at[2 + d], core_recv.at[2 + d], core).wait_recv()
        remote(r_out.at[w], r_out.at[w], slab_send.at[d], slab_recv.at[d], core).wait_send()
    remote(r_out.at[w], r_out.at[w], core_send.at[0], core_recv.at[0], core).wait_send()
    remote(s_out.at[g], s_out.at[g], core_send.at[1], core_recv.at[1], core).wait_send()
    remote(r_out.at[theirs + s], r_out.at[theirs + s], core_send.at[0], core_recv.at[0], core).wait_recv()
    remote(s_out.at[1 - g], s_out.at[1 - g], core_send.at[1], core_recv.at[1], core).wait_recv()
    for copy in pair + sent:
        copy.wait_send()


def weight_gather(s_pack, r_pack):
    nf = lax.axis_size("fsdp")
    ns = lax.axis_size("slab")
    s_shape = (2, nf // 2, 2) + s_pack.shape[1:]
    r_shape = (2 * ns, nf // 2, 2) + r_pack.shape[1:]
    dma = pltpu.SemaphoreType.DMA
    return pl.pallas_call(
        gather_kernel,
        out_shape=[jax.ShapeDtypeStruct(s_shape, BF16), jax.ShapeDtypeStruct(r_shape, BF16)],
        in_specs=[ANY, ANY],
        out_specs=[ANY, ANY],
        scratch_shapes=[
            dma((2,)), dma((2,)), dma((2,)), dma((2, 16)), dma((2, 16)),
            dma((ns - 1,)), dma((ns - 1,)), dma((ns + 1,)), dma((ns + 1,)),
        ],
        compiler_params=pltpu.CompilerParams(collective_id=0, has_side_effects=True),
        name="weights",
    )(s_pack, r_pack)


def reduce_kernel(
    g_in, out, landed, terms, arrived, a_send, a_recv, b_send, b_recv, c_send, c_recv
):
    nf = lax.axis_size("fsdp")
    ns = lax.axis_size("slab")
    nw = 2 * ns
    f = lax.axis_index("fsdp")
    g = lax.axis_index("grp")
    s = lax.axis_index("slab")
    w = g * ns + s

    def block_peer(d):
        other_g = lax.rem(g + d // ns, 2)
        other_s = lax.rem(s + d % ns, ns)
        return other_g * ns + other_s, {"grp": other_g, "slab": other_s}

    block = [block_peer(d) for d in range(1, nw)]
    ring = [lax.rem(f + d, nf) for d in range(1, nf)]
    greet([target for _, target in block] + [{"fsdp": p} for p in ring])
    first = []
    for d, (index, target) in enumerate(block):
        copy = remote(g_in.at[index], landed.at[w], a_send.at[d], a_recv.at[d], target)
        copy.start()
        first.append(copy)
    landed[w] = g_in[w]
    for copy in first:
        copy.wait()
    total = landed[0].astype(F32)
    for index in range(1, nw):
        total = total + landed[index].astype(F32)
    for index in range(nf):
        terms[index, 0:3] = total[3 * index : 3 * index + 3]
        terms[index, 3:4] = total[3 * index : 3 * index + 1]
    second = []
    for d, p in enumerate(ring):
        copy = remote(terms.at[p], arrived.at[f], b_send.at[d], b_recv.at[d], {"fsdp": p})
        copy.start()
        second.append(copy)
    arrived[f] = terms[f]
    for copy in second:
        copy.wait()
    out[w] = jnp.sum(arrived[...], axis=0)
    third = []
    for d, (index, target) in enumerate(block):
        copy = remote(out.at[w], out.at[w], c_send.at[d], c_recv.at[d], target)
        copy.start()
        third.append(copy)
    for copy in third:
        copy.wait()


def grad_reduce(chunks):
    nf = lax.axis_size("fsdp")
    nw = 2 * lax.axis_size("slab")
    dma = pltpu.SemaphoreType.DMA
    return pl.pallas_call(
        reduce_kernel,
        out_shape=jax.ShapeDtypeStruct((nw, 4, 128), F32),
        in_specs=[VMEM],
        out_specs=VMEM,
        scratch_shapes=[
            pltpu.VMEM(chunks.shape, BF16),
            pltpu.VMEM((nf, 4, 128), F32),
            pltpu.VMEM((nf, 4, 128), F32),
            dma((nw - 1,)), dma((nw - 1,)), dma((nf - 1,)), dma((nf - 1,)),
            dma((nw - 1,)), dma((nw - 1,)),
        ],
        compiler_params=pltpu.CompilerParams(collective_id=1, has_side_effects=True),
        name="gradient",
    )(chunks)


def grad_total(grad):
    nf = lax.axis_size("fsdp")
    nw = 2 * lax.axis_size("slab")
    chunks = grad.astype(BF16).reshape(nf, nw, 6, 64).transpose(1, 0, 2, 3)
    return grad_reduce(chunks.reshape(nw, nf * 3, 128))[:, :3].reshape(96, 64)


def norm_rows(values, epsilon):
    average = jnp.mean(values, axis=-1, keepdims=True)
    centered = values - average
    return centered / jnp.sqrt(jnp.mean(centered * centered, axis=-1, keepdims=True) + epsilon)


def affine_norm(values, gain, shift):
    return norm_rows(values, 1e-05) * gain + shift


def exact_gelu(values):
    return jax.nn.gelu(values, approximate=False)


def flow_sigma(step_index):
    remain = 1.0 - step_index.astype(F32) / STEPS
    return 3.0 * remain / (1.0 + 2.0 * remain)


def resize_table(out_count, in_count):
    stretch = in_count / out_count
    centers = (np.arange(out_count) + 0.5) * stretch
    places = np.arange(in_count) + 0.5
    weights = np.maximum(0.0, 1.0 - np.abs(places[None, :] - centers[:, None]) / stretch)
    return weights / weights.sum(axis=1, keepdims=True)


def match_score(embed, text):
    dots = jnp.sum(embed * text, axis=-1)
    sizes = jnp.sqrt(jnp.sum(embed * embed, axis=-1) + 1e-06) * jnp.sqrt(
        jnp.sum(text * text, axis=-1) + 1e-06
    )
    return 100.0 * dots / sizes


def pad_rows(values, rows):
    flat = values.reshape(-1)
    return jnp.pad(flat, (0, rows * 128 - flat.shape[0])).reshape(rows, 128)


def dot(a, b, dims=((1,), (0,)), precision=None):
    return lax.dot_general(a, b, (dims, ((), ())), precision=precision, preferred_element_type=F32)


S_ROWS = 304
R_ROWS = 48


def pack_weights(proj, conv, head, patch, attn_in, attn_out, mlp_in, mlp_bias, mlp_out, vit):
    attn = attn_in.reshape(40, 2, 3, HEAD_DIM)
    s_pack = jnp.stack(
        [
            pad_rows(
                jnp.concatenate([mlp_in.T.reshape(-1), attn[:, :, :2].reshape(-1), mlp_bias]), S_ROWS
            ),
            pad_rows(
                jnp.concatenate([mlp_out.reshape(-1), attn_out.T.reshape(-1), attn[:, :, 2].reshape(-1)]),
                S_ROWS,
            ),
        ]
    )
    first = pad_rows(proj, R_ROWS)[None]
    second = pad_rows(
        jnp.concatenate([conv.reshape(144, 16).T.reshape(-1), head.reshape(-1)]), R_ROWS
    )[None]
    third = pad_rows(patch.T, 4 * R_ROWS).reshape(4, R_ROWS, 128)
    fourth = jnp.pad(vit.reshape(10, 32, 128), ((0, 0), (0, R_ROWS - 32), (0, 0)))
    r_pack = jnp.concatenate([first, second, third, fourth])
    return s_pack, r_pack


def unpack_weights(s_all, r_all):
    nf = s_all.shape[1] * 2
    flat = s_all.reshape(2, nf, S_ROWS * 128)
    in_share = flat[0, :, :25600].reshape(nf * 20, 1280)
    qk = flat[0, :, 25600:38400].reshape(nf * 40, 2, 2, HEAD_DIM)
    bias = flat[0, :, 38400:38420].reshape(nf * 20)
    out_share = flat[1, :, :25600].reshape(nf * 20, 1280)
    attn_rows = flat[1, :, 25600:32000].reshape(nf * 40, 160)
    value = flat[1, :, 32000:38400].reshape(nf * 40, 2, HEAD_DIM)
    proj = r_all[0].reshape(nf * 96, 64)
    second = r_all[1].reshape(nf, R_ROWS * 128)
    conv = second[:, :2304].reshape(nf * 16, 144)
    head = second[:, 2304:5376].reshape(nf * 16, 192)
    third = r_all[2:6].reshape(4, nf, R_ROWS * 128).transpose(1, 0, 2).reshape(nf, -1)
    patch = third[:, :23520].reshape(nf * 40, 588)
    fourth = r_all[6:16].reshape(10, nf, R_ROWS, 128)[:, :, :32]
    vit = fourth.transpose(1, 0, 2, 3).reshape(nf * 40, 1024)
    return in_share, qk, bias, out_share, attn_rows, value, proj, conv, head, patch, vit


def all_weights(*shards):
    return unpack_weights(*weight_gather(*pack_weights(*shards)))


def local(
    hidden, modulation, noisy, step_index, proj_weight, proj_bias, conv_weight, conv_bias,
    norm_gain, norm_shift, head_weight, head_bias, patch_weight, position, class_token,
    vit_gain, vit_shift, attn_in, attn_out, attn_out_bias, mlp_in, mlp_in_bias, mlp_out,
    mlp_out_bias, vit_proj, text_embed,
):
    ns = lax.axis_size("slab")
    nf = lax.axis_size("fsdp")
    place = lax.axis_index("slab")
    total_images = nf * lax.axis_size("grp")
    root = HEAD_DIM**0.5
    before, after = lax.rem(place + ns - 1, ns), lax.rem(place + 1, ns)
    in_share, qk_w, bias_share, out_share, attn_rows, value_w, proj, conv, head, patch, vit = (
        all_weights(
            proj_weight, conv_weight, head_weight, patch_weight, attn_in, attn_out, mlp_in,
            mlp_in_bias, mlp_out, vit_proj,
        )
    )
    key_w = qk_w[:, :, 1]

    class_pre = affine_norm(class_token[None], vit_gain[0], vit_shift[0])
    class_unit = affine_norm(class_pre, vit_gain[1], vit_shift[1]).astype(BF16)
    query_key = jnp.einsum("d,dhje->hje", class_unit[0], qk_w, preferred_element_type=F32)
    query = query_key[:, 0].astype(BF16)
    class_key = query_key[:, 1].astype(BF16)
    class_val = jnp.einsum("d,dhe->he", class_unit[0], value_w, preferred_element_type=F32).astype(BF16)
    class_exp = jnp.exp(
        jnp.sum(query.astype(F32) * class_key.astype(F32), axis=-1) / root
    )
    key_dir = jnp.einsum("he,dhe->hd", query, key_w, preferred_element_type=F32)

    tokens = hidden.reshape(512, 3072)
    modulated = (
        norm_rows(tokens.astype(F32), 1e-06) * (1.0 + modulation[0, 1].astype(F32)[None])
        + modulation[0, 0].astype(F32)[None]
    ).astype(BF16)
    sigma = flow_sigma(step_index)[0]
    velocity = dot(modulated, proj) + proj_bias
    clean = noisy.reshape(512, 64).astype(F32) - sigma * velocity
    lat_tok = (clean / LAT_SCALE + LAT_SHIFT).astype(BF16)

    perm = np.zeros((64, 64), np.float32)
    for c in range(16):
        for p in range(2):
            for q in range(2):
                perm[4 * c + 2 * p + q, q * 32 + p * 16 + c] = 1
    perm = jnp.asarray(perm, BF16)
    inter = np.zeros((2, 64, 128), np.float32)
    for q in range(2):
        inter[q, np.arange(64), 2 * np.arange(64) + q] = 1
    inter = jnp.asarray(inter, BF16)
    ordered = dot(lat_tok, perm).astype(BF16).reshape(8, 64, 2, 32)
    latent = jnp.einsum("ijhk,hjq->ikq", ordered, inter, preferred_element_type=F32)
    latent = latent.astype(BF16).reshape(16, 16, 128)
    rims = jnp.concatenate([latent[0], latent[15]])
    rims_all, dirs_all = slab_spread([rims, pad_rows(key_dir, 24)], 2)
    key_dirs = dirs_all[:, :20].reshape(16, 1280)
    low = jnp.where(place > 0, rims_all[before, 16:], 0).astype(BF16)
    high = jnp.where(place < ns - 1, rims_all[after, :16], 0).astype(BF16)
    ext = jnp.concatenate([low[None], latent, high[None]])
    ext = jnp.pad(ext, ((0, 0), (0, 0), (1, 1)))
    cols = jnp.concatenate(
        [ext[t // 3 : t // 3 + 16, :, t % 3 : t % 3 + 128] for t in range(9)], axis=1
    )
    conv_out = (
        jnp.einsum("ok,rkq->roq", conv, cols, preferred_element_type=F32) + conv_bias[None, :, None]
    )
    cells = 128 * 128 * 16
    sums = jnp.stack([jnp.sum(conv_out, axis=(0, 2)), jnp.sum(conv_out * conv_out, axis=(0, 2))])
    totals = jnp.sum(slab_spread([sums.reshape(8, 128)], 3)[0], axis=0)
    totals = jnp.sum(totals.reshape(2, GROUPS, 16), axis=2) / cells
    inverse = 1.0 / jnp.sqrt(totals[1] - totals[0] * totals[0] + 1e-06)
    average_c = jnp.repeat(totals[0], 16)[None, :, None]
    inverse_c = jnp.repeat(inverse, 16)[None, :, None]
    normed = (conv_out - average_c) * inverse_c
    gain_c = norm_gain[None, :, None]
    gained = normed * gain_c + norm_shift[None, :, None]
    active_vae = (gained * jax.nn.sigmoid(gained)).astype(BF16)
    head_t = head.reshape(512, 3, 8, 8).transpose(3, 1, 2, 0).reshape(192, 512)
    bias_t = head_bias.reshape(3, 8, 8).transpose(2, 0, 1).reshape(192)
    pixels = (
        jnp.einsum("ko,roq->rkq", head_t, active_vae, preferred_element_type=F32)
        + bias_t[None, :, None]
    ).astype(BF16)
    table = resize_table(224, 1024).astype(np.float32)
    spread_t = table.reshape(224, 128, 8).transpose(2, 1, 0)
    t_high = spread_t.astype(jnp.bfloat16)
    t_low = (spread_t - t_high.astype(np.float32)).astype(jnp.bfloat16)
    t_high, t_low = jnp.asarray(t_high), jnp.asarray(t_low)
    rows_all = np.zeros((8, 30, 128), np.float32)
    for s in range(8):
        for i in range(30):
            if 0 <= 28 * s + i - 1 < 224:
                rows_all[s, i] = table[28 * s + i - 1, 128 * s : 128 * s + 128]
    row_w = lax.dynamic_index_in_dim(jnp.asarray(rows_all), place, keepdims=False).reshape(30, 16, 8)
    view = pixels.reshape(16, 8, 24, 128)
    narrow = jnp.einsum("rxkq,xqj->rkj", view, t_high, preferred_element_type=F32) + jnp.einsum(
        "rxkq,xqj->rkj", view, t_low, preferred_element_type=F32
    )
    shrunk = jnp.einsum("iry,rcyj->cij", row_w, narrow.reshape(16, 3, 8, 224), precision=HIGH)
    edges = jnp.stack([shrunk[:, 0], shrunk[:, 29]])
    edges = slab_spread([pad_rows(edges, 16)], 4)[0].reshape(ns, 2048)[:, :1344].reshape(ns, 2, 3, 224)
    shrunk = shrunk[:, 1:29]
    shrunk = jnp.concatenate(
        [shrunk[:, :1] + edges[before, 1][:, None], shrunk[:, 1:27], shrunk[:, 27:] + edges[after, 0][:, None]],
        axis=1,
    )
    pix_mean = jnp.asarray(PIX_MEAN, F32).reshape(3, 1, 1)
    pix_std = jnp.asarray(PIX_STD, F32).reshape(3, 1, 1)
    image = ((shrunk + 1.0) * 0.5 - pix_mean) / pix_std
    patches = (
        image.reshape(3, 2, 14, 16, 14).transpose(1, 3, 0, 2, 4).reshape(32, 588).astype(BF16)
    )
    embedded = dot(patches, patch, ((1,), (1,))) + position.astype(F32)
    pre_x, pre_back = jax.vjp(lambda v: affine_norm(v, vit_gain[0], vit_shift[0]), embedded)
    unit, unit_back = jax.vjp(lambda v: affine_norm(v, vit_gain[1], vit_shift[1]), pre_x)
    unit = unit.astype(BF16).astype(F32)

    token_exp = jnp.exp(dot(key_dirs, unit, ((1,), (1,)), HIGH) / root)
    gathered = dot(token_exp, unit, precision=HIGH)
    part = jnp.concatenate(
        [
            gathered.reshape(8, 20, 128),
            jnp.broadcast_to(jnp.sum(token_exp, axis=1).reshape(8, 2, 1), (8, 2, 128)),
            jnp.zeros((8, 2, 128), F32),
        ],
        axis=1,
    )
    mine = jnp.sum(slab_spread([part], 5, swap=True)[0], axis=0)
    denominator = class_exp + mine[20:22, 0]
    heads = jnp.einsum("hd,dhe->he", mine[:20].reshape(2, 1280), value_w.astype(F32), precision=HIGH)
    heads = (heads + class_exp[:, None] * class_val.astype(F32)) / denominator[:, None]
    attn_part = dot(heads.astype(BF16).reshape(1, 160), attn_rows, ((1,), (1,)))

    def slab_sum(vector, cid):
        return jnp.sum(slab_spread([pad_rows(vector, 16)], cid)[0], axis=0)[:10].reshape(1, 1280)

    block_mid = class_pre + slab_sum(attn_part, 6) + attn_out_bias
    mlp_input, mid_back = jax.vjp(lambda v: affine_norm(v, vit_gain[2], vit_shift[2]), block_mid)
    preact = dot(mlp_input.astype(BF16), in_share, ((1,), (1,))) + bias_share.astype(F32)
    active, gelu_back = jax.vjp(exact_gelu, preact)
    mlp_part = dot(active.astype(BF16), out_share)
    block_out = block_mid + slab_sum(mlp_part, 7) + mlp_out_bias
    post, post_back = jax.vjp(lambda v: affine_norm(v, vit_gain[3], vit_shift[3]), block_out)
    embed = dot(post.astype(BF16), vit)
    score, score_back = jax.vjp(lambda v: match_score(v, text_embed), embed)
    d_embed = score_back(jnp.full_like(score, -1.0 / total_images))[0].astype(BF16)
    d_post = dot(d_embed, vit, ((1,), (1,)))
    d_second = post_back(d_post)[0]
    d_active = dot(d_second.astype(BF16), out_share, ((1,), (1,)))
    d_pre = gelu_back(d_active)[0].astype(BF16)
    d_input = slab_sum(dot(d_pre, in_share), 8)
    d_first = d_second + mid_back(d_input)[0]
    d_heads = dot(d_first.astype(BF16), attn_rows).astype(BF16).reshape(2, HEAD_DIM)
    value_dir = jnp.einsum("he,dhe->hd", d_heads, value_w, preferred_element_type=F32)
    expected = jnp.sum(d_heads.astype(F32) * heads, axis=-1)
    back = jnp.concatenate(
        [
            value_dir.reshape(20, 128),
            jnp.broadcast_to(denominator[:, None], (2, 128)),
            jnp.broadcast_to(expected[:, None], (2, 128)),
        ]
    )
    back = slab_spread([back], 9)[0]
    value_dirs = back[:, :20].reshape(16, 1280)
    token_weight = token_exp / back[:, 20:22, :1].reshape(16, 1)
    token_dots = dot(value_dirs, unit, ((1,), (1,)), HIGH)
    logit_grads = token_weight * (token_dots - back[:, 22:24, :1].reshape(16, 1))
    weights = jnp.concatenate([logit_grads / root, token_weight.astype(BF16).astype(F32)])
    d_unit = dot(weights, jnp.concatenate([key_dirs, value_dirs]), ((0,), (0,)), HIGH)
    d_embedded = pre_back(unit_back(d_unit)[0])[0].astype(BF16)
    d_patches = dot(d_embedded, patch)
    d_image = d_patches.reshape(2, 16, 3, 14, 14).transpose(2, 0, 3, 1, 4).reshape(3, 28, 224)
    d_image = d_image / (2.0 * pix_std)
    rims = jnp.stack([d_image[:, 0], d_image[:, 27]])
    rims = slab_spread([pad_rows(rims, 16)], 10)[0].reshape(ns, 2048)[:, :1344].reshape(ns, 2, 3, 224)
    d_image = jnp.concatenate([rims[before, 1][:, None], d_image, rims[after, 0][:, None]], axis=1)
    d_narrow = jnp.einsum("iry,cij->rcyj", row_w, d_image, precision=HIGH).reshape(16, 24, 224)
    n_high = d_narrow.astype(BF16)
    n_low = (d_narrow - n_high.astype(F32)).astype(BF16)

    def widen(a, b):
        return jnp.einsum("rkj,xqj->rxkq", a, b, preferred_element_type=F32)

    d_cells = widen(n_high, t_high) + (widen(n_low, t_high) + widen(n_high, t_low))
    d_cells = d_cells.astype(BF16).reshape(16, 192, 128)
    d_act = jnp.einsum("ko,rkq->roq", head_t, d_cells, preferred_element_type=F32)
    gate = jax.nn.sigmoid(gained)
    d_normed = d_act * (gate * (1.0 + gained * (1.0 - gate))) * gain_c
    sums = jnp.stack([jnp.sum(d_normed, axis=(0, 2)), jnp.sum(d_normed * normed, axis=(0, 2))])
    totals = jnp.sum(slab_spread([sums.reshape(8, 128)], 11)[0], axis=0)
    totals = jnp.sum(totals.reshape(2, GROUPS, 16), axis=2) / cells
    d_conv = (
        (d_normed - jnp.repeat(totals[0], 16)[None, :, None])
        - normed * jnp.repeat(totals[1], 16)[None, :, None]
    ) * inverse_c
    d_cols = jnp.einsum("ok,roq->rkq", conv, d_conv.astype(BF16), preferred_element_type=F32)
    d_lat = jnp.zeros((18, 16, 130), F32)
    for t in range(9):
        a, b = t // 3, t % 3
        d_lat = d_lat + jnp.pad(
            d_cols[:, 16 * t : 16 * t + 16], ((a, 2 - a), (0, 0), (b, 2 - b))
        )
    d_lat = d_lat[:, :, 1:129]
    rims = slab_spread([jnp.concatenate([d_lat[0], d_lat[17]])], 12)[0]
    from_low = jnp.where(place > 0, rims[before, 16:], 0.0)
    from_high = jnp.where(place < ns - 1, rims[after, :16], 0.0)
    d_lat = jnp.concatenate(
        [(d_lat[1] + from_low)[None], d_lat[2:16], (d_lat[16] + from_high)[None]]
    )
    d_vel = (-sigma * (d_lat / LAT_SCALE)).astype(BF16).reshape(8, 32, 128)
    d_vel = jnp.einsum("ikq,hjq->ijhk", d_vel, inter, preferred_element_type=F32)
    d_vel = dot(d_vel.astype(BF16).reshape(512, 64), perm, ((1,), (1,))).astype(BF16)
    return grad_total(dot(modulated, d_vel, ((0,), (0,)))), score


def solution(mesh):
    placed = (
        P(("fsdp", "grp"), "slab", None, None),
        P(("fsdp", "grp"), None, None),
        P(("fsdp", "grp"), "slab", None, None),
        P(("fsdp", "grp")),
        P("fsdp", None),
        P(),
        P(None, None, None, "fsdp"),
        P(),
        P(),
        P(),
        P("fsdp", None),
        P(),
        P(None, "fsdp"),
        P("slab", None),
        P(),
        P(),
        P(),
        P("fsdp", "slab"),
        P("slab", "fsdp"),
        P(),
        P(None, ("fsdp", "slab")),
        P(("fsdp", "slab")),
        P(("fsdp", "slab"), None),
        P(),
        P("fsdp", None),
        P(("fsdp", "grp"), None),
    )
    return jax.shard_map(
        local,
        mesh=mesh,
        in_specs=placed,
        out_specs=(P("fsdp", None), P(("fsdp", "grp"))),
        check_vma=False,
    )
```

```python
import functools

import jax
import jax.numpy as jnp
import numpy as np
from jax import lax
from jax.experimental import pallas as pl
from jax.experimental.pallas import tpu as pltpu
from jax.sharding import PartitionSpec as P

HEAD_DIM = 80
STEPS = 28
LAT_SCALE = 0.3611
LAT_SHIFT = 0.1159
PIX_MEAN = (0.48145466, 0.4578275, 0.40821073)
PIX_STD = (0.26862954, 0.26130258, 0.27577711)
HIGH = lax.Precision.HIGHEST
MESH = pl.DeviceIdType.MESH
F32 = jnp.float32
BF16 = jnp.bfloat16
ANY = pl.BlockSpec(memory_space=pl.ANY)
VMEM = pl.BlockSpec(memory_space=pltpu.VMEM)
SMEM = pl.BlockSpec(memory_space=pltpu.SMEM)
ROOT = HEAD_DIM**0.5
WIDTH = 1280
WIDE = 1536
CELLS = 128 * 128 * 16
NF, NS, NZ = 32, 8, 16
LANES = 2048


def nn(a, b, precision=None):
    return lax.dot_general(
        a, b, (((1,), (0,)), ((), ())), precision=precision, preferred_element_type=F32
    )


def nt(a, b, precision=None):
    return lax.dot_general(
        a, b, (((1,), (1,)), ((), ())), precision=precision, preferred_element_type=F32
    )


def halves(values):
    high = values.astype(BF16)
    return high, (values - high.astype(F32)).astype(BF16)


def three(product, a, b):
    return product(a[0], b[0]) + (product(a[1], b[0]) + product(a[0], b[1]))


def remote(source, dest, send, recv, target):
    return pltpu.make_async_remote_copy(
        src_ref=source, dst_ref=dest, send_sem=send, recv_sem=recv,
        device_id=target, device_id_type=MESH,
    )


def iota(shape, dim):
    return lax.broadcasted_iota(jnp.int32, shape, dim)


def norm_stats(values, mask, epsilon):
    average = jnp.sum(values, axis=-1, keepdims=True) * (1.0 / WIDTH)
    centered = (values - average) * mask
    square = jnp.sum(centered * centered, axis=-1, keepdims=True) * (1.0 / WIDTH)
    inverse = 1.0 / jnp.sqrt(square + epsilon)
    return centered * inverse, inverse


def norm_back(grads, scaled, inverse, gain):
    grads = grads * gain
    first = jnp.sum(grads, axis=-1, keepdims=True) * (1.0 / WIDTH)
    second = jnp.sum(grads * scaled, axis=-1, keepdims=True) * (1.0 / WIDTH)
    return (grads - first - scaled * second) * inverse


class Weights:
    def __init__(self, s_in, r_in, s_buf, r_buf, sems):
        self.s_in, self.r_in, self.s_buf, self.r_buf = s_in, r_in, s_buf, r_buf
        (self.z_send, self.z_recv, self.sh_send, self.sh_recv, self.fw_send, self.fw_recv,
         self.loc, self.pair_sem, self.ring_send, self.ring_recv, self.core_sem) = sems
        self.f = lax.axis_index("fsdp")
        self.g = lax.axis_index("grp")
        self.s = lax.axis_index("slab")
        self.w = self.g * NS + self.s
        self.z, self.half = self.f // 2, lax.rem(self.f, 2)
        self.core = {"grp": 1 - self.g}
        self.sent = []

    def r_start(self, slot):
        source = self.r_in.at[slot, self.w]
        mine = pltpu.make_async_copy(
            source, self.r_buf.at[slot, self.w, self.f], self.loc.at[slot]
        )
        mine.start()

        def send(d, carry):
            target = {"fsdp": lax.rem(self.f + d, NF)}
            remote(
                source, self.r_buf.at[slot, self.w, self.f],
                self.z_send.at[slot], self.z_recv.at[slot], target,
            ).start()
            return carry

        lax.fori_loop(1, NF, send, 0)

    def r_share(self, slot):
        block = self.r_buf.at[slot, self.w]
        many = self.r_buf.at[slot, self.w, pl.ds(0, NF - 1)]
        remote(many, many, self.z_send.at[slot], self.z_recv.at[slot], self.core).wait_recv()
        pltpu.make_async_copy(
            self.r_in.at[slot, self.w], self.r_buf.at[slot, self.w, self.f], self.loc.at[slot]
        ).wait()
        for d in range(1, NS):
            remote(
                block, block, self.sh_send.at[slot, d - 1], self.sh_recv.at[slot, d - 1],
                {"slab": lax.rem(self.s + d, NS)},
            ).start()

    def r_core(self, slot):
        for d in range(1, NS):
            block = self.r_buf.at[slot, self.g * NS + lax.rem(self.s + NS - d, NS)]
            remote(
                block, block, self.sh_send.at[slot, d - 1], self.sh_recv.at[slot, d - 1], self.core
            ).wait_recv()
        many = self.r_buf.at[slot, pl.ds(self.g * NS, NS)]
        remote(many, many, self.fw_send.at[slot], self.fw_recv.at[slot], self.core).start()

    def r_done(self, slot):
        many = self.r_buf.at[slot, pl.ds((1 - self.g) * NS, NS)]
        remote(many, many, self.fw_send.at[slot], self.fw_recv.at[slot], self.core).wait_recv()

    def s_pair(self):
        dest = self.s_buf.at[self.g, self.z, self.half]
        return remote(
            self.s_in.at[self.g], dest, self.pair_sem.at[0], self.pair_sem.at[1],
            {"fsdp": self.z * 2 + 1 - self.half},
        ), pltpu.make_async_copy(self.s_in.at[self.g], dest, self.loc.at[3])

    def s_start(self):
        for copy in self.s_pair():
            copy.start()

    def s_step(self, step, way):
        sign = NZ - 1 if way == 0 else 1
        block = self.s_buf.at[self.g, lax.rem(self.z + sign * step, NZ)]
        hop = 1 if way == 0 else NZ - 1
        target = {"fsdp": lax.rem(self.z + hop, NZ) * 2 + self.half}
        slot = way * 8 + step
        return remote(block, block, self.ring_send.at[slot], self.ring_recv.at[slot], target)

    def s_share(self, block):
        block = self.s_buf.at[self.g, lax.rem(block, NZ)]
        remote(block, block, self.core_sem.at[0], self.core_sem.at[1], self.core).start()

    def s_pump(self, step):
        steps = (NZ // 2, NZ // 2 - 1)
        if step == 0:
            pair, own = self.s_pair()
            own.wait()
            pair.wait_recv()
            self.s_share(self.z)
        for way in (0, 1):
            if 0 < step <= steps[way]:
                self.s_step(step - 1, way).wait_recv()
            if step < steps[way]:
                self.s_step(step, way).start()
            if 0 < step <= steps[way]:
                self.s_share(self.z + (NZ - step if way == 0 else step))

    def s_done(self):
        theirs, mine = self.s_buf.at[1 - self.g], self.s_buf.at[self.g]
        remote(theirs, theirs, self.core_sem.at[0], self.core_sem.at[1], self.core).wait_recv()
        remote(mine, mine, self.core_sem.at[0], self.core_sem.at[1], self.core).wait_send()
        self.s_pair()[0].wait_send()
        for way, steps in ((0, NZ // 2), (1, NZ // 2 - 1)):
            for step in range(steps):
                self.s_step(step, way).wait_send()

    def r_finish(self, slot):
        many = self.r_buf.at[slot, self.w, pl.ds(0, NF - 1)]
        remote(many, many, self.z_send.at[slot], self.z_recv.at[slot], self.core).wait_send()
        block = self.r_buf.at[slot, self.w]
        for d in range(1, NS):
            remote(
                block, block, self.sh_send.at[slot, d - 1], self.sh_recv.at[slot, d - 1], self.core
            ).wait_send()
        many = self.r_buf.at[slot, pl.ds(self.g * NS, NS)]
        remote(many, many, self.fw_send.at[slot], self.fw_recv.at[slot], self.core).wait_send()


def greet(targets):
    barrier = pltpu.get_barrier_semaphore()
    for target in targets:
        pl.semaphore_signal(barrier, inc=1, device_id=target, device_id_type=MESH)
    pl.semaphore_wait(barrier, len(targets))


def block_targets(g, s):
    found = []
    for d in range(1, 2 * NS):
        other_g = lax.rem(g + d // NS, 2)
        other_s = lax.rem(s + d % NS, NS)
        found.append((other_g * NS + other_s, {"grp": other_g, "slab": other_s}))
    return found


def greet_all():
    f, g, s = lax.axis_index("fsdp"), lax.axis_index("grp"), lax.axis_index("slab")
    greet(
        [target for _, target in block_targets(g, s)]
        + [{"fsdp": lax.rem(f + d, NF)} for d in range(1, NF)]
    )


def reduce_gradient(mine, landed, terms, arrived, collected, sems):
    a_send, a_recv, b_send, b_recv, c_send, c_recv = sems
    f, g, s = lax.axis_index("fsdp"), lax.axis_index("grp"), lax.axis_index("slab")
    w = g * NS + s
    block = block_targets(g, s)
    copies = []
    for d, (index, target) in enumerate(block):
        copy = remote(mine.at[index], landed.at[w], a_send.at[d], a_recv.at[d], target)
        copy.start()
        copies.append(copy)
    landed[w] = mine[w]
    for copy in copies:
        copy.wait()
    total = landed[0].astype(F32)
    for index in range(1, 2 * NS):
        total = total + landed[index].astype(F32)
    for index in range(NF):
        rows, lanes = 4 * (index // 8), 96 * (index % 8)
        terms[index, :, 0:96] = total[rows : rows + 4, lanes : lanes + 96]
        terms[index, :, 96:128] = jnp.zeros((4, 32), F32)
    copies = []
    for d in range(1, NF):
        p = lax.rem(f + d, NF)
        copy = remote(terms.at[p], arrived.at[f], b_send.at[d - 1], b_recv.at[d - 1], {"fsdp": p})
        copy.start()
        copies.append(copy)
    arrived[f] = terms[f]
    for copy in copies:
        copy.wait()
    collected[w] = jnp.sum(arrived[...], axis=0)
    copies = []
    for d, (index, target) in enumerate(block):
        copy = remote(collected.at[w], collected.at[w], c_send.at[d], c_recv.at[d], target)
        copy.start()
        copies.append(copy)
    for copy in copies:
        copy.wait()


def step_kernel(
    fetch, hidden, s_in, r_in, mods, noisy, sigma_ref, proj_bias, vecs, text, chan, head_bias,
    perm, perm_t, inter, tth, ttl, rmh, rml, ph0, ph1, lane_rows,
    grad_out, score_out,
    hid, mod, s_buf, r_buf, proj_full, ext, halo_out, halo_in, nrm, dnrm, acc, stat_out, stat_in,
    cols_buf, pix, head_t, head_p, edge_out, edge_in, kd_out, kd_in, dirs, u_out, u_in,
    row_out, row_in, vd_out, vd_in, rim_out, rim_in, gsplit, mine, landed, terms, arrived, collected,
    x_send, x_recv, hid_sem, *sems,
):
    s = lax.axis_index("slab")
    low, high = s > 0, s < NS - 1
    low_f, high_f = jnp.where(low, 1.0, 0.0), jnp.where(high, 1.0, 0.0)
    before, after = {"slab": lax.rem(s + NS - 1, NS)}, {"slab": lax.rem(s + 1, NS)}
    hid_copy = pltpu.make_async_copy(hidden, hid, hid_sem.at[0])
    hid_copy.start()
    sigma = sigma_ref[0, 0]
    live = []

    def to_all(kind, source, dest, swap=False):
        copies = []
        for d in range(1, NS):
            p = lax.rem(s + d, NS)
            copies.append(
                remote(
                    source.at[p] if swap else source, dest.at[s],
                    x_send.at[kind, d - 1], x_recv.at[kind, d - 1], {"slab": p},
                )
            )
        for copy in copies:
            copy.start()
        live.extend(copies)
        return copies

    def to_sides(kind, source, dest):
        copies = [
            remote(source.at[0], dest.at[0], x_send.at[kind, 0], x_recv.at[kind, 0], after),
            remote(source.at[1], dest.at[1], x_send.at[kind, 1], x_recv.at[kind, 1], before),
        ]
        for copy in copies:
            copy.start()
        live.extend(copies)
        return copies

    def landed_all(copies):
        for copy in copies:
            copy.wait_recv()

    if fetch:
        greet_all()
        weights = Weights(s_in, r_in, s_buf, r_buf, sems[:11])
        weights.r_start(0)
        weights.s_start()
        weights.r_start(1)
        weights.r_start(2)
    else:
        greet([{"slab": lax.rem(s + d, NS)} for d in range(1, NS)])
        s_buf[...] = s_in[...]
        r_buf[...] = r_in[...]
        weights = None

    def pump(step):
        if weights is not None:
            weights.s_pump(step)

    hid_copy.wait()
    scale = 1.0 + mods[1:2].astype(F32)
    shift = mods[0:1].astype(F32)

    def modulate(lo, hi):
        def body(i, carry):
            rows = pl.ds(pl.multiple_of(i * 16, 16), 16)
            values = hid[rows, :].astype(F32)
            average = jnp.mean(values, axis=-1, keepdims=True)
            centered = values - average
            square = jnp.mean(centered * centered, axis=-1, keepdims=True)
            scaled = centered * (1.0 / jnp.sqrt(square + 1e-06))
            mod[rows, :] = (scaled * scale + shift).astype(BF16)
            return carry

        lax.fori_loop(lo, hi, body, 0)

    modulate(0, 16)
    pump(0)
    modulate(16, 32)
    if weights is not None:
        weights.r_share(0)
        weights.s_pump(1)
        weights.r_core(0)
        weights.r_done(0)

    def blocks(first, count):
        parts = [r_buf[n // 16, n % 16] for n in range(first, first + count)]
        return jnp.concatenate(parts, axis=1).reshape(NF * 16 * count, 128)

    def s_unit(index):
        return s_buf[index // 9, :, :, index % 9].reshape(WIDE, 128)

    for f in range(NF):
        for n in range(6):
            proj_full[96 * f + 16 * n : 96 * f + 16 * n + 16, :] = r_buf[0, n, f]
    velocity = nn(mod[...], proj_full[...])[:, :64] + proj_bias[...]
    clean = noisy[...].astype(F32) - sigma * velocity
    lat_tok = (clean / LAT_SCALE + LAT_SHIFT).astype(BF16)
    tok_t = nt(perm_t[...], lat_tok)
    stacked = jnp.concatenate(
        [
            jnp.concatenate(
                [tok_t[0:32, 128 * k : 128 * k + 128], tok_t[32:64, 128 * k : 128 * k + 128]], axis=1
            )
            for k in range(4)
        ],
        axis=0,
    ).astype(BF16)
    latent = nn(stacked, inter[...]).astype(BF16)
    for k in range(4):
        for i2 in range(2):
            for p in range(2):
                r = 4 * k + 2 * i2 + p + 1
                for b in range(3):
                    at = (i2 * 3 + b) * 128
                    ext[16 * b : 16 * b + 16, 128 * r : 128 * r + 128] = latent[
                        32 * k + 16 * p : 32 * k + 16 * p + 16, at : at + 128
                    ]
    halo_out[0] = ext[:, 2048:2176]
    halo_out[1] = ext[:, 128:256]
    copies = to_sides(0, halo_out, halo_in)
    identity = (iota((512, 512), 0) == iota((512, 512), 1)).astype(F32)
    same = (iota((512, 512), 0) // 16 == iota((512, 512), 1) // 16).astype(F32)
    chan_cols = nt(identity, chan[...], HIGH)
    conv_bias, gain, gshift = chan_cols[:, 0:1], chan_cols[:, 1:2], chan_cols[:, 2:3]
    eye = (iota((128, 128), 0) == iota((128, 128), 1)).astype(BF16)
    conv0 = r_buf[0, 6].reshape(512, 128)
    head0 = r_buf[0, 7].reshape(512, 128)
    tail = r_buf[0, 8].reshape(512, 128)
    head_p[...] = (nn(head0, ph0[...]) + nn(tail, ph1[...])).astype(BF16)
    head_t[...] = (
        lax.dot_general(ph0[...], head0, (((0,), (1,)), ((), ())), preferred_element_type=F32)
        + lax.dot_general(ph1[...], tail, (((0,), (1,)), ((), ())), preferred_element_type=F32)
    ).astype(BF16)
    bias_cols = nt(
        lax.dot_general(
            ph0[...].astype(F32), eye.astype(F32), (((0,), (0,)), ((), ())),
            preferred_element_type=F32,
        ),
        head_bias[:, 0:128], HIGH,
    ) + nt(
        lax.dot_general(
            ph1[...].astype(F32), eye.astype(F32), (((0,), (0,)), ((), ())),
            preferred_element_type=F32,
        ),
        head_bias[:, 128:256], HIGH,
    )
    head_col = bias_cols[:, 0:1]
    pump(2)
    landed_all(copies)
    ext[:, 0:128] = (halo_in[0].astype(F32) * low_f).astype(BF16)
    ext[:, 2176:2304] = (halo_in[1].astype(F32) * high_f).astype(BF16)
    acc[...] = jnp.zeros_like(acc)

    def conv_chunk(i, carry):
        at = pl.multiple_of(i * 256, 256)
        parts = [ext[:, pl.ds(pl.multiple_of(at + 128 * a, 128), 256)] for a in range(3)]
        columns = jnp.concatenate(parts + [jnp.zeros((112, 256), BF16)], axis=0)
        out = nn(conv0, columns[0:128]) + nn(tail, columns[128:256]) + conv_bias
        nrm[:, pl.ds(at, 256)] = out
        acc[0] += out[:, 0:128] + out[:, 128:256]
        square = out * out
        acc[1] += square[:, 0:128] + square[:, 128:256]
        return carry

    lax.fori_loop(0, 8, conv_chunk, 0)

    def group_totals(kind, step=None):
        ones = jnp.ones((8, 128), F32)
        first, second = nt(ones, acc[0], HIGH), nt(ones, acc[1], HIGH)
        k = kind - 1
        stat_out[k] = jnp.where(iota((8, 512), 0) == 0, first, second)
        copies = to_all(kind, stat_out.at[k], stat_in.at[k])
        stat_in[k, s] = stat_out[k]
        if step is not None:
            pump(step)
        landed_all(copies)
        total = stat_in[k, 0]
        for index in range(1, NS):
            total = total + stat_in[k, index]
        columns = nt(same, total, HIGH)
        return columns[:, 0:1] * (1.0 / CELLS), columns[:, 1:2] * (1.0 / CELLS)

    average, square = group_totals(1, 3)
    inverse = 1.0 / jnp.sqrt(square - average * average + 1e-06)
    if weights is not None:
        weights.r_share(1)
        weights.r_share(2)

    def head_chunk(i, carry):
        at = pl.multiple_of(i * 256, 256)
        normed = (nrm[:, pl.ds(at, 256)] - average) * inverse
        nrm[:, pl.ds(at, 256)] = normed
        gained = normed * gain + gshift
        active = (gained * (1.0 / (1.0 + jnp.exp(-gained)))).astype(BF16)
        cells = (nn(head_t[...], active) + head_col).astype(BF16)
        for rr in range(2):
            rows = pl.ds(pl.multiple_of(i * 64 + 32 * rr, 32), 32)
            for x in range(8):
                pix[rows, 128 * x : 128 * x + 128] = cells[
                    32 * x : 32 * x + 32, 128 * rr : 128 * rr + 128
                ]
        return carry

    lax.fori_loop(0, 8, head_chunk, 0)
    pump(4)
    narrow = halves(nt(tth[...], pix[...]) + nt(ttl[...], pix[...]))
    raw = jnp.zeros((80, 512), F32)
    for m in range(3):
        part = [half[80 * m : 80 * m + 80] for half in narrow]
        table = [rmh[512 * m : 512 * m + 512, :], rml[512 * m : 512 * m + 512, :]]
        raw = raw + three(nn, part, table)
    edge_out[0, 0] = raw[:, 256:384]
    edge_out[0, 1] = raw[:, 384:512]
    copies = to_sides(2 + 1, edge_out.at[0], edge_in.at[0])
    pump(5)
    if weights is not None:
        weights.r_core(1)
        weights.s_pump(6)
    corr0 = jnp.where(low, 1.0, lane_rows[0:1, :])
    corr1 = jnp.where(high, 1.0, lane_rows[1:2, :])
    img_scale, img_shift = lane_rows[2:3, :], lane_rows[3:4, :]
    if weights is not None:
        weights.r_done(1)
    landed_all(copies)
    top = (raw[:, 0:128] * corr0 + edge_in[0, 0] * low_f) * img_scale + img_shift
    bottom = (raw[:, 128:256] * corr1 + edge_in[0, 1] * high_f) * img_scale + img_shift
    patches = jnp.concatenate(
        [
            jnp.concatenate([part[16 * u : 16 * u + 16] for u in range(5)], axis=1)
            for part in (top, bottom)
        ],
        axis=0,
    ).astype(BF16)
    embedded = vecs[16:48, :]
    for u in range(5):
        embedded = embedded + nt(patches[:, 128 * u : 128 * u + 128], blocks(9 + 3 * u, 3))
    lane = iota((1, WIDE), 1)
    inner = lax.rem(lane, 48)
    mask = (inner < 40).astype(F32)
    gains = [vecs[1 + i : 2 + i, :] for i in range(4)]
    shifts = [vecs[5 + i : 6 + i, :] for i in range(4)]
    hat0, inv0 = norm_stats(embedded, mask, 1e-05)
    hat1, inv1 = norm_stats(hat0 * gains[0] + shifts[0], mask, 1e-05)
    unit = hat1 * gains[1] + shifts[1]
    unit_b = unit.astype(BF16)
    unit = unit_b.astype(F32)
    if weights is not None:
        weights.s_pump(7)
        weights.r_core(2)
        weights.s_pump(8)
        weights.s_done()

    class_hat, _ = norm_stats(vecs[0:1, :], mask, 1e-05)
    class_pre = class_hat * gains[0] + shifts[0]
    class_hat, _ = norm_stats(class_pre, mask, 1e-05)
    class_unit = jnp.broadcast_to(class_hat * gains[1] + shifts[1], (8, WIDE)).astype(BF16)
    attn = [s_unit(i) for i in range(4)]
    class_qkv = jnp.concatenate([nn(class_unit, attn[i]) for i in range(4)], axis=1)
    class_qkv = class_qkv.astype(BF16).astype(F32)
    place512 = iota((8, 512), 1)
    row512 = iota((8, 512), 0)
    start = jnp.where(row512 == 0, 0, 240)
    in_head = row512 < 2
    key_at = in_head & (place512 >= start + 80) & (place512 < start + 160)
    val_at = in_head & (place512 >= start + 160) & (place512 < start + 240)
    query = jnp.where(key_at, pltpu.roll(class_qkv, 80, 1), 0.0)
    class_exp = jnp.exp(jnp.sum(query * class_qkv, axis=-1, keepdims=True) / ROOT)
    query_b = query.astype(BF16)
    key_dir = nt(query_b[:, 0:128], attn[0])
    for i in range(1, 4):
        key_dir = key_dir + nt(query_b[:, 128 * i : 128 * i + 128], attn[i])
    kd_out[...] = key_dir[0:2]
    copies = to_all(4, kd_out, kd_in)
    kd_in[s] = key_dir[0:2]
    landed_all(copies)
    for index in range(NS):
        dirs[2 * index : 2 * index + 2, :] = kd_in[index]
    token_exp = jnp.exp(nt(dirs[0:16, :], unit, HIGH) / ROOT)
    gathered = nn(token_exp, unit, HIGH)
    sums = jnp.broadcast_to(jnp.sum(token_exp, axis=1, keepdims=True), (16, WIDE))
    for index in range(NS):
        u_out[index, 0:2] = gathered[2 * index : 2 * index + 2]
        u_out[index, 2:4] = sums[2 * index : 2 * index + 2]
    copies = to_all(5, u_out, u_in, swap=True)
    u_in[s] = u_out[s]
    landed_all(copies)
    total = u_in[0]
    for index in range(1, NS):
        total = total + u_in[index]
    denominator = class_exp[0:2] + total[2:4, 0:1]
    mixed = halves(jnp.concatenate([total[0:2], jnp.zeros((6, WIDE), F32)], axis=0))
    first = nn(mixed[0], attn[1]) + nn(mixed[1], attn[1])
    second = nn(mixed[0], attn[3]) + nn(mixed[1], attn[3])
    heads1 = jnp.where(val_at[0:1, 128:256], first[0:1] + class_exp[0:1] * class_qkv[0:1, 128:256], 0.0)
    heads3 = jnp.where(val_at[1:2, 384:512], second[1:2] + class_exp[1:2] * class_qkv[0:1, 384:512], 0.0)
    heads1 = heads1 / denominator[0:1]
    heads3 = heads3 / denominator[1:2]
    rows1 = s_unit(4)
    rows3 = s_unit(5)

    def wide8(row):
        return jnp.broadcast_to(row, (8, row.shape[1])).astype(BF16)

    attn_part = nt(wide8(heads1), rows1) + nt(wide8(heads3), rows3)

    def slab_sum(kind, k, row):
        row_out[k] = row[0:1]
        copies = to_all(kind, row_out.at[k], row_in.at[k])
        row_in[k, s] = row[0:1]
        landed_all(copies)
        total = row_in[k, 0]
        for index in range(1, NS):
            total = total + row_in[k, index]
        return total

    block_mid = class_pre + slab_sum(6, 0, attn_part) + vecs[9:10, :]
    hat2, inv2 = norm_stats(block_mid, mask, 1e-05)
    mlp_input = hat2 * gains[2] + shifts[2]
    mlp_input = wide8(jnp.where(lane == 40, 1.0, mlp_input))
    hidden_units = [s_unit(6 + i) for i in range(12)]
    preact = nt(mlp_input[:, 0:128], hidden_units[0])
    for i in range(1, 12):
        preact = preact + nt(mlp_input[:, 128 * i : 128 * i + 128], hidden_units[i])
    preact = jnp.where(inner < 20, preact, 0.0)
    cdf = 0.5 * (1.0 + lax.erf(preact * 0.7071067811865476))
    active = preact * cdf
    active = pltpu.roll(active, 20, 1).astype(BF16)
    mlp_part = jnp.concatenate([nn(active, hidden_units[i]) for i in range(12)], axis=1)
    block_out = block_mid + slab_sum(7, 1, mlp_part) + vecs[10:11, :]
    hat3, inv3 = norm_stats(block_out, mask, 1e-05)
    post = wide8(hat3 * gains[3] + shifts[3])
    if weights is not None:
        weights.r_done(2)
    vit = [blocks(24 + 3 * u, 3) for u in range(8)]
    embed = jnp.concatenate([nn(post, vit[u]) for u in range(8)], axis=1)[0:1]
    words = text[...]
    dots = jnp.sum(embed * words, axis=-1, keepdims=True)
    size_e = jnp.sum(embed * embed, axis=-1, keepdims=True) + 1e-06
    size_t = jnp.sum(words * words, axis=-1, keepdims=True) + 1e-06
    sizes = jnp.sqrt(size_e) * jnp.sqrt(size_t)
    score = 100.0 * dots / sizes
    score_out[...] = jnp.broadcast_to(score, (8, 128))
    d_embed = wide8((-1.0 / 64.0) * (100.0 * words / sizes - score * embed / size_e))
    d_post = nt(d_embed[:, 0:128], vit[0])
    for u in range(1, 8):
        d_post = d_post + nt(d_embed[:, 128 * u : 128 * u + 128], vit[u])
    d_second = norm_back(d_post[0:1], hat3, inv3, gains[3])
    d_second_b = wide8(d_second)
    d_active = nt(d_second_b[:, 0:128], hidden_units[0])
    for i in range(1, 12):
        d_active = d_active + nt(d_second_b[:, 128 * i : 128 * i + 128], hidden_units[i])
    d_active = pltpu.roll(d_active, WIDE - 20, 1)
    slope = cdf + preact * jnp.exp(-0.5 * preact * preact) * 0.3989422804014327
    d_pre = jnp.where(inner < 20, d_active * slope, 0.0).astype(BF16)
    input_part = jnp.concatenate([nn(d_pre, hidden_units[i]) for i in range(12)], axis=1)
    d_input = slab_sum(8, 2, input_part)
    d_first = wide8(d_second + norm_back(d_input, hat2, inv2, gains[2]))
    d_heads1 = nn(d_first, rows1).astype(BF16)
    d_heads3 = nn(d_first, rows3).astype(BF16)
    value0 = nt(jnp.where(val_at[0:1, 128:256], d_heads1.astype(F32), 0.0).astype(BF16), attn[1])
    value1 = nt(jnp.where(val_at[1:2, 384:512], d_heads3.astype(F32), 0.0).astype(BF16), attn[3])
    expect0 = jnp.sum(d_heads1[0:1].astype(F32) * heads1, axis=-1, keepdims=True)
    expect1 = jnp.sum(d_heads3[0:1].astype(F32) * heads3, axis=-1, keepdims=True)
    vd_out[0:1, :] = value0[0:1]
    vd_out[1:2, :] = value1[0:1]
    vd_out[2:3, :] = jnp.where(lane < 128, denominator[0:1], denominator[1:2])
    vd_out[3:4, :] = jnp.where(lane < 128, expect0, expect1)
    copies = to_all(9, vd_out, vd_in)
    vd_in[s] = vd_out[...]
    token_logits = nt(unit, dirs[0:16, :], HIGH) / ROOT
    landed_all(copies)
    head_at = iota((1, 16), 1)
    denominators = jnp.zeros((1, 16), F32)
    expects = jnp.zeros((1, 16), F32)
    for index in range(NS):
        dirs[16 + 2 * index : 18 + 2 * index, :] = vd_in[index, 0:2]
        for h in range(2):
            here = head_at == 2 * index + h
            denominators = jnp.where(here, vd_in[index, 2:3, 128 * h : 128 * h + 1], denominators)
            expects = jnp.where(here, vd_in[index, 3:4, 128 * h : 128 * h + 1], expects)
    token_weight = jnp.exp(token_logits) / denominators
    token_dots = nt(unit, dirs[16:32, :], HIGH)
    logit_grads = token_weight * (token_dots - expects)
    d_unit = nn(logit_grads / ROOT, dirs[0:16, :], HIGH) + nn(
        token_weight.astype(BF16).astype(F32), dirs[16:32, :], HIGH
    )
    d_pre_x = norm_back(d_unit, hat1, inv1, gains[1])
    d_embedded = norm_back(d_pre_x, hat0, inv0, gains[0]).astype(BF16)
    d_parts = [nn(d_embedded, blocks(9 + 3 * u, 3)) for u in range(5)]
    d_top = jnp.concatenate([part[0:16] for part in d_parts], axis=0) * img_scale
    d_bottom = jnp.concatenate([part[16:32] for part in d_parts], axis=0) * img_scale
    edge_out[1, 0] = d_bottom
    edge_out[1, 1] = d_top
    copies = to_sides(10, edge_out.at[1], edge_in.at[1])
    landed_all(copies)
    d_raw = halves(
        jnp.concatenate(
            [d_top * corr0, d_bottom * corr1, edge_in[1, 1] * high_f, edge_in[1, 0] * low_f], axis=1
        )
    )
    d_narrow = []
    for m in range(3):
        table = [rmh[512 * m : 512 * m + 512, :], rml[512 * m : 512 * m + 512, :]]
        d_narrow.append(halves(three(nt, table, d_raw)))
    for x in range(8):
        d_pix = jnp.zeros((512, 128), F32)
        for m in range(3):
            table = [
                t[80 * m : 80 * m + 80, 128 * x : 128 * x + 128] for t in (tth, ttl)
            ]
            d_pix = d_pix + three(nn, d_narrow[m], table)
        d_pix = d_pix.astype(BF16)
        for r in range(16):
            cols_buf[32 * x : 32 * x + 32, 128 * r : 128 * r + 128] = d_pix[32 * r : 32 * r + 32]
    acc[...] = jnp.zeros_like(acc)

    def head_back(i, carry):
        at = pl.multiple_of(i * 256, 256)
        grads = nn(head_p[...], cols_buf[:, pl.ds(at, 256)])
        normed = nrm[:, pl.ds(at, 256)]
        gained = normed * gain + gshift
        gate = 1.0 / (1.0 + jnp.exp(-gained))
        grads = grads * (gate * (1.0 + gained * (1.0 - gate))) * gain
        dnrm[:, pl.ds(at, 256)] = grads
        acc[0] += grads[:, 0:128] + grads[:, 128:256]
        both = grads * normed
        acc[1] += both[:, 0:128] + both[:, 128:256]
        return carry

    lax.fori_loop(0, 8, head_back, 0)
    conv0_t = nt(eye, conv0).astype(BF16)
    tail_t = nt(eye[0:16], tail).astype(BF16)
    mean0, mean1 = group_totals(2)

    def conv_back(i, carry):
        at = pl.multiple_of(i * 256, 256)
        grads = (dnrm[:, pl.ds(at, 256)] - mean0 - nrm[:, pl.ds(at, 256)] * mean1) * inverse
        grads = grads.astype(BF16)
        dnrm[0:128, pl.ds(at, 256)] = nn(conv0_t, grads)
        dnrm[128:144, pl.ds(at, 256)] = nn(tail_t, grads)
        return carry

    lax.fori_loop(0, 8, conv_back, 0)
    total = jnp.zeros((16, 2304), F32)
    column = lax.rem(iota((16, 2304), 1), 128)
    for b in range(3):
        part = jnp.zeros((16, 2304), F32)
        for a in range(3):
            t = 3 * a + b
            pieces = [dnrm[16 * t : 16 * t + 16, :]]
            if a:
                pieces = [jnp.zeros((16, 128 * a), F32)] + pieces
            if a < 2:
                pieces = pieces + [jnp.zeros((16, 256 - 128 * a), F32)]
            part = part + jnp.concatenate(pieces, axis=1)
        if b == 0:
            part = jnp.where(column < 127, pltpu.roll(part, 2303, 1), 0.0)
        if b == 2:
            part = jnp.where(column > 0, pltpu.roll(part, 1, 1), 0.0)
        total = total + part
    rim_out[0] = total[:, 2176:2304]
    rim_out[1] = total[:, 0:128]
    copies = to_sides(11, rim_out, rim_in)
    landed_all(copies)
    rows = [total[:, 128 * r + 128 : 128 * r + 256] for r in range(16)]
    rows[0] = rows[0] + rim_in[0] * low_f
    rows[15] = rows[15] + rim_in[1] * high_f
    rows = [-sigma * (row / LAT_SCALE) for row in rows]
    stacked = jnp.concatenate(
        [
            jnp.concatenate([rows[4 * k + p], rows[4 * k + 2 + p]], axis=1)
            for k in range(4)
            for p in range(2)
        ],
        axis=0,
    ).astype(BF16)
    centre = jnp.concatenate([inter[:, 128:256], inter[:, 512:640]], axis=1)
    tok = nt(stacked, centre)
    tok_t = jnp.concatenate(
        [
            jnp.concatenate(
                [tok[32 * k : 32 * k + 32, 128 * q : 128 * q + 128] for k in range(4)], axis=1
            )
            for q in range(2)
        ],
        axis=0,
    ).astype(BF16)
    d_vel = nn(perm[...], tok_t).astype(BF16)
    for quarter in range(4):
        part = nn(d_vel, mod[:, 768 * quarter : 768 * quarter + 768])
        for w in range(2 * NS):
            gsplit[w, 4 * quarter : 4 * quarter + 4] = part[4 * w : 4 * w + 4]
    for copy in live:
        copy.wait_send()
    if weights is not None:
        for slot in range(3):
            weights.r_finish(slot)
        mine[...] = gsplit[...].astype(BF16)
        reduce_gradient(mine, landed, terms, arrived, collected, sems[11:])
        whole = jnp.concatenate([collected[w] for w in range(2 * NS)], axis=0)
        grad_out[...] = jnp.transpose(whole)[0:96, :]
    else:
        grad_out[...] = gsplit[...]


def resize_table(out_count, in_count):
    stretch = in_count / out_count
    centers = (np.arange(out_count) + 0.5) * stretch
    places = np.arange(in_count) + 0.5
    weights = np.maximum(0.0, 1.0 - np.abs(places[None, :] - centers[:, None]) / stretch)
    return weights / weights.sum(axis=1, keepdims=True)


def split_const(values):
    high = values.astype(np.float32).astype(jnp.bfloat16)
    rest = (values - high.astype(np.float64)).astype(jnp.bfloat16)
    return jnp.asarray(high), jnp.asarray(rest)


def constants():
    perm = np.zeros((64, 64))
    for c in range(16):
        for p in range(2):
            for q in range(2):
                perm[4 * c + 2 * p + q, q * 32 + p * 16 + c] = 1
    inter = np.zeros((2, 2, 64, 2, 3, 128))
    for q in range(2):
        for i2 in range(2):
            for j in range(64):
                for b in range(3):
                    at = 2 * j + q - b + 1
                    if 0 <= at < 128:
                        inter[q, i2, j, i2, b, at] = 1
    table = resize_table(224, 1024)
    columns = np.zeros((3, 5, 16, 8, 128))
    for m in range(3):
        for u in range(5):
            if 3 * u + m < 14:
                for pc in range(16):
                    columns[m, u, pc] = table[14 * pc + 3 * u + m].reshape(128, 8).T
    rows = np.zeros((3, 16, 4, 8, 4, 128))
    local = table[28 * 3 : 28 * 3 + 28, 128 * 3 : 128 * 3 + 128].reshape(28, 16, 8)
    to_next = table[28 * 4, 128 * 3 : 128 * 3 + 128].reshape(16, 8)
    to_prev = table[28 * 3 - 1, 128 * 3 : 128 * 3 + 128].reshape(16, 8)
    for m in range(3):
        for c in range(3):
            for a in range(14):
                at = 42 * m + 14 * c + a
                rows[m, :, c, :, 0, at] = local[a]
                rows[m, :, c, :, 1, at] = local[14 + a]
            rows[m, :, c, :, 2, 42 * m + 14 * c] = to_next
            rows[m, :, c, :, 3, 42 * m + 14 * c + 13] = to_prev
    lanes = np.zeros((8, 128))
    lanes[0:2] = 1
    for m in range(3):
        for c in range(3):
            for a in range(14):
                at = 42 * m + 14 * c + a
                lanes[2, at] = 0.5 / PIX_STD[c]
                lanes[3, at] = (0.5 - PIX_MEAN[c]) / PIX_STD[c]
            lanes[0, 42 * m + 14 * c] = table[0, 0] / table[28, 128]
            lanes[1, 42 * m + 14 * c + 13] = table[223, 1023] / table[27, 127]
    ph = np.zeros((2, 128, 8, 32))
    for c in range(3):
        for y in range(8):
            for x in range(8):
                k = 64 * c + 8 * y + x
                if k < 128:
                    ph[0, k, x, 8 * c + y] = 1
                else:
                    ph[1, 16 + k - 128, x, 8 * c + y] = 1
    tth, ttl = split_const(columns.reshape(240, 1024))
    rmh, rml = split_const(rows.reshape(1536, 512))
    one = lambda v: jnp.asarray(v.astype(jnp.bfloat16))
    ph = ph.reshape(2, 128, 256)
    return (
        one(perm), one(perm.T), one(inter.reshape(256, 768)), tth, ttl, rmh, rml,
        one(ph[0]), one(ph[1]), jnp.asarray(lanes.astype(np.float32)),
    )


def widen(values):
    shape = values.shape[:-1]
    view = values.reshape(shape + (32, 40))
    return jnp.pad(view, [(0, 0)] * len(shape) + [(0, 0), (0, 8)]).reshape(shape + (WIDE,))


def pack_weights(proj, conv, head, patch, attn_in, attn_out, mlp_in, mlp_bias, mlp_out, vit):
    attn = jnp.pad(attn_in, ((0, 8), (0, 32))).reshape(48, 4, 128).transpose(1, 0, 2)
    back = attn_out.T
    out0 = jnp.pad(back[:, :80], ((0, 8), (32, 16)))
    out1 = jnp.pad(back[:, 80:], ((0, 8), (16, 32)))
    mlp = widen(jnp.concatenate([mlp_in.T, mlp_out]))
    bias = jnp.pad(mlp_bias[:, None], ((0, 20), (40, WIDE - 41)))
    mlp = jnp.pad(mlp + bias, ((0, 8), (0, 0))).reshape(48, 12, 128).transpose(1, 0, 2)
    s_pack = jnp.concatenate([attn, out0[None], out1[None], mlp]).reshape(2, 9, 48, 128)
    first = jnp.pad(proj, ((0, 0), (0, 64))).reshape(6, 16, 128)
    conv_t = conv.reshape(144, 16).T
    second = jnp.stack(
        [
            conv_t[:, :128],
            head[:, :128],
            jnp.pad(jnp.concatenate([conv_t[:, 128:], head[:, 128:]], axis=1), ((0, 0), (0, 48))),
        ]
    )
    third = jnp.pad(patch.reshape(3, 14, 14, 40).transpose(2, 0, 1, 3), ((0, 1), (0, 0), (0, 0), (0, 0)))
    third = jnp.pad(third.reshape(5, 126, 40), ((0, 0), (0, 2), (0, 8)))
    third = third.transpose(0, 2, 1).reshape(15, 16, 128)
    fourth = jnp.pad(vit, ((0, 8), (0, 0))).reshape(48, 8, 128).transpose(1, 0, 2).reshape(24, 16, 128)
    r_pack = jnp.concatenate([first, second, third, fourth]).reshape(3, 16, 16, 128)
    return s_pack, r_pack


def run_step(packs, fetch, grad_shape, small, consts):
    vm, dma = pltpu.VMEM, pltpu.SemaphoreType.DMA
    scratch = [
        vm((512, 3072), BF16), vm((512, 3072), BF16),
        vm((2, NZ, 2, 9, 48, 128), BF16), vm((3, 16, NF, 16, 128), BF16),
        vm((3072, 128), BF16), vm((48, 2304), BF16), vm((2, 48, 128), BF16), vm((2, 48, 128), BF16),
        vm((512, LANES), F32), vm((512, LANES), F32), vm((2, 512, 128), F32),
        vm((2, 8, 512), F32), vm((2, NS, 8, 512), F32),
        vm((256, LANES), BF16), vm((512, 1024), BF16), vm((256, 512), BF16), vm((512, 256), BF16),
        vm((2, 2, 80, 128), F32), vm((2, 2, 80, 128), F32),
        vm((2, WIDE), F32), vm((NS, 2, WIDE), F32), vm((32, WIDE), F32),
        vm((NS, 4, WIDE), F32), vm((NS, 4, WIDE), F32),
        vm((3, 1, WIDE), F32), vm((3, NS, 1, WIDE), F32),
        vm((4, WIDE), F32), vm((NS, 4, WIDE), F32),
        vm((2, 16, 128), F32), vm((2, 16, 128), F32),
        vm((16, 16, 768), F32), vm((16, 16, 768), BF16), vm((16, 16, 768), BF16),
        vm((NF, 4, 128), F32), vm((NF, 4, 128), F32), vm((16, 4, 128), F32),
        dma((12, NS - 1)), dma((12, NS - 1)), dma((1,)),
        dma((3,)), dma((3,)), dma((3, NS - 1)), dma((3, NS - 1)), dma((3,)), dma((3,)),
        dma((4,)), dma((2,)), dma((16,)), dma((16,)), dma((2,)),
        dma((15,)), dma((15,)), dma((31,)), dma((31,)), dma((15,)), dma((15,)),
    ]
    hidden, mods, noisy, sigma, proj_bias, vecs, text, chan, head_bias = small
    return pl.pallas_call(
        functools.partial(step_kernel, fetch),
        out_shape=[jax.ShapeDtypeStruct(grad_shape, F32), jax.ShapeDtypeStruct((8, 128), F32)],
        in_specs=[ANY] + ([ANY] * 2 if fetch else [VMEM] * 2) + [VMEM] * 2 + [SMEM] + [VMEM] * 15,
        out_specs=[VMEM, VMEM],
        scratch_shapes=scratch,
        compiler_params=pltpu.CompilerParams(
            collective_id=0, has_side_effects=True, vmem_limit_bytes=60 * 1024 * 1024
        ),
        name="step",
    )(hidden, *packs, mods, noisy, sigma, proj_bias, vecs, text, chan, head_bias, *consts)


def flow_sigma(step_index):
    remain = 1.0 - step_index.astype(F32) / STEPS
    return 3.0 * remain / (1.0 + 2.0 * remain)


def prepare(
    hidden, modulation, noisy, step_index, proj_bias, conv_bias, norm_gain, norm_shift, head_bias,
    position, class_token, vit_gain, vit_shift, attn_out_bias, mlp_out_bias, text_embed,
):
    stack = jnp.concatenate(
        [
            class_token[None], vit_gain, vit_shift, attn_out_bias[None], mlp_out_bias[None],
            jnp.zeros((5, WIDTH), F32), position.astype(F32),
        ]
    )
    chan = jnp.concatenate(
        [conv_bias[None], norm_gain[None], norm_shift[None], jnp.zeros((5, 512), F32)]
    )
    return (
        hidden.reshape(512, 3072), modulation[0], noisy.reshape(512, 64),
        flow_sigma(step_index).reshape(1, 1), proj_bias[None], widen(stack), text_embed, chan,
        jnp.broadcast_to(
            jnp.pad(
                jnp.concatenate([head_bias[:128], jnp.zeros((16,), F32), head_bias[128:]]), (0, 48)
            ),
            (8, 256),
        ),
    )


def local(
    hidden, modulation, noisy, step_index, proj_weight, proj_bias, conv_weight, conv_bias,
    norm_gain, norm_shift, head_weight, head_bias, patch_weight, position, class_token,
    vit_gain, vit_shift, attn_in, attn_out, attn_out_bias, mlp_in, mlp_in_bias, mlp_out,
    mlp_out_bias, vit_proj, text_embed,
):
    packs = pack_weights(
        proj_weight, conv_weight, head_weight, patch_weight, attn_in, attn_out, mlp_in,
        mlp_in_bias, mlp_out, vit_proj,
    )
    small = prepare(
        hidden, modulation, noisy, step_index, proj_bias, conv_bias, norm_gain, norm_shift,
        head_bias, position, class_token, vit_gain, vit_shift, attn_out_bias, mlp_out_bias,
        text_embed,
    )
    grad, score = run_step(packs, True, (96, 64), small, constants())
    return grad, score[0, 0:1]


def solution(mesh):
    placed = (
        P(("fsdp", "grp"), "slab", None, None),
        P(("fsdp", "grp"), None, None),
        P(("fsdp", "grp"), "slab", None, None),
        P(("fsdp", "grp")),
        P("fsdp", None),
        P(),
        P(None, None, None, "fsdp"),
        P(),
        P(),
        P(),
        P("fsdp", None),
        P(),
        P(None, "fsdp"),
        P("slab", None),
        P(),
        P(),
        P(),
        P("fsdp", "slab"),
        P("slab", "fsdp"),
        P(),
        P(None, ("fsdp", "slab")),
        P(("fsdp", "slab")),
        P(("fsdp", "slab"), None),
        P(),
        P("fsdp", None),
        P(("fsdp", "grp"), None),
    )
    return jax.shard_map(
        local,
        mesh=mesh,
        in_specs=placed,
        out_specs=(P("fsdp", None), P(("fsdp", "grp"))),
        check_vma=False,
    )
```

```python
import functools

import jax
import jax.numpy as jnp
import numpy as np
from jax import lax
from jax.experimental import pallas as pl
from jax.experimental.pallas import tpu as pltpu
from jax.sharding import PartitionSpec as P

HEAD_DIM = 80
STEPS = 28
LAT_SCALE = 0.3611
LAT_SHIFT = 0.1159
PIX_MEAN = (0.48145466, 0.4578275, 0.40821073)
PIX_STD = (0.26862954, 0.26130258, 0.27577711)
HIGH = lax.Precision.HIGHEST
MESH = pl.DeviceIdType.MESH
F32 = jnp.float32
BF16 = jnp.bfloat16
ANY = pl.BlockSpec(memory_space=pl.ANY)
VMEM = pl.BlockSpec(memory_space=pltpu.VMEM)
SMEM = pl.BlockSpec(memory_space=pltpu.SMEM)
ROOT = HEAD_DIM**0.5
WIDTH = 1280
WIDE = 1536
CELLS = 128 * 128 * 16
NF, NS, NZ = 32, 8, 16
LANES = 2048


def nn(a, b, precision=None):
    return lax.dot_general(
        a, b, (((1,), (0,)), ((), ())), precision=precision, preferred_element_type=F32
    )


def nt(a, b, precision=None):
    return lax.dot_general(
        a, b, (((1,), (1,)), ((), ())), precision=precision, preferred_element_type=F32
    )


def halves(values):
    high = values.astype(BF16)
    return high, (values - high.astype(F32)).astype(BF16)


def thirds(values):
    high, rest = halves(values)
    middle = (values - high.astype(F32) - rest.astype(F32)).astype(BF16)
    return [high, rest, middle]


def remote(source, dest, send, recv, target):
    return pltpu.make_async_remote_copy(
        src_ref=source, dst_ref=dest, send_sem=send, recv_sem=recv,
        device_id=target, device_id_type=MESH,
    )


def iota(shape, dim):
    return lax.broadcasted_iota(jnp.int32, shape, dim)


def norm_stats(values, mask, epsilon):
    average = jnp.sum(values, axis=-1, keepdims=True) * (1.0 / WIDTH)
    centered = (values - average) * mask
    square = jnp.sum(centered * centered, axis=-1, keepdims=True) * (1.0 / WIDTH)
    inverse = 1.0 / jnp.sqrt(square + epsilon)
    return centered * inverse, inverse


def norm_back(grads, scaled, inverse, gain):
    grads = grads * gain
    first = jnp.sum(grads, axis=-1, keepdims=True) * (1.0 / WIDTH)
    second = jnp.sum(grads * scaled, axis=-1, keepdims=True) * (1.0 / WIDTH)
    return (grads - first - scaled * second) * inverse


class Weights:
    def __init__(self, a_in, b_in, r_in, a_buf, b_buf, r_buf, sems):
        self.ins, self.r_in = (a_in, b_in), r_in
        self.a_buf, self.b_buf, self.r_buf = a_buf, b_buf, r_buf
        (self.z_send, self.z_recv, self.sh_send, self.sh_recv, self.fw_send, self.fw_recv,
         self.loc, self.pair_sem, self.ring_send, self.ring_recv, self.core_sem) = sems
        self.f = lax.axis_index("fsdp")
        self.g = lax.axis_index("grp")
        self.s = lax.axis_index("slab")
        self.w = self.g * NS + self.s
        self.z, self.half = self.f // 2, lax.rem(self.f, 2)
        self.core = {"grp": 1 - self.g}

    def r_own(self, slot):
        return pltpu.make_async_copy(
            self.r_in.at[slot, self.w], self.r_buf.at[slot, self.w, self.f], self.loc.at[slot]
        )

    def r_start(self, slot):
        self.r_own(slot).start()

        def send(d, carry):
            target = {"fsdp": lax.rem(self.f + d, NF)}
            remote(
                self.r_in.at[slot, self.w], self.r_buf.at[slot, self.w, self.f],
                self.z_send.at[slot], self.z_recv.at[slot], target,
            ).start()
            return carry

        lax.fori_loop(1, NF, send, 0)

    def r_share(self, slot):
        block = self.r_buf.at[slot, self.w]
        if slot < 2:
            many = self.r_buf.at[slot, self.w, pl.ds(0, NF - 1)]
            remote(many, many, self.z_send.at[slot], self.z_recv.at[slot], self.core).wait_recv()
            self.r_own(slot).wait()
        for d in range(1, NS):
            remote(
                block, block, self.sh_send.at[slot, d - 1], self.sh_recv.at[slot, d - 1],
                {"slab": lax.rem(self.s + d, NS)},
            ).start()

    def r_core(self, slot):
        for d in range(1, NS):
            block = self.r_buf.at[slot, self.g * NS + lax.rem(self.s + NS - d, NS)]
            remote(
                block, block, self.sh_send.at[slot, d - 1], self.sh_recv.at[slot, d - 1], self.core
            ).wait_recv()
        many = self.r_buf.at[slot, pl.ds(self.g * NS, NS)]
        remote(many, many, self.fw_send.at[slot], self.fw_recv.at[slot], self.core).start()

    def r_done(self, slot):
        many = self.r_buf.at[slot, pl.ds((1 - self.g) * NS, NS)]
        remote(many, many, self.fw_send.at[slot], self.fw_recv.at[slot], self.core).wait_recv()

    def view(self, kind, z):
        z = lax.rem(z, NZ)
        if kind == 0:
            return self.a_buf.at[self.g, z]
        if kind == 1:
            return self.r_buf.at[2, self.w, pl.ds(2 * z, 2)]
        return self.b_buf.at[self.g, z]

    def own(self):
        return [
            pltpu.make_async_copy(
                self.ins[0].at[self.g], self.a_buf.at[self.g, self.z, self.half], self.loc.at[3]
            ),
            self.r_own(2),
            pltpu.make_async_copy(self.ins[1].at[self.g], self.b_buf.at[self.g, self.z], self.loc.at[4]),
        ]

    def pair(self):
        other = {"fsdp": self.z * 2 + 1 - self.half}
        return [
            remote(
                self.ins[0].at[self.g], self.a_buf.at[self.g, self.z, self.half],
                self.pair_sem.at[0, 0], self.pair_sem.at[0, 1], other,
            ),
            remote(
                self.r_in.at[2, self.w], self.r_buf.at[2, self.w, self.f],
                self.pair_sem.at[1, 0], self.pair_sem.at[1, 1], other,
            ),
        ]

    def start(self):
        for copy in self.pair() + self.own():
            copy.start()

    def step(self, kind, step, way):
        sign = NZ - 1 if way == 0 else 1
        block = self.view(kind, self.z + sign * step)
        hop = 1 if way == 0 else NZ - 1
        target = {"fsdp": lax.rem(self.z + hop, NZ) * 2 + self.half}
        slot = way * 8 + step
        return remote(
            block, block, self.ring_send.at[kind, slot], self.ring_recv.at[kind, slot], target
        )

    def share(self, kind, z):
        if kind == 1:
            return
        block, k = self.view(kind, z), kind // 2
        remote(block, block, self.core_sem.at[k, 0], self.core_sem.at[k, 1], self.core).start()

    def pump(self, kinds, step):
        steps = (NZ // 2, NZ // 2 - 1)
        for kind in kinds:
            if step == 0:
                self.own()[kind].wait()
                if kind < 2:
                    self.pair()[kind].wait_recv()
            for way in (0, 1):
                if 0 < step <= steps[way]:
                    self.step(kind, step - 1, way).wait_recv()
                if step < steps[way]:
                    self.step(kind, step, way).start()
            if step == 0:
                self.share(kind, self.z)
            for way in (0, 1):
                if 0 < step <= steps[way]:
                    self.share(kind, self.z + (NZ - step if way == 0 else step))

    def landed(self, kind):
        buffer, k = (self.a_buf, self.b_buf)[kind // 2], kind // 2
        theirs = buffer.at[1 - self.g]
        remote(theirs, theirs, self.core_sem.at[k, 0], self.core_sem.at[k, 1], self.core).wait_recv()

    def finish(self):
        for k, buffer in enumerate((self.a_buf, self.b_buf)):
            mine = buffer.at[self.g]
            remote(mine, mine, self.core_sem.at[k, 0], self.core_sem.at[k, 1], self.core).wait_send()
        for copy in self.pair():
            copy.wait_send()
        for kind in range(3):
            for way, steps in ((0, NZ // 2), (1, NZ // 2 - 1)):
                for step in range(steps):
                    self.step(kind, step, way).wait_send()
        for slot in range(3):
            if slot < 2:
                many = self.r_buf.at[slot, self.w, pl.ds(0, NF - 1)]
                remote(many, many, self.z_send.at[slot], self.z_recv.at[slot], self.core).wait_send()
            block = self.r_buf.at[slot, self.w]
            for d in range(1, NS):
                remote(
                    block, block, self.sh_send.at[slot, d - 1], self.sh_recv.at[slot, d - 1], self.core
                ).wait_send()
            many = self.r_buf.at[slot, pl.ds(self.g * NS, NS)]
            remote(many, many, self.fw_send.at[slot], self.fw_recv.at[slot], self.core).wait_send()


def greet(targets):
    barrier = pltpu.get_barrier_semaphore()
    for target in targets:
        pl.semaphore_signal(barrier, inc=1, device_id=target, device_id_type=MESH)
    pl.semaphore_wait(barrier, len(targets))


def block_targets(g, s):
    found = []
    for d in range(1, 2 * NS):
        other_g = lax.rem(g + d // NS, 2)
        other_s = lax.rem(s + d % NS, NS)
        found.append((other_g * NS + other_s, {"grp": other_g, "slab": other_s}))
    return found


def pair_targets(f, s):
    z, half = f // 2, lax.rem(f, 2)
    found = []
    for h in range(2):
        there = z * 2 + lax.rem(half + h, 2)
        for d in range(NS):
            if h or d:
                found.append((h * NS + d - 1, {"fsdp": there, "slab": lax.rem(s + d, NS)}))
    return found


def greet_all():
    f, g, s = lax.axis_index("fsdp"), lax.axis_index("grp"), lax.axis_index("slab")
    greet(
        [target for _, target in block_targets(g, s)]
        + [{"fsdp": lax.rem(f + d, NF)} for d in range(1, NF)]
        + [target for _, target in pair_targets(f, s)[NS:]]
    )


def reduce_gradient(mine, landed, terms, arrived, collected, sems):
    a_send, a_recv, b_send, b_recv, c_send, c_recv = sems
    f, g, s = lax.axis_index("fsdp"), lax.axis_index("grp"), lax.axis_index("slab")
    w = g * NS + s
    block = block_targets(g, s)
    copies = []
    for d, (index, target) in enumerate(block):
        copy = remote(mine.at[index], landed.at[w], a_send.at[d], a_recv.at[d], target)
        copy.start()
        copies.append(copy)
    landed[w] = mine[w]
    for copy in copies:
        copy.wait()
    total = landed[0].astype(F32)
    for index in range(1, 2 * NS):
        total = total + landed[index].astype(F32)
    for index in range(NF):
        rows, lanes = 4 * (index // 8), 96 * (index % 8)
        terms[index, :, 0:96] = total[rows : rows + 4, lanes : lanes + 96]
        terms[index, :, 96:128] = jnp.zeros((4, 32), F32)
    copies = []
    for d in range(1, NF):
        p = lax.rem(f + d, NF)
        copy = remote(terms.at[p], arrived.at[f], b_send.at[d - 1], b_recv.at[d - 1], {"fsdp": p})
        copy.start()
        copies.append(copy)
    arrived[f] = terms[f]
    for copy in copies:
        copy.wait()
    collected[w] = jnp.sum(arrived[...], axis=0)
    copies = []
    for d, (index, target) in enumerate(block):
        copy = remote(collected.at[w], collected.at[w], c_send.at[d], c_recv.at[d], target)
        copy.start()
        copies.append(copy)
    for copy in copies:
        copy.wait()


def step_kernel(
    fetch, hidden, a_in, b_in, r_in, mods, noisy, sigma_ref, proj_bias, vecs, text, chan, head_bias,
    perm, perm_t, inter, columns_w, rows_w, ph0, ph1, lane_rows,
    grad_out, score_out,
    hid, mod, a_buf, b_buf, r_buf, proj_full, ext, halo_out, halo_in, nrm, dnrm, acc, stat_out, stat_in,
    cols_buf, pix, head_t, head_p, edge_out, edge_in, kd_out, kd_in, dirs, u_out, u_in,
    row_out, row_in, text_in, vd_out, vd_in, rim_out, rim_in, gsplit, mine, landed, terms, arrived, collected,
    x_send, x_recv, hid_sem, *sems,
):
    s = lax.axis_index("slab")
    f = lax.axis_index("fsdp")
    half = lax.rem(f, 2)
    low, high = s > 0, s < NS - 1
    low_f, high_f = jnp.where(low, 1.0, 0.0), jnp.where(high, 1.0, 0.0)
    before, after = {"slab": lax.rem(s + NS - 1, NS)}, {"slab": lax.rem(s + 1, NS)}
    hid_copy = pltpu.make_async_copy(hidden, hid, hid_sem.at[0])
    hid_copy.start()
    sigma = sigma_ref[0, 0]
    live = []

    def to_all(kind, source, dest, swap=False):
        copies = []
        for d in range(1, NS):
            p = lax.rem(s + d, NS)
            copies.append(
                remote(
                    source.at[p] if swap else source, dest.at[s],
                    x_send.at[kind, d - 1], x_recv.at[kind, d - 1], {"slab": p},
                )
            )
        for copy in copies:
            copy.start()
        live.extend(copies)
        return copies

    def to_sides(kind, source, dest):
        copies = [
            remote(source.at[0], dest.at[0], x_send.at[kind, 0], x_recv.at[kind, 0], after),
            remote(source.at[1], dest.at[1], x_send.at[kind, 1], x_recv.at[kind, 1], before),
        ]
        for copy in copies:
            copy.start()
        live.extend(copies)
        return copies

    def landed_all(copies):
        for copy in copies:
            copy.wait_recv()

    if fetch:
        greet_all()
        weights = Weights(a_in, b_in, r_in, a_buf, b_buf, r_buf, sems[:11])
        weights.r_start(0)
        weights.start()
        weights.r_start(1)
    else:
        greet([target for _, target in pair_targets(f, s)])
        a_buf[...] = a_in[...]
        b_buf[...] = b_in[0]
        r_buf[...] = r_in[...]
        weights = None
    words_copy = remote(
        text, text_in.at[half], x_send.at[12, 0], x_recv.at[12, 0], {"fsdp": f + 1 - 2 * half}
    )
    words_copy.start()
    live.append(words_copy)
    text_in[half] = text[...]

    def pump(*steps):
        if weights is not None:
            for kinds, step in zip(((0, 1), (2,)), steps):
                if step is not None:
                    weights.pump(kinds, step)

    hid_copy.wait()
    scale = 1.0 + mods[1:2].astype(F32)
    shift = mods[0:1].astype(F32)

    def modulate(lo, hi):
        def body(i, carry):
            rows = pl.ds(pl.multiple_of(i * 32, 32), 32)
            values = hid[rows, :].astype(F32)
            average = jnp.mean(values, axis=-1, keepdims=True)
            centered = values - average
            square = jnp.mean(centered * centered, axis=-1, keepdims=True)
            scaled = centered * (1.0 / jnp.sqrt(square + 1e-06))
            mod[rows, :] = (scaled * scale + shift).astype(BF16)
            return carry

        lax.fori_loop(lo, hi, body, 0)

    modulate(0, 6)
    pump(0, 0)
    modulate(6, 16)
    pump(1)
    if weights is not None:
        weights.r_share(0)
        pump(2, 1)
        weights.r_core(0)
        pump(3)
        weights.r_done(0)

    def blocks(first, count):
        parts = [r_buf[n // 16, n % 16] for n in range(first, first + count)]
        return jnp.concatenate(parts, axis=1).reshape(NF * 16 * count, 128)

    def a_unit(index):
        return a_buf[index // 3, :, :, index % 3].reshape(WIDE, 128)

    for k in range(NF):
        for n in range(6):
            proj_full[96 * k + 16 * n : 96 * k + 16 * n + 16, :] = r_buf[0, n, k]
    velocity = nn(mod[...], proj_full[...])[:, :64] + proj_bias[...]
    clean = noisy[...].astype(F32) - sigma * velocity
    lat_tok = (clean / LAT_SCALE + LAT_SHIFT).astype(BF16)
    tok_t = nt(perm_t[...], lat_tok)
    stacked = jnp.concatenate(
        [
            jnp.concatenate(
                [tok_t[0:32, 128 * k : 128 * k + 128], tok_t[32:64, 128 * k : 128 * k + 128]], axis=1
            )
            for k in range(4)
        ],
        axis=0,
    ).astype(BF16)
    latent = nn(stacked, inter[...]).astype(BF16)
    for k in range(4):
        for i2 in range(2):
            for p in range(2):
                r = 4 * k + 2 * i2 + p + 1
                for b in range(3):
                    at = (i2 * 3 + b) * 128
                    ext[16 * b : 16 * b + 16, 128 * r : 128 * r + 128] = latent[
                        32 * k + 16 * p : 32 * k + 16 * p + 16, at : at + 128
                    ]
    halo_out[0] = ext[:, 2048:2176]
    halo_out[1] = ext[:, 128:256]
    copies = to_sides(0, halo_out, halo_in)
    same = (iota((512, 512), 0) // 16 == iota((512, 512), 1) // 16).astype(BF16)

    def columns_of(rows):
        width = rows.shape[1]
        return jnp.transpose(jnp.concatenate([rows, jnp.zeros((120, width), F32)], axis=0))

    chan_cols = columns_of(chan[...])
    conv_bias, gain, gshift = chan_cols[:, 0:1], chan_cols[:, 1:2], chan_cols[:, 2:3]
    eye = (iota((128, 128), 0) == iota((128, 128), 1)).astype(BF16)
    conv0 = r_buf[0, 6].reshape(512, 128)
    head0 = r_buf[0, 7].reshape(512, 128)
    tail = r_buf[0, 8].reshape(512, 128)
    head_p[...] = (nn(head0, ph0[...]) + nn(tail, ph1[...])).astype(BF16)
    head_t[...] = (
        lax.dot_general(ph0[...], head0, (((0,), (1,)), ((), ())), preferred_element_type=F32)
        + lax.dot_general(ph1[...], tail, (((0,), (1,)), ((), ())), preferred_element_type=F32)
    ).astype(BF16)
    bias_row = nn(head_bias[:, 0:128], ph0[...].astype(F32), HIGH) + nn(
        head_bias[:, 128:256], ph1[...].astype(F32), HIGH
    )
    head_col = columns_of(bias_row)[:, 0:1]
    pump(4, 2)
    landed_all(copies)
    ext[:, 0:128] = (halo_in[0].astype(F32) * low_f).astype(BF16)
    ext[:, 2176:2304] = (halo_in[1].astype(F32) * high_f).astype(BF16)
    acc[...] = jnp.zeros_like(acc)

    def conv_chunk(i, carry):
        at = pl.multiple_of(i * 256, 256)
        parts = [ext[:, pl.ds(pl.multiple_of(at + 128 * a, 128), 256)] for a in range(3)]
        columns = jnp.concatenate(parts + [jnp.zeros((112, 256), BF16)], axis=0)
        out = nn(conv0, columns[0:128]) + nn(tail, columns[128:256]) + conv_bias
        nrm[:, pl.ds(at, 256)] = out
        acc[0] += out[:, 0:128] + out[:, 128:256]
        square = out * out
        acc[1] += square[:, 0:128] + square[:, 128:256]
        return carry

    lax.fori_loop(0, 8, conv_chunk, 0)

    def group_totals(kind, step=None):
        ones = jnp.ones((8, 128), BF16)
        first, second = [
            nt(ones, part[0]) + (nt(ones, part[1]) + nt(ones, part[2]))
            for part in (thirds(acc[0]), thirds(acc[1]))
        ]
        k = kind - 1
        stat_out[k] = jnp.where(iota((8, 512), 0) == 0, first, second)
        copies = to_all(kind, stat_out.at[k], stat_in.at[k])
        stat_in[k, s] = stat_out[k]
        if step is not None:
            pump(*step)
        landed_all(copies)
        total = stat_in[k, 0]
        for index in range(1, NS):
            total = total + stat_in[k, index]
        sums = nn(jnp.concatenate(thirds(total), axis=0), same)
        columns = columns_of(sums[0:8] + (sums[8:16] + sums[16:24]))
        return columns[:, 0:1] * (1.0 / CELLS), columns[:, 1:2] * (1.0 / CELLS)

    average, square = group_totals(1, (5, 3))
    inverse = 1.0 / jnp.sqrt(square - average * average + 1e-06)
    if weights is not None:
        weights.r_share(1)

    def head_chunk(i, carry):
        at = pl.multiple_of(i * 256, 256)
        normed = (nrm[:, pl.ds(at, 256)] - average) * inverse
        nrm[:, pl.ds(at, 256)] = normed
        gained = normed * gain + gshift
        active = (gained * (1.0 / (1.0 + jnp.exp(-gained)))).astype(BF16)
        cells = (nn(head_t[...], active) + head_col).astype(BF16)
        for rr in range(2):
            rows = pl.ds(pl.multiple_of(i * 64 + 32 * rr, 32), 32)
            for x in range(8):
                pix[rows, 128 * x : 128 * x + 128] = cells[
                    32 * x : 32 * x + 32, 128 * rr : 128 * rr + 128
                ]
        return carry

    lax.fori_loop(0, 8, head_chunk, 0)
    pump(6, 4)
    narrow = nt(columns_w[...], pix[...]).astype(BF16)
    raw = jnp.zeros((80, 512), F32)
    for m in range(3):
        raw = raw + nn(narrow[128 * m : 128 * m + 80], rows_w[512 * m : 512 * m + 512, :])
    edge_out[0, 0] = raw[:, 256:384]
    edge_out[0, 1] = raw[:, 384:512]
    copies = to_sides(2 + 1, edge_out.at[0], edge_in.at[0])
    pump(7, 5)
    if weights is not None:
        weights.r_core(1)
    corr0 = jnp.where(low, 1.0, lane_rows[0:1, :])
    corr1 = jnp.where(high, 1.0, lane_rows[1:2, :])
    img_scale, img_shift = lane_rows[2:3, :], lane_rows[3:4, :]
    if weights is not None:
        weights.r_done(1)
    landed_all(copies)
    top = (raw[:, 0:128] * corr0 + edge_in[0, 0] * low_f) * img_scale + img_shift
    bottom = (raw[:, 128:256] * corr1 + edge_in[0, 1] * high_f) * img_scale + img_shift
    patches = jnp.concatenate(
        [
            jnp.concatenate([part[16 * u : 16 * u + 16] for u in range(5)], axis=1)
            for part in (top, bottom)
        ],
        axis=0,
    ).astype(BF16)
    embedded = vecs[16:48, :]
    for u in range(5):
        embedded = embedded + nt(patches[:, 128 * u : 128 * u + 128], blocks(9 + 3 * u, 3))
    lane = iota((1, WIDE), 1)
    inner = lax.rem(lane, 48)
    mask = (inner < 40).astype(F32)
    gains = [vecs[1 + i : 2 + i, :] for i in range(4)]
    shifts = [vecs[5 + i : 6 + i, :] for i in range(4)]
    pump(8, 6)
    if weights is not None:
        weights.r_share(2)
        weights.landed(0)

    class_hat, _ = norm_stats(vecs[0:1, :], mask, 1e-05)
    class_pre = class_hat * gains[0] + shifts[0]
    class_hat, _ = norm_stats(class_pre, mask, 1e-05)
    class_unit = jnp.broadcast_to(class_hat * gains[1] + shifts[1], (8, WIDE)).astype(BF16)
    attn = [a_unit(i) for i in range(4)]
    class_qkv = jnp.concatenate([nn(class_unit, attn[i]) for i in range(4)], axis=1)
    class_qkv = class_qkv.astype(BF16).astype(F32)
    place512 = iota((8, 512), 1)
    row512 = iota((8, 512), 0)
    start = jnp.where(row512 == 0, 0, 240)
    in_head = row512 < 2
    key_at = in_head & (place512 >= start + 80) & (place512 < start + 160)
    val_at = in_head & (place512 >= start + 160) & (place512 < start + 240)
    query = jnp.where(key_at, pltpu.roll(class_qkv, 80, 1), 0.0)
    class_exp = jnp.exp(jnp.sum(query * class_qkv, axis=-1, keepdims=True) / ROOT)
    query_b = query.astype(BF16)
    key_dir = nt(query_b[:, 0:128], attn[0])
    for i in range(1, 4):
        key_dir = key_dir + nt(query_b[:, 128 * i : 128 * i + 128], attn[i])
    kd_out[...] = key_dir[0:2]
    copies = to_all(4, kd_out, kd_in)
    kd_in[s] = key_dir[0:2]
    hat0, inv0 = norm_stats(embedded, mask, 1e-05)
    hat1, inv1 = norm_stats(hat0 * gains[0] + shifts[0], mask, 1e-05)
    unit = hat1 * gains[1] + shifts[1]
    unit_b = unit.astype(BF16)
    unit = unit_b.astype(F32)
    pump(None, 7)
    landed_all(copies)
    for index in range(NS):
        dirs[2 * index : 2 * index + 2, :] = kd_in[index]
    token_exp = jnp.exp(nt(dirs[0:16, :], unit, HIGH) / ROOT)
    gathered = nn(token_exp, unit, HIGH)
    sums = jnp.broadcast_to(jnp.sum(token_exp, axis=1, keepdims=True), (16, WIDE))
    for index in range(NS):
        u_out[index, 0:2] = gathered[2 * index : 2 * index + 2]
        u_out[index, 2:4] = sums[2 * index : 2 * index + 2]
    copies = to_all(5, u_out, u_in, swap=True)
    u_in[s] = u_out[s]
    pump(None, 8)
    if weights is not None:
        weights.r_core(2)
    landed_all(copies)
    total = u_in[0]
    for index in range(1, NS):
        total = total + u_in[index]
    denominator = class_exp[0:2] + total[2:4, 0:1]
    mixed = halves(jnp.concatenate([total[0:2], jnp.zeros((6, WIDE), F32)], axis=0))
    first = nn(mixed[0], attn[1]) + nn(mixed[1], attn[1])
    second = nn(mixed[0], attn[3]) + nn(mixed[1], attn[3])
    heads1 = jnp.where(val_at[0:1, 128:256], first[0:1] + class_exp[0:1] * class_qkv[0:1, 128:256], 0.0)
    heads3 = jnp.where(val_at[1:2, 384:512], second[1:2] + class_exp[1:2] * class_qkv[0:1, 384:512], 0.0)
    heads1 = heads1 / denominator[0:1]
    heads3 = heads3 / denominator[1:2]
    rows1 = a_unit(4)
    rows3 = a_unit(5)

    def wide8(row):
        if row.shape[0] == 1:
            return jnp.broadcast_to(row, (8, row.shape[1])).astype(BF16)
        return jnp.concatenate([row, jnp.zeros((6, row.shape[1]), F32)], axis=0).astype(BF16)

    def mine_of(rows):
        return jnp.where(half == 0, rows[0:1], rows[1:2])

    attn_part = nt(wide8(heads1), rows1) + nt(wide8(heads3), rows3)

    def pair_sum(kind, k, rows):
        row_out[k] = rows[0:2]
        copies = [
            remote(
                row_out.at[k], row_in.at[k, half, s], x_send.at[kind, index], x_recv.at[kind, index],
                target,
            )
            for index, target in pair_targets(f, s)
        ]
        for copy in copies:
            copy.start()
        live.extend(copies)
        row_in[k, half, s] = row_out[k]
        landed_all(copies)
        sums = []
        for h in range(2):
            total = row_in[k, h, 0]
            for index in range(1, NS):
                total = total + row_in[k, h, index]
            sums.append(total)
        return sums

    sums = pair_sum(6, 0, attn_part)
    block_mid = class_pre + jnp.concatenate([sums[0][0:1], sums[1][0:1]], axis=0) + vecs[9:10, :]
    hat2, inv2 = norm_stats(block_mid, mask, 1e-05)
    mlp_input = hat2 * gains[2] + shifts[2]
    mlp_input = wide8(jnp.where(lane == 40, 1.0, mlp_input))
    if weights is not None:
        weights.landed(2)
    hidden_units = [b_buf[i // 6, :, i % 6].reshape(WIDE // 2, 128) for i in range(12)]
    unit_at = lax.rem(iota((1, WIDE // 2), 1), 48) < 20
    preact = nt(mlp_input[:, 0:128], hidden_units[0])
    for i in range(1, 12):
        preact = preact + nt(mlp_input[:, 128 * i : 128 * i + 128], hidden_units[i])
    preact = jnp.where(unit_at, preact, 0.0)
    cdf = 0.5 * (1.0 + lax.erf(preact * 0.7071067811865476))
    active = preact * cdf
    active = pltpu.roll(active, 20, 1).astype(BF16)
    mlp_part = jnp.concatenate([nn(active, hidden_units[i]) for i in range(12)], axis=1)
    sums = pair_sum(7, 1, mlp_part)
    block_out = block_mid + (sums[0] + sums[1]) + vecs[10:11, :]
    hat3, inv3 = norm_stats(block_out, mask, 1e-05)
    post = wide8(hat3 * gains[3] + shifts[3])
    if weights is not None:
        weights.r_done(2)
    vit = [blocks(24 + 3 * u, 3) for u in range(8)]
    embed = jnp.concatenate([nn(post, vit[u]) for u in range(8)], axis=1)[0:2]
    words_copy.wait_recv()
    words = jnp.concatenate([text_in[0], text_in[1]], axis=0)
    dots = jnp.sum(embed * words, axis=-1, keepdims=True)
    size_e = jnp.sum(embed * embed, axis=-1, keepdims=True) + 1e-06
    size_t = jnp.sum(words * words, axis=-1, keepdims=True) + 1e-06
    sizes = jnp.sqrt(size_e) * jnp.sqrt(size_t)
    score = 100.0 * dots / sizes
    score_out[...] = jnp.broadcast_to(mine_of(score), (8, 128))
    d_embed = wide8((-1.0 / 64.0) * (100.0 * words / sizes - score * embed / size_e))
    d_post = nt(d_embed[:, 0:128], vit[0])
    for u in range(1, 8):
        d_post = d_post + nt(d_embed[:, 128 * u : 128 * u + 128], vit[u])
    d_second = norm_back(d_post[0:2], hat3, inv3, gains[3])
    d_second_b = wide8(d_second)
    d_active = nt(d_second_b[:, 0:128], hidden_units[0])
    for i in range(1, 12):
        d_active = d_active + nt(d_second_b[:, 128 * i : 128 * i + 128], hidden_units[i])
    d_active = pltpu.roll(d_active, WIDE // 2 - 20, 1)
    slope = cdf + preact * jnp.exp(-0.5 * preact * preact) * 0.3989422804014327
    d_pre = jnp.where(unit_at, d_active * slope, 0.0).astype(BF16)
    input_part = jnp.concatenate([nn(d_pre, hidden_units[i]) for i in range(12)], axis=1)
    sums = pair_sum(8, 2, input_part)
    d_first = d_second + norm_back(sums[0] + sums[1], hat2, inv2, gains[2])
    d_first = wide8(mine_of(d_first))
    d_heads1 = nn(d_first, rows1).astype(BF16)
    d_heads3 = nn(d_first, rows3).astype(BF16)
    value0 = nt(jnp.where(val_at[0:1, 128:256], d_heads1.astype(F32), 0.0).astype(BF16), attn[1])
    value1 = nt(jnp.where(val_at[1:2, 384:512], d_heads3.astype(F32), 0.0).astype(BF16), attn[3])
    expect0 = jnp.sum(d_heads1[0:1].astype(F32) * heads1, axis=-1, keepdims=True)
    expect1 = jnp.sum(d_heads3[0:1].astype(F32) * heads3, axis=-1, keepdims=True)
    vd_out[0:1, :] = value0[0:1]
    vd_out[1:2, :] = value1[0:1]
    vd_out[2:3, :] = jnp.where(lane < 128, denominator[0:1], denominator[1:2])
    vd_out[3:4, :] = jnp.where(lane < 128, expect0, expect1)
    copies = to_all(9, vd_out, vd_in)
    vd_in[s] = vd_out[...]
    token_logits = nt(unit, dirs[0:16, :], HIGH) / ROOT
    landed_all(copies)
    head_at = iota((1, 16), 1)
    denominators = jnp.zeros((1, 16), F32)
    expects = jnp.zeros((1, 16), F32)
    for index in range(NS):
        dirs[16 + 2 * index : 18 + 2 * index, :] = vd_in[index, 0:2]
        for h in range(2):
            here = head_at == 2 * index + h
            denominators = jnp.where(here, vd_in[index, 2:3, 128 * h : 128 * h + 1], denominators)
            expects = jnp.where(here, vd_in[index, 3:4, 128 * h : 128 * h + 1], expects)
    token_weight = jnp.exp(token_logits) / denominators
    token_dots = nt(unit, dirs[16:32, :], HIGH)
    logit_grads = token_weight * (token_dots - expects)
    d_unit = nn(logit_grads / ROOT, dirs[0:16, :], HIGH) + nn(
        token_weight.astype(BF16).astype(F32), dirs[16:32, :], HIGH
    )
    d_pre_x = norm_back(d_unit, hat1, inv1, gains[1])
    d_embedded = norm_back(d_pre_x, hat0, inv0, gains[0]).astype(BF16)
    d_parts = [nn(d_embedded, blocks(9 + 3 * u, 3)) for u in range(5)]
    d_top = jnp.concatenate([part[0:16] for part in d_parts], axis=0) * img_scale
    d_bottom = jnp.concatenate([part[16:32] for part in d_parts], axis=0) * img_scale
    edge_out[1, 0] = d_bottom
    edge_out[1, 1] = d_top
    copies = to_sides(10, edge_out.at[1], edge_in.at[1])
    landed_all(copies)
    d_raw = jnp.concatenate(
        [
            jnp.concatenate(
                [d_top * corr0, d_bottom * corr1, edge_in[1, 1] * high_f, edge_in[1, 0] * low_f],
                axis=1,
            ),
            jnp.zeros((48, 512), F32),
        ],
        axis=0,
    ).astype(BF16)
    d_narrow = jnp.concatenate(
        [nt(rows_w[512 * m : 512 * m + 512, :], d_raw) for m in range(3)], axis=1
    ).astype(BF16)
    for k in range(4):
        d_pix = nn(d_narrow, columns_w[:, 256 * k : 256 * k + 256]).astype(BF16)
        for x in range(2):
            rows = slice(64 * k + 32 * x, 64 * k + 32 * x + 32)
            for r in range(16):
                cols_buf[rows, 128 * r : 128 * r + 128] = d_pix[
                    32 * r : 32 * r + 32, 128 * x : 128 * x + 128
                ]
    acc[...] = jnp.zeros_like(acc)

    def head_back(i, carry):
        at = pl.multiple_of(i * 256, 256)
        grads = nn(head_p[...], cols_buf[:, pl.ds(at, 256)])
        normed = nrm[:, pl.ds(at, 256)]
        gained = normed * gain + gshift
        gate = 1.0 / (1.0 + jnp.exp(-gained))
        grads = grads * (gate * (1.0 + gained * (1.0 - gate))) * gain
        dnrm[:, pl.ds(at, 256)] = grads
        acc[0] += grads[:, 0:128] + grads[:, 128:256]
        both = grads * normed
        acc[1] += both[:, 0:128] + both[:, 128:256]
        return carry

    lax.fori_loop(0, 8, head_back, 0)
    conv0_t = nt(eye, conv0).astype(BF16)
    tail_t = nt(eye[0:16], tail).astype(BF16)
    mean0, mean1 = group_totals(2)

    def conv_back(i, carry):
        at = pl.multiple_of(i * 256, 256)
        grads = (dnrm[:, pl.ds(at, 256)] - mean0 - nrm[:, pl.ds(at, 256)] * mean1) * inverse
        grads = grads.astype(BF16)
        dnrm[0:128, pl.ds(at, 256)] = nn(conv0_t, grads)
        dnrm[128:144, pl.ds(at, 256)] = nn(tail_t, grads)
        return carry

    lax.fori_loop(0, 8, conv_back, 0)
    total = jnp.zeros((16, 2304), F32)
    column = lax.rem(iota((16, 2304), 1), 128)
    for b in range(3):
        part = jnp.zeros((16, 2304), F32)
        for a in range(3):
            t = 3 * a + b
            pieces = [dnrm[16 * t : 16 * t + 16, :]]
            if a:
                pieces = [jnp.zeros((16, 128 * a), F32)] + pieces
            if a < 2:
                pieces = pieces + [jnp.zeros((16, 256 - 128 * a), F32)]
            part = part + jnp.concatenate(pieces, axis=1)
        if b == 0:
            part = jnp.where(column < 127, pltpu.roll(part, 2303, 1), 0.0)
        if b == 2:
            part = jnp.where(column > 0, pltpu.roll(part, 1, 1), 0.0)
        total = total + part
    rim_out[0] = total[:, 2176:2304]
    rim_out[1] = total[:, 0:128]
    copies = to_sides(11, rim_out, rim_in)
    landed_all(copies)
    rows = [total[:, 128 * r + 128 : 128 * r + 256] for r in range(16)]
    rows[0] = rows[0] + rim_in[0] * low_f
    rows[15] = rows[15] + rim_in[1] * high_f
    rows = [-sigma * (row / LAT_SCALE) for row in rows]
    stacked = jnp.concatenate(
        [
            jnp.concatenate([rows[4 * k + p], rows[4 * k + 2 + p]], axis=1)
            for k in range(4)
            for p in range(2)
        ],
        axis=0,
    ).astype(BF16)
    centre = jnp.concatenate([inter[:, 128:256], inter[:, 512:640]], axis=1)
    tok = nt(stacked, centre)
    tok_t = jnp.concatenate(
        [
            jnp.concatenate(
                [tok[32 * k : 32 * k + 32, 128 * q : 128 * q + 128] for k in range(4)], axis=1
            )
            for q in range(2)
        ],
        axis=0,
    ).astype(BF16)
    d_vel = nn(perm[...], tok_t).astype(BF16)
    for quarter in range(4):
        part = nn(d_vel, mod[:, 768 * quarter : 768 * quarter + 768])
        for w in range(2 * NS):
            gsplit[w, 4 * quarter : 4 * quarter + 4] = part[4 * w : 4 * w + 4]
    for copy in live:
        copy.wait_send()
    if weights is not None:
        weights.finish()
        mine[...] = gsplit[...].astype(BF16)
        reduce_gradient(mine, landed, terms, arrived, collected, sems[11:])
        whole = jnp.concatenate([collected[w] for w in range(2 * NS)], axis=0)
        grad_out[...] = jnp.transpose(whole)[0:96, :]
    else:
        grad_out[...] = gsplit[...]


def resize_table(out_count, in_count):
    stretch = in_count / out_count
    centers = (np.arange(out_count) + 0.5) * stretch
    places = np.arange(in_count) + 0.5
    weights = np.maximum(0.0, 1.0 - np.abs(places[None, :] - centers[:, None]) / stretch)
    return weights / weights.sum(axis=1, keepdims=True)


def constants():
    perm = np.zeros((64, 64))
    for c in range(16):
        for p in range(2):
            for q in range(2):
                perm[4 * c + 2 * p + q, q * 32 + p * 16 + c] = 1
    inter = np.zeros((2, 2, 64, 2, 3, 128))
    for q in range(2):
        for i2 in range(2):
            for j in range(64):
                for b in range(3):
                    at = 2 * j + q - b + 1
                    if 0 <= at < 128:
                        inter[q, i2, j, i2, b, at] = 1
    table = resize_table(224, 1024)
    columns = np.zeros((3, 8, 16, 8, 128))
    for m in range(3):
        for u in range(5):
            if 3 * u + m < 14:
                for pc in range(16):
                    columns[m, u, pc] = table[14 * pc + 3 * u + m].reshape(128, 8).T
    rows = np.zeros((3, 16, 4, 8, 4, 128))
    local = table[28 * 3 : 28 * 3 + 28, 128 * 3 : 128 * 3 + 128].reshape(28, 16, 8)
    to_next = table[28 * 4, 128 * 3 : 128 * 3 + 128].reshape(16, 8)
    to_prev = table[28 * 3 - 1, 128 * 3 : 128 * 3 + 128].reshape(16, 8)
    for m in range(3):
        for c in range(3):
            for a in range(14):
                at = 42 * m + 14 * c + a
                rows[m, :, c, :, 0, at] = local[a]
                rows[m, :, c, :, 1, at] = local[14 + a]
            rows[m, :, c, :, 2, 42 * m + 14 * c] = to_next
            rows[m, :, c, :, 3, 42 * m + 14 * c + 13] = to_prev
    lanes = np.zeros((8, 128))
    lanes[0:2] = 1
    for m in range(3):
        for c in range(3):
            for a in range(14):
                at = 42 * m + 14 * c + a
                lanes[2, at] = 0.5 / PIX_STD[c]
                lanes[3, at] = (0.5 - PIX_MEAN[c]) / PIX_STD[c]
            lanes[0, 42 * m + 14 * c] = table[0, 0] / table[28, 128]
            lanes[1, 42 * m + 14 * c + 13] = table[223, 1023] / table[27, 127]
    ph = np.zeros((2, 128, 8, 32))
    for c in range(3):
        for y in range(8):
            for x in range(8):
                k = 64 * c + 8 * y + x
                if k < 128:
                    ph[0, k, x, 8 * c + y] = 1
                else:
                    ph[1, 16 + k - 128, x, 8 * c + y] = 1
    one = lambda v: jnp.asarray(v.astype(jnp.bfloat16))
    ph = ph.reshape(2, 128, 256)
    return (
        one(perm), one(perm.T), one(inter.reshape(256, 768)),
        one(columns.reshape(384, 1024)), one(rows.reshape(1536, 512)),
        one(ph[0]), one(ph[1]), jnp.asarray(lanes.astype(np.float32)),
    )


def widen(values):
    shape = values.shape[:-1]
    view = values.reshape(shape + (32, 40))
    return jnp.pad(view, [(0, 0)] * len(shape) + [(0, 0), (0, 8)]).reshape(shape + (WIDE,))


def pack_weights(proj, conv, head, patch, attn_in, attn_out, mlp_in, mlp_bias, mlp_out, vit):
    attn = jnp.pad(attn_in, ((0, 8), (0, 32))).reshape(48, 4, 128).transpose(1, 0, 2)
    back = attn_out.T
    out0 = jnp.pad(back[:, :80], ((0, 8), (32, 16)))
    out1 = jnp.pad(back[:, 80:], ((0, 8), (16, 32)))
    mlp = widen(jnp.concatenate([mlp_in.T, mlp_out]))
    bias = jnp.pad(mlp_bias[:, None], ((0, 20), (40, WIDE - 41)))
    mlp = jnp.pad(mlp + bias, ((0, 8), (0, 0))).reshape(48, 12, 128).transpose(1, 0, 2)
    a_pack = jnp.concatenate([attn, out0[None], out1[None]]).reshape(2, 3, 48, 128)
    b_pack = mlp.reshape(2, 6, 48, 128)
    first = jnp.pad(proj, ((0, 0), (0, 64))).reshape(6, 16, 128)
    conv_t = conv.reshape(144, 16).T
    second = jnp.stack(
        [
            conv_t[:, :128],
            head[:, :128],
            jnp.pad(jnp.concatenate([conv_t[:, 128:], head[:, 128:]], axis=1), ((0, 0), (0, 48))),
        ]
    )
    third = jnp.pad(patch.reshape(3, 14, 14, 40).transpose(2, 0, 1, 3), ((0, 1), (0, 0), (0, 0), (0, 0)))
    third = jnp.pad(third.reshape(5, 126, 40), ((0, 0), (0, 2), (0, 8)))
    third = third.transpose(0, 2, 1).reshape(15, 16, 128)
    fourth = jnp.pad(vit, ((0, 8), (0, 0))).reshape(48, 8, 128).transpose(1, 0, 2).reshape(24, 16, 128)
    r_pack = jnp.concatenate([first, second, third, fourth]).reshape(3, 16, 16, 128)
    return a_pack, b_pack, r_pack


def run_step(packs, fetch, grad_shape, small, consts):
    vm, dma = pltpu.VMEM, pltpu.SemaphoreType.DMA
    scratch = [
        vm((512, 3072), BF16), vm((512, 3072), BF16),
        vm((2, NZ, 2, 3, 48, 128), BF16), vm((2, NZ, 6, 48, 128), BF16), vm((3, 16, NF, 16, 128), BF16),
        vm((3072, 128), BF16), vm((48, 2304), BF16), vm((2, 48, 128), BF16), vm((2, 48, 128), BF16),
        vm((512, LANES), F32), vm((512, LANES), F32), vm((2, 512, 128), F32),
        vm((2, 8, 512), F32), vm((2, NS, 8, 512), F32),
        vm((256, LANES), BF16), vm((512, 1024), BF16), vm((256, 512), BF16), vm((512, 256), BF16),
        vm((2, 2, 80, 128), F32), vm((2, 2, 80, 128), F32),
        vm((2, WIDE), F32), vm((NS, 2, WIDE), F32), vm((32, WIDE), F32),
        vm((NS, 4, WIDE), F32), vm((NS, 4, WIDE), F32),
        vm((3, 2, WIDE), F32), vm((3, 2, NS, 2, WIDE), F32), vm((2, 1, 1024), F32),
        vm((4, WIDE), F32), vm((NS, 4, WIDE), F32),
        vm((2, 16, 128), F32), vm((2, 16, 128), F32),
        vm((16, 16, 768), F32), vm((16, 16, 768), BF16), vm((16, 16, 768), BF16),
        vm((NF, 4, 128), F32), vm((NF, 4, 128), F32), vm((16, 4, 128), F32),
        dma((13, 15)), dma((13, 15)), dma((1,)),
        dma((3,)), dma((3,)), dma((3, NS - 1)), dma((3, NS - 1)), dma((3,)), dma((3,)),
        dma((5,)), dma((2, 2)), dma((3, 16)), dma((3, 16)), dma((2, 2)),
        dma((15,)), dma((15,)), dma((31,)), dma((31,)), dma((15,)), dma((15,)),
    ]
    hidden, mods, noisy, sigma, proj_bias, vecs, text, chan, head_bias = small
    return pl.pallas_call(
        functools.partial(step_kernel, fetch),
        out_shape=[jax.ShapeDtypeStruct(grad_shape, F32), jax.ShapeDtypeStruct((8, 128), F32)],
        in_specs=[ANY] + ([ANY] * 3 if fetch else [VMEM] * 3) + [VMEM] * 2 + [SMEM] + [VMEM] * 13,
        out_specs=[VMEM, VMEM],
        scratch_shapes=scratch,
        compiler_params=pltpu.CompilerParams(
            collective_id=0, has_side_effects=True, vmem_limit_bytes=60 * 1024 * 1024
        ),
        name="step",
    )(hidden, *packs, mods, noisy, sigma, proj_bias, vecs, text, chan, head_bias, *consts)


def flow_sigma(step_index):
    remain = 1.0 - step_index.astype(F32) / STEPS
    return 3.0 * remain / (1.0 + 2.0 * remain)


def prepare(
    hidden, modulation, noisy, step_index, proj_bias, conv_bias, norm_gain, norm_shift, head_bias,
    position, class_token, vit_gain, vit_shift, attn_out_bias, mlp_out_bias, text_embed,
):
    stack = jnp.concatenate(
        [
            class_token[None], vit_gain, vit_shift, attn_out_bias[None], mlp_out_bias[None],
            jnp.zeros((5, WIDTH), F32), position.astype(F32),
        ]
    )
    chan = jnp.concatenate(
        [conv_bias[None], norm_gain[None], norm_shift[None], jnp.zeros((5, 512), F32)]
    )
    return (
        hidden.reshape(512, 3072), modulation[0], noisy.reshape(512, 64),
        flow_sigma(step_index).reshape(1, 1), proj_bias[None], widen(stack), text_embed, chan,
        jnp.broadcast_to(
            jnp.pad(
                jnp.concatenate([head_bias[:128], jnp.zeros((16,), F32), head_bias[128:]]), (0, 48)
            ),
            (8, 256),
        ),
    )


def local(
    hidden, modulation, noisy, step_index, proj_weight, proj_bias, conv_weight, conv_bias,
    norm_gain, norm_shift, head_weight, head_bias, patch_weight, position, class_token,
    vit_gain, vit_shift, attn_in, attn_out, attn_out_bias, mlp_in, mlp_in_bias, mlp_out,
    mlp_out_bias, vit_proj, text_embed,
):
    packs = pack_weights(
        proj_weight, conv_weight, head_weight, patch_weight, attn_in, attn_out, mlp_in,
        mlp_in_bias, mlp_out, vit_proj,
    )
    small = prepare(
        hidden, modulation, noisy, step_index, proj_bias, conv_bias, norm_gain, norm_shift,
        head_bias, position, class_token, vit_gain, vit_shift, attn_out_bias, mlp_out_bias,
        text_embed,
    )
    grad, score = run_step(packs, True, (96, 64), small, constants())
    return grad, score[0, 0:1]


def solution(mesh):
    placed = (
        P(("fsdp", "grp"), "slab", None, None),
        P(("fsdp", "grp"), None, None),
        P(("fsdp", "grp"), "slab", None, None),
        P(("fsdp", "grp")),
        P("fsdp", None),
        P(),
        P(None, None, None, "fsdp"),
        P(),
        P(),
        P(),
        P("fsdp", None),
        P(),
        P(None, "fsdp"),
        P("slab", None),
        P(),
        P(),
        P(),
        P("fsdp", "slab"),
        P("slab", "fsdp"),
        P(),
        P(None, ("fsdp", "slab")),
        P(("fsdp", "slab")),
        P(("fsdp", "slab"), None),
        P(),
        P("fsdp", None),
        P(("fsdp", "grp"), None),
    )
    return jax.shard_map(
        local,
        mesh=mesh,
        in_specs=placed,
        out_specs=(P("fsdp", None), P(("fsdp", "grp"))),
        check_vma=False,
    )
```

```python
import functools

import jax
import jax.numpy as jnp
import numpy as np
from jax import lax
from jax.experimental import pallas as pl
from jax.experimental.pallas import tpu as pltpu
from jax.sharding import PartitionSpec as P

HEAD_DIM = 80
STEPS = 28
LAT_SCALE = 0.3611
LAT_SHIFT = 0.1159
PIX_MEAN = (0.48145466, 0.4578275, 0.40821073)
PIX_STD = (0.26862954, 0.26130258, 0.27577711)
HIGH = lax.Precision.HIGHEST
MESH = pl.DeviceIdType.MESH
F32 = jnp.float32
BF16 = jnp.bfloat16
ANY = pl.BlockSpec(memory_space=pl.ANY)
VMEM = pl.BlockSpec(memory_space=pltpu.VMEM)
SMEM = pl.BlockSpec(memory_space=pltpu.SMEM)
ROOT = HEAD_DIM**0.5
WIDTH = 1280
WIDE = 1536
CELLS = 128 * 128 * 16
NF, NS, NZ = 32, 8, 16
LANES = 2048


def nn(a, b, precision=None):
    return lax.dot_general(
        a, b, (((1,), (0,)), ((), ())), precision=precision, preferred_element_type=F32
    )


def nt(a, b, precision=None):
    return lax.dot_general(
        a, b, (((1,), (1,)), ((), ())), precision=precision, preferred_element_type=F32
    )


def halves(values):
    high = values.astype(BF16)
    return high, (values - high.astype(F32)).astype(BF16)


def thirds(values):
    high, rest = halves(values)
    middle = (values - high.astype(F32) - rest.astype(F32)).astype(BF16)
    return [high, rest, middle]


def remote(source, dest, send, recv, target):
    return pltpu.make_async_remote_copy(
        src_ref=source, dst_ref=dest, send_sem=send, recv_sem=recv,
        device_id=target, device_id_type=MESH,
    )


def iota(shape, dim):
    return lax.broadcasted_iota(jnp.int32, shape, dim)


def norm_stats(values, mask, epsilon):
    average = jnp.sum(values, axis=-1, keepdims=True) * (1.0 / WIDTH)
    centered = (values - average) * mask
    square = jnp.sum(centered * centered, axis=-1, keepdims=True) * (1.0 / WIDTH)
    inverse = 1.0 / jnp.sqrt(square + epsilon)
    return centered * inverse, inverse


def norm_back(grads, scaled, inverse, gain):
    grads = grads * gain
    first = jnp.sum(grads, axis=-1, keepdims=True) * (1.0 / WIDTH)
    second = jnp.sum(grads * scaled, axis=-1, keepdims=True) * (1.0 / WIDTH)
    return (grads - first - scaled * second) * inverse


class Weights:
    def __init__(self, c_own, p_own, a_own, b_own, c_buf, p_buf, a_buf, b_buf, sems):
        self.c_own, self.p_own, self.owns = c_own, p_own, (a_own, b_own)
        self.c_buf, self.p_buf, self.bufs = c_buf, p_buf, (a_buf, b_buf)
        (self.z_send, self.z_recv, self.sh_send, self.sh_recv, self.fw_send, self.fw_recv,
         self.loc, self.pair_sem, self.ring_send, self.ring_recv, self.core_sem) = sems
        self.f = lax.axis_index("fsdp")
        self.g = lax.axis_index("grp")
        self.s = lax.axis_index("slab")
        self.w = self.g * NS + self.s
        self.z, self.half = self.f // 2, lax.rem(self.f, 2)
        self.core = {"grp": 1 - self.g}
        self.inside = self.f // 16 == self.g

    def to_fsdp(self, source, dest, k):
        def send(d, carry):
            target = {"fsdp": lax.rem(self.f + d, NF)}
            remote(source, dest, self.z_send.at[k], self.z_recv.at[k], target).start()
            return carry

        lax.fori_loop(1, NF, send, 0)

    def c_copy(self):
        return pltpu.make_async_copy(
            self.c_own.at[self.s], self.c_buf.at[self.s, self.f], self.loc.at[0]
        )

    def c_start(self):
        @pl.when(self.inside)
        def _():
            self.c_copy().start()
            self.to_fsdp(self.c_own.at[self.s], self.c_buf.at[self.s, self.f], 0)

    def c_part(self, n):
        return self.c_buf.at[n, pl.ds(16 * self.g, 16)]

    def c_share(self):
        @pl.when(self.inside)
        def _():
            self.c_copy().wait()
            many = self.c_buf.at[self.s, pl.ds(16 * self.g, 15)]
            remote(many, many, self.z_send.at[0], self.z_recv.at[0], self.core).wait_recv()

        @pl.when(jnp.logical_not(self.inside))
        def _():
            many = self.c_part(self.s)
            remote(many, many, self.z_send.at[0], self.z_recv.at[0], self.core).wait_recv()

        for d in range(1, NS):
            self.share_copy(0, d, self.c_part(self.s)).start()

    def share_copy(self, k, d, block):
        return remote(
            block, block, self.sh_send.at[k, d - 1], self.sh_recv.at[k, d - 1],
            {"slab": lax.rem(self.s + d, NS)},
        )

    def core_copy(self, k, block):
        return remote(block, block, self.fw_send.at[k], self.fw_recv.at[k], self.core)

    def c_core(self):
        for d in range(1, NS):
            self.share_copy(0, d, self.c_part(lax.rem(self.s + NS - d, NS))).wait_recv()
        self.core_copy(0, self.c_buf.at[:, pl.ds(16 * self.g, 16)]).start()

    def c_done(self):
        self.core_copy(0, self.c_buf.at[:, pl.ds(16 - 16 * self.g, 16)]).wait_recv()

    def p_copy(self):
        return pltpu.make_async_copy(
            self.p_own.at[self.w], self.p_buf.at[self.w, self.f], self.loc.at[1]
        )

    def p_start(self):
        self.p_copy().start()
        self.to_fsdp(self.p_own.at[self.w], self.p_buf.at[self.w, self.f], 1)

    def p_ready(self):
        many = self.p_buf.at[self.w, pl.ds(0, NF - 1)]
        remote(many, many, self.z_send.at[1], self.z_recv.at[1], self.core).wait_recv()
        self.p_copy().wait()

    def p_share(self, *pieces):
        for d in pieces:
            self.share_copy(1, d, self.p_buf.at[self.w]).start()

    def p_core(self):
        for d in range(1, NS):
            block = self.p_buf.at[self.g * NS + lax.rem(self.s + NS - d, NS)]
            self.share_copy(1, d, block).wait_recv()
        self.core_copy(1, self.p_buf.at[pl.ds(self.g * NS, NS)]).start()

    def p_done(self):
        self.core_copy(1, self.p_buf.at[pl.ds((1 - self.g) * NS, NS)]).wait_recv()

    def view(self, kind, z):
        return self.bufs[kind].at[self.g, lax.rem(z, NZ)]

    def own(self, kind):
        dest = self.view(kind, self.z)
        dest = dest.at[self.half] if kind == 0 else dest
        return pltpu.make_async_copy(self.owns[kind], dest, self.loc.at[2 + kind])

    def pair(self):
        return remote(
            self.owns[0], self.bufs[0].at[self.g, self.z, self.half],
            self.pair_sem.at[0], self.pair_sem.at[1], {"fsdp": self.z * 2 + 1 - self.half},
        )

    def start(self):
        self.pair().start()
        self.own(0).start()
        self.own(1).start()

    def step(self, kind, step, way):
        sign = NZ - 1 if way == 0 else 1
        block = self.view(kind, self.z + sign * step)
        hop = 1 if way == 0 else NZ - 1
        target = {"fsdp": lax.rem(self.z + hop, NZ) * 2 + self.half}
        slot = way * 8 + step
        return remote(
            block, block, self.ring_send.at[kind, slot], self.ring_recv.at[kind, slot], target
        )

    def share(self, kind, z):
        block = self.view(kind, z)
        remote(block, block, self.core_sem.at[kind, 0], self.core_sem.at[kind, 1], self.core).start()

    def pump(self, kind, step):
        steps = (NZ // 2, NZ // 2 - 1)
        if step == 0:
            self.own(kind).wait()
            if kind == 0:
                self.pair().wait_recv()
        for way in (0, 1):
            if 0 < step <= steps[way]:
                self.step(kind, step - 1, way).wait_recv()
            if step < steps[way]:
                self.step(kind, step, way).start()
        if step == 0:
            self.share(kind, self.z)
        for way in (0, 1):
            if 0 < step <= steps[way]:
                self.share(kind, self.z + (NZ - step if way == 0 else step))

    def landed(self, kind):
        theirs = self.bufs[kind].at[1 - self.g]
        remote(
            theirs, theirs, self.core_sem.at[kind, 0], self.core_sem.at[kind, 1], self.core
        ).wait_recv()

    def finish(self):
        for kind in range(2):
            mine = self.bufs[kind].at[self.g]
            remote(
                mine, mine, self.core_sem.at[kind, 0], self.core_sem.at[kind, 1], self.core
            ).wait_send()
            for way, steps in ((0, NZ // 2), (1, NZ // 2 - 1)):
                for step in range(steps):
                    self.step(kind, step, way).wait_send()
        self.pair().wait_send()

        @pl.when(self.inside)
        def _():
            many = self.c_buf.at[self.s, pl.ds(0, NF - 1)]
            remote(many, many, self.z_send.at[0], self.z_recv.at[0], self.core).wait_send()

        many = self.p_buf.at[self.w, pl.ds(0, NF - 1)]
        remote(many, many, self.z_send.at[1], self.z_recv.at[1], self.core).wait_send()
        for d in range(1, NS):
            self.share_copy(0, d, self.c_part(self.s)).wait_send()
            self.share_copy(1, d, self.p_buf.at[self.w]).wait_send()
        self.core_copy(0, self.c_buf.at[:, pl.ds(16 * self.g, 16)]).wait_send()
        self.core_copy(1, self.p_buf.at[pl.ds(self.g * NS, NS)]).wait_send()


def greet(targets):
    barrier = pltpu.get_barrier_semaphore()
    for target in targets:
        pl.semaphore_signal(barrier, inc=1, device_id=target, device_id_type=MESH)


def greeted(targets):
    pl.semaphore_wait(pltpu.get_barrier_semaphore(), len(targets))


def block_targets(g, s):
    found = []
    for d in range(1, 2 * NS):
        other_g = lax.rem(g + d // NS, 2)
        other_s = lax.rem(s + d % NS, NS)
        found.append((other_g * NS + other_s, {"grp": other_g, "slab": other_s}))
    return found


def pair_targets(f, s):
    z, half = f // 2, lax.rem(f, 2)
    found = []
    for h in range(2):
        there = z * 2 + lax.rem(half + h, 2)
        for d in range(NS):
            if h or d:
                found.append((h * NS + d - 1, {"fsdp": there, "slab": lax.rem(s + d, NS)}))
    return found


def all_targets():
    f, g, s = lax.axis_index("fsdp"), lax.axis_index("grp"), lax.axis_index("slab")
    return (
        [target for _, target in block_targets(g, s)]
        + [{"fsdp": lax.rem(f + d, NF)} for d in range(1, NF)]
        + [target for _, target in pair_targets(f, s)[NS:]]
    )


def reduce_gradient(mine, landed, terms, arrived, collected, sems):
    a_send, a_recv, b_send, b_recv, c_send, c_recv = sems
    f, g, s = lax.axis_index("fsdp"), lax.axis_index("grp"), lax.axis_index("slab")
    w = g * NS + s
    block = block_targets(g, s)
    copies = []
    for d, (index, target) in enumerate(block):
        copy = remote(mine.at[index], landed.at[w], a_send.at[d], a_recv.at[d], target)
        copy.start()
        copies.append(copy)
    landed[w] = mine[w]
    for copy in copies:
        copy.wait()
    total = landed[0].astype(F32)
    for index in range(1, 2 * NS):
        total = total + landed[index].astype(F32)
    for index in range(NF):
        rows, lanes = 4 * (index // 8), 96 * (index % 8)
        terms[index, :, 0:96] = total[rows : rows + 4, lanes : lanes + 96]
        terms[index, :, 96:128] = jnp.zeros((4, 32), F32)
    copies = []
    for d in range(1, NF):
        p = lax.rem(f + d, NF)
        copy = remote(terms.at[p], arrived.at[f], b_send.at[d - 1], b_recv.at[d - 1], {"fsdp": p})
        copy.start()
        copies.append(copy)
    arrived[f] = terms[f]
    for copy in copies:
        copy.wait()
    collected[w] = jnp.sum(arrived[...], axis=0)
    copies = []
    for d, (index, target) in enumerate(block):
        copy = remote(collected.at[w], collected.at[w], c_send.at[d], c_recv.at[d], target)
        copy.start()
        copies.append(copy)
    for copy in copies:
        copy.wait()


def pack_tiles(
    g, s, proj_in, conv_in, tail_in, head_in, patch_in, attn_in, back_in, up_in, bias_in, down_in,
    vit_in, patch_perm, wide_w, fill, c_own, p_own, a_own, b_own,
):
    proj = proj_in[...].astype(F32)
    proj = jnp.concatenate([proj[0:48], proj[48:96]], axis=1).astype(BF16)
    for n in range(3):
        c_own[n] = proj[16 * n : 16 * n + 16]
    c_own[3] = conv_in[:, 0:128]
    c_own[4] = head_in[:, 0:128]
    c_own[5] = tail_in[...]
    patch = nn(patch_in[...], patch_perm[...])
    patch = jnp.concatenate([patch, jnp.zeros((8, 640), F32)], axis=0).astype(BF16)
    for u in range(5):
        for rb in range(3):
            n = 3 * u + rb
            block = patch[16 * rb : 16 * rb + 16, 128 * u : 128 * u + 128]
            if n < 2:
                c_own[6 + n] = block
            else:
                p_own[n - 2] = block
    for n in range(13, 16):
        p_own[n] = jnp.zeros((16, 128), BF16)

    def tall(rows, lanes):
        values = rows.astype(F32)
        more = lanes - values.shape[1]
        if more:
            values = jnp.concatenate([values, jnp.zeros((40, more), F32)], axis=1)
        return jnp.concatenate([values, jnp.zeros((8, lanes), F32)], axis=0)

    attn = tall(attn_in[...], 512)
    back = tall(back_in[...], 256)
    vit = tall(vit_in[:, pl.ds(pl.multiple_of(128 * s, 128), 128)], 128)
    tiles = [attn[:, 128 * u : 128 * u + 128] for u in range(4)] + [back[:, 0:128], back[:, 128:256]]
    for u in range(3):
        a_own[48 * u : 48 * u + 48, :] = jnp.where(g == 0, tiles[u], tiles[3 + u]).astype(BF16)
    last = jnp.concatenate([vit[32:48], jnp.zeros((16, 128), F32)], axis=0)
    a_own[144:176, :] = jnp.where(g == 0, vit[0:32], last).astype(BF16)
    fill[0:20, :] = up_in[...].astype(F32)
    fill[20:40, :] = down_in[...].astype(F32)
    fill[40:48, :] = jnp.zeros((8, WIDTH), F32)
    values = fill[...].astype(BF16)
    wide = jnp.concatenate([nn(values[:, 0:640], wide_w[...]), nn(values[:, 640:1280], wide_w[...])], axis=1)
    bias = jnp.where(
        iota((48, 20), 0) == iota((48, 20), 1), jnp.broadcast_to(bias_in[...].astype(F32), (48, 20)), 0.0
    )
    bias = jnp.sum(bias, axis=1, keepdims=True)
    wide = jnp.where(iota((48, WIDE), 1) == 40, bias, wide)
    wide = jnp.where(g == 0, wide[:, 0:768], wide[:, 768:1536]).astype(BF16)
    for u in range(6):
        b_own[u] = wide[:, 128 * u : 128 * u + 128]


def step_kernel(
    fetch, hidden, shards, mods, noisy, sigma_ref, proj_bias, class_in, gain_in, shift_in,
    back_bias, down_bias, position_in, text, conv_b_in, norm_g_in, norm_s_in, head_b_in,
    perm, perm_t, inter, columns_w, rows_w, ph0, ph1, lane_rows, patch_perm, wide_w,
    grad_out, score_out,
    hid, mod, c_own, p_own, a_own, b_own, c_buf, p_buf, a_buf, b_buf, vecs, fill,
    proj_full, ext, halo_out, halo_in, nrm, dnrm, acc, stat_out, stat_in,
    cols_buf, pix, head_t, head_p, edge_out, edge_in, kd_out, kd_in, dirs, u_out, u_in,
    row_out, row_in, text_in, emb_out, emb_in, vd_out, vd_in, rim_out, rim_in, gsplit, mine, landed,
    terms, arrived, collected,
    x_send, x_recv, hid_sem, *sems,
):
    s = lax.axis_index("slab")
    f = lax.axis_index("fsdp")
    half = lax.rem(f, 2)
    low, high = s > 0, s < NS - 1
    low_f, high_f = jnp.where(low, 1.0, 0.0), jnp.where(high, 1.0, 0.0)
    before, after = {"slab": lax.rem(s + NS - 1, NS)}, {"slab": lax.rem(s + 1, NS)}
    hid_copy = pltpu.make_async_copy(hidden, hid, hid_sem.at[0])
    hid_copy.start()
    sigma = sigma_ref[0, 0]
    live = []

    def to_all(kind, source, dest, swap=False):
        copies = []
        for d in range(1, NS):
            p = lax.rem(s + d, NS)
            copies.append(
                remote(
                    source.at[p] if swap else source, dest.at[s],
                    x_send.at[kind, d - 1], x_recv.at[kind, d - 1], {"slab": p},
                )
            )
        for copy in copies:
            copy.start()
        live.extend(copies)
        return copies

    def to_sides(kind, source, dest):
        copies = [
            remote(source.at[0], dest.at[0], x_send.at[kind, 0], x_recv.at[kind, 0], after),
            remote(source.at[1], dest.at[1], x_send.at[kind, 1], x_recv.at[kind, 1], before),
        ]
        for copy in copies:
            copy.start()
        live.extend(copies)
        return copies

    def landed_all(copies):
        for copy in copies:
            copy.wait_recv()

    targets = all_targets() if fetch else [target for _, target in pair_targets(f, s)]
    greet(targets)

    scale = 1.0 + mods[1:2].astype(F32)
    shift = mods[0:1].astype(F32)

    def modulate(lo, hi):
        def body(i, carry):
            rows = pl.ds(pl.multiple_of(i * 32, 32), 32)
            values = hid[rows, :].astype(F32)
            average = jnp.mean(values, axis=-1, keepdims=True)
            centered = values - average
            square = jnp.mean(centered * centered, axis=-1, keepdims=True)
            scaled = centered * (1.0 / jnp.sqrt(square + 1e-06))
            mod[rows, :] = (scaled * scale + shift).astype(BF16)
            return carry

        lax.fori_loop(lo, hi, body, 0)

    if fetch:
        weights = Weights(c_own, p_own, a_own, b_own, c_buf, p_buf, a_buf, b_buf, sems[:11])
        pack_tiles(
            weights.g, s, *shards, patch_perm, wide_w, fill, c_own, p_own, a_own, b_own
        )
    else:
        weights = None
        for ref, given in zip((c_buf, p_buf, a_buf, b_buf), shards):
            ref[...] = given[...]
    hid_copy.wait()
    modulate(0, 8)
    greeted(targets)
    if fetch:
        weights.c_start()
        weights.start()
        weights.p_start()
    words_copy = remote(
        text, text_in.at[half], x_send.at[12, 0], x_recv.at[12, 0], {"fsdp": f + 1 - 2 * half}
    )
    words_copy.start()
    live.append(words_copy)
    text_in[half] = text[...]

    def pump(*steps):
        if weights is not None:
            for kind, step in enumerate(steps):
                if step is not None:
                    weights.pump(kind, step)

    fill[0:1, :] = class_in[...]
    fill[1:5, :] = gain_in[...]
    fill[5:9, :] = shift_in[...]
    fill[9:10, :] = back_bias[...]
    fill[10:11, :] = down_bias[...]
    fill[11:16, :] = jnp.zeros((5, WIDTH), F32)
    fill[16:48, :] = position_in[...].astype(F32)
    for k in range(2):
        parts = jnp.concatenate(thirds(fill[:, 640 * k : 640 * k + 640]), axis=0)
        parts = nn(parts, wide_w[...])
        vecs[:, 768 * k : 768 * k + 768] = parts[0:48] + (parts[48:96] + parts[96:144])
    pump(None, 0)
    modulate(8, 12)
    pump(0)
    modulate(12, 16)
    if weights is not None:
        weights.c_share()
        pump(1)
        weights.c_core()
        pump(2, 1)
        weights.c_done()

    def patch_unit(u):
        parts = []
        for rb in range(3):
            n = 3 * u + rb
            parts.append(c_buf[6 + n] if n < 2 else p_buf[n - 2])
        return jnp.concatenate(parts, axis=1).reshape(WIDE, 128)

    def a_unit(index):
        k = index % 3
        return a_buf[index // 3, :, :, 48 * k : 48 * k + 48].reshape(WIDE, 128)

    for n in range(3):
        both = c_buf[n].reshape(512, 128).astype(F32)
        turned = pltpu.roll(both, 64, 1).astype(BF16)
        for k in range(NF):
            at = 96 * k + 16 * n
            proj_full[at : at + 16, :] = c_buf[n, k]
            proj_full[at + 48 : at + 64, :] = turned[16 * k : 16 * k + 16]
    velocity = nn(mod[...], proj_full[...])[:, :64] + proj_bias[...]
    clean = noisy[...].astype(F32) - sigma * velocity
    lat_tok = (clean / LAT_SCALE + LAT_SHIFT).astype(BF16)
    tok_t = nt(perm_t[...], lat_tok)
    stacked = jnp.concatenate(
        [
            jnp.concatenate(
                [tok_t[0:32, 128 * k : 128 * k + 128], tok_t[32:64, 128 * k : 128 * k + 128]], axis=1
            )
            for k in range(4)
        ],
        axis=0,
    ).astype(BF16)
    latent = nn(stacked, inter[...]).astype(BF16)
    for k in range(4):
        for i2 in range(2):
            for p in range(2):
                r = 4 * k + 2 * i2 + p + 1
                for b in range(3):
                    at = (i2 * 3 + b) * 128
                    ext[16 * b : 16 * b + 16, 128 * r : 128 * r + 128] = latent[
                        32 * k + 16 * p : 32 * k + 16 * p + 16, at : at + 128
                    ]
    halo_out[0] = ext[:, 2048:2176]
    halo_out[1] = ext[:, 128:256]
    copies = to_sides(0, halo_out, halo_in)
    same = (iota((512, 512), 0) // 16 == iota((512, 512), 1) // 16).astype(BF16)

    def columns_of(rows):
        width = rows.shape[1]
        return jnp.transpose(jnp.concatenate([rows, jnp.zeros((120, width), F32)], axis=0))

    chan = jnp.concatenate(
        [conv_b_in[...], norm_g_in[...], norm_s_in[...], jnp.zeros((5, 512), F32)], axis=0
    )
    chan_cols = columns_of(chan)
    conv_bias, gain, gshift = chan_cols[:, 0:1], chan_cols[:, 1:2], chan_cols[:, 2:3]
    eye = (iota((128, 128), 0) == iota((128, 128), 1)).astype(BF16)
    conv0 = c_buf[3].reshape(512, 128)
    head0 = c_buf[4].reshape(512, 128)
    tail = c_buf[5].reshape(512, 128)
    head_p[...] = (nn(head0, ph0[...]) + nn(tail, ph1[...])).astype(BF16)
    head_t[...] = (
        lax.dot_general(ph0[...], head0, (((0,), (1,)), ((), ())), preferred_element_type=F32)
        + lax.dot_general(ph1[...], tail, (((0,), (1,)), ((), ())), preferred_element_type=F32)
    ).astype(BF16)
    head_bias = jnp.broadcast_to(head_b_in[...], (8, 256))
    bias_row = nn(head_bias[:, 0:128], ph0[...].astype(F32), HIGH) + nn(
        head_bias[:, 128:256], ph1[...].astype(F32), HIGH
    )
    head_col = columns_of(bias_row)[:, 0:1]
    pump(3, 2)
    if weights is not None:
        weights.p_ready()
    landed_all(copies)
    if weights is not None:
        weights.p_share(1, 2, 3)
    ext[:, 0:128] = (halo_in[0].astype(F32) * low_f).astype(BF16)
    ext[:, 2176:2304] = (halo_in[1].astype(F32) * high_f).astype(BF16)
    acc[...] = jnp.zeros_like(acc)

    def conv_chunk(i, carry):
        at = pl.multiple_of(i * 256, 256)
        parts = [ext[:, pl.ds(pl.multiple_of(at + 128 * a, 128), 256)] for a in range(3)]
        columns = jnp.concatenate(parts + [jnp.zeros((112, 256), BF16)], axis=0)
        out = nn(conv0, columns[0:128]) + nn(tail, columns[128:256]) + conv_bias
        nrm[:, pl.ds(at, 256)] = out
        acc[0] += out[:, 0:128] + out[:, 128:256]
        square = out * out
        acc[1] += square[:, 0:128] + square[:, 128:256]
        return carry

    lax.fori_loop(0, 8, conv_chunk, 0)

    def group_totals(kind, step=None):
        ones = jnp.ones((8, 128), BF16)
        first, second = [
            nt(ones, part[0]) + (nt(ones, part[1]) + nt(ones, part[2]))
            for part in (thirds(acc[0]), thirds(acc[1]))
        ]
        k = kind - 1
        stat_out[k] = jnp.where(iota((8, 512), 0) == 0, first, second)
        copies = to_all(kind, stat_out.at[k], stat_in.at[k])
        stat_in[k, s] = stat_out[k]
        if step is not None:
            pump(*step)
        landed_all(copies)
        total = stat_in[k, 0]
        for index in range(1, NS):
            total = total + stat_in[k, index]
        sums = nn(jnp.concatenate(thirds(total), axis=0), same)
        columns = columns_of(sums[0:8] + (sums[8:16] + sums[16:24]))
        return columns[:, 0:1] * (1.0 / CELLS), columns[:, 1:2] * (1.0 / CELLS)

    average, square = group_totals(1, (4, 3))
    inverse = 1.0 / jnp.sqrt(square - average * average + 1e-06)
    if weights is not None:
        weights.p_share(4, 5, 6, 7)

    def head_chunk(i, carry):
        at = pl.multiple_of(i * 256, 256)
        normed = (nrm[:, pl.ds(at, 256)] - average) * inverse
        nrm[:, pl.ds(at, 256)] = normed
        gained = normed * gain + gshift
        active = (gained * (1.0 / (1.0 + jnp.exp(-gained)))).astype(BF16)
        cells = (nn(head_t[...], active) + head_col).astype(BF16)
        for rr in range(2):
            rows = pl.ds(pl.multiple_of(i * 64 + 32 * rr, 32), 32)
            for x in range(8):
                pix[rows, 128 * x : 128 * x + 128] = cells[
                    32 * x : 32 * x + 32, 128 * rr : 128 * rr + 128
                ]
        return carry

    lax.fori_loop(0, 8, head_chunk, 0)
    pump(5, 4)
    narrow = nt(columns_w[...], pix[...]).astype(BF16)
    raw = jnp.zeros((80, 512), F32)
    for m in range(3):
        raw = raw + nn(narrow[128 * m : 128 * m + 80], rows_w[512 * m : 512 * m + 512, :])
    edge_out[0, 0] = raw[:, 256:384]
    edge_out[0, 1] = raw[:, 384:512]
    copies = to_sides(2 + 1, edge_out.at[0], edge_in.at[0])
    pump(6, 5)
    if weights is not None:
        weights.p_core()
    corr0 = jnp.where(low, 1.0, lane_rows[0:1, :])
    corr1 = jnp.where(high, 1.0, lane_rows[1:2, :])
    img_scale, img_shift = lane_rows[2:3, :], lane_rows[3:4, :]
    if weights is not None:
        weights.p_done()
    landed_all(copies)
    top = (raw[:, 0:128] * corr0 + edge_in[0, 0] * low_f) * img_scale + img_shift
    bottom = (raw[:, 128:256] * corr1 + edge_in[0, 1] * high_f) * img_scale + img_shift
    patches = jnp.concatenate(
        [
            jnp.concatenate([part[16 * u : 16 * u + 16] for u in range(5)], axis=1)
            for part in (top, bottom)
        ],
        axis=0,
    ).astype(BF16)
    pump(7)
    embedded = vecs[16:48, :]
    for u in range(5):
        embedded = embedded + nt(patches[:, 128 * u : 128 * u + 128], patch_unit(u))
    lane = iota((1, WIDE), 1)
    inner = lax.rem(lane, 48)
    mask = (inner < 40).astype(F32)
    gains = [vecs[1 + i : 2 + i, :] for i in range(4)]
    shifts = [vecs[5 + i : 6 + i, :] for i in range(4)]
    pump(8, 6)
    if weights is not None:
        weights.landed(0)

    class_hat, _ = norm_stats(vecs[0:1, :], mask, 1e-05)
    class_pre = class_hat * gains[0] + shifts[0]
    class_hat, _ = norm_stats(class_pre, mask, 1e-05)
    class_unit = jnp.broadcast_to(class_hat * gains[1] + shifts[1], (8, WIDE)).astype(BF16)
    attn = [a_unit(i) for i in range(4)]
    class_qkv = jnp.concatenate([nn(class_unit, attn[i]) for i in range(4)], axis=1)
    class_qkv = class_qkv.astype(BF16).astype(F32)
    place512 = iota((8, 512), 1)
    row512 = iota((8, 512), 0)
    start = jnp.where(row512 == 0, 0, 240)
    in_head = row512 < 2
    key_at = in_head & (place512 >= start + 80) & (place512 < start + 160)
    val_at = in_head & (place512 >= start + 160) & (place512 < start + 240)
    query = jnp.where(key_at, pltpu.roll(class_qkv, 80, 1), 0.0)
    class_exp = jnp.exp(jnp.sum(query * class_qkv, axis=-1, keepdims=True) / ROOT)
    query_b = query.astype(BF16)
    key_dir = nt(query_b[:, 0:128], attn[0])
    for i in range(1, 4):
        key_dir = key_dir + nt(query_b[:, 128 * i : 128 * i + 128], attn[i])
    kd_out[...] = key_dir[0:2]
    copies = to_all(4, kd_out, kd_in)
    kd_in[s] = key_dir[0:2]
    hat0, inv0 = norm_stats(embedded, mask, 1e-05)
    hat1, inv1 = norm_stats(hat0 * gains[0] + shifts[0], mask, 1e-05)
    unit = hat1 * gains[1] + shifts[1]
    unit_b = unit.astype(BF16)
    unit = unit_b.astype(F32)
    pump(None, 7)
    landed_all(copies)
    for index in range(NS):
        dirs[2 * index : 2 * index + 2, :] = kd_in[index]
    token_exp = jnp.exp(nt(dirs[0:16, :], unit, HIGH) / ROOT)
    gathered = nn(token_exp, unit, HIGH)
    sums = jnp.broadcast_to(jnp.sum(token_exp, axis=1, keepdims=True), (16, WIDE))
    for index in range(NS):
        u_out[index, 0:2] = gathered[2 * index : 2 * index + 2]
        u_out[index, 2:4] = sums[2 * index : 2 * index + 2]
    copies = to_all(5, u_out, u_in, swap=True)
    u_in[s] = u_out[s]
    pump(None, 8)
    landed_all(copies)
    total = u_in[0]
    for index in range(1, NS):
        total = total + u_in[index]
    denominator = class_exp[0:2] + total[2:4, 0:1]
    mixed = halves(jnp.concatenate([total[0:2], jnp.zeros((6, WIDE), F32)], axis=0))
    first = nn(mixed[0], attn[1]) + nn(mixed[1], attn[1])
    second = nn(mixed[0], attn[3]) + nn(mixed[1], attn[3])
    heads1 = jnp.where(val_at[0:1, 128:256], first[0:1] + class_exp[0:1] * class_qkv[0:1, 128:256], 0.0)
    heads3 = jnp.where(val_at[1:2, 384:512], second[1:2] + class_exp[1:2] * class_qkv[0:1, 384:512], 0.0)
    heads1 = heads1 / denominator[0:1]
    heads3 = heads3 / denominator[1:2]
    rows1 = a_unit(4)
    rows3 = a_unit(5)

    def wide8(row):
        if row.shape[0] == 1:
            return jnp.broadcast_to(row, (8, row.shape[1])).astype(BF16)
        return jnp.concatenate([row, jnp.zeros((6, row.shape[1]), F32)], axis=0).astype(BF16)

    def mine_of(rows):
        return jnp.where(half == 0, rows[0:1], rows[1:2])

    attn_part = nt(wide8(heads1), rows1) + nt(wide8(heads3), rows3)

    def pair_sum(kind, k, rows):
        row_out[k] = rows[0:2]
        copies = [
            remote(
                row_out.at[k], row_in.at[k, half, s], x_send.at[kind, index], x_recv.at[kind, index],
                target,
            )
            for index, target in pair_targets(f, s)
        ]
        for copy in copies:
            copy.start()
        live.extend(copies)
        row_in[k, half, s] = row_out[k]
        landed_all(copies)
        sums = []
        for h in range(2):
            total = row_in[k, h, 0]
            for index in range(1, NS):
                total = total + row_in[k, h, index]
            sums.append(total)
        return sums

    sums = pair_sum(6, 0, attn_part)
    block_mid = class_pre + jnp.concatenate([sums[0][0:1], sums[1][0:1]], axis=0) + vecs[9:10, :]
    hat2, inv2 = norm_stats(block_mid, mask, 1e-05)
    mlp_input = hat2 * gains[2] + shifts[2]
    mlp_input = wide8(jnp.where(lane == 40, 1.0, mlp_input))
    if weights is not None:
        weights.landed(1)
    hidden_units = [b_buf[i // 6, :, i % 6].reshape(WIDE // 2, 128) for i in range(12)]
    unit_at = lax.rem(iota((1, WIDE // 2), 1), 48) < 20
    preact = nt(mlp_input[:, 0:128], hidden_units[0])
    for i in range(1, 12):
        preact = preact + nt(mlp_input[:, 128 * i : 128 * i + 128], hidden_units[i])
    preact = jnp.where(unit_at, preact, 0.0)
    cdf = 0.5 * (1.0 + lax.erf(preact * 0.7071067811865476))
    active = preact * cdf
    active = pltpu.roll(active, 20, 1).astype(BF16)
    mlp_part = jnp.concatenate([nn(active, hidden_units[i]) for i in range(12)], axis=1)
    sums = pair_sum(7, 1, mlp_part)
    block_out = block_mid + (sums[0] + sums[1]) + vecs[10:11, :]
    hat3, inv3 = norm_stats(block_out, mask, 1e-05)
    post = wide8(hat3 * gains[3] + shifts[3])
    vit = jnp.concatenate([a_buf[0, :, :, 144:176], a_buf[1, :, :, 144:160]], axis=2).reshape(WIDE, 128)
    embed = nn(post, vit)[0:2]
    words_copy.wait_recv()
    words = jnp.concatenate([text_in[0], text_in[1]], axis=0)
    own_words = jnp.concatenate(
        [text_in[k, :, pl.ds(pl.multiple_of(128 * s, 128), 128)] for k in range(2)], axis=0
    )
    four = jnp.concatenate([own_words, embed], axis=0)
    exact = four.astype(BF16).astype(F32)
    eight = nt(jnp.concatenate([exact, four - exact], axis=0).astype(BF16), vit)
    four = eight[0:4] + eight[4:8]
    dots = jnp.sum(embed * own_words, axis=-1, keepdims=True)
    squares = jnp.sum(embed * embed, axis=-1, keepdims=True)
    emb_out[0:2, :] = four[0:2]
    emb_out[2:4, :] = jnp.where(lane == 40, dots, jnp.where(lane == 41, squares, four[2:4]))
    copies = to_all(13, emb_out, emb_in)
    emb_in[s] = emb_out[...]
    landed_all(copies)
    total = emb_in[0]
    for index in range(1, NS):
        total = total + emb_in[index]
    dots, size_e = total[2:4, 40:41], total[2:4, 41:42] + 1e-06
    size_t = jnp.sum(words * words, axis=-1, keepdims=True) + 1e-06
    sizes = jnp.sqrt(size_e) * jnp.sqrt(size_t)
    score = 100.0 * dots / sizes
    score_out[...] = jnp.broadcast_to(mine_of(score), (8, 128))
    d_post = (-1.0 / 64.0) * ((100.0 / sizes) * total[0:2] - (score / size_e) * total[2:4])
    d_second = norm_back(d_post[0:2], hat3, inv3, gains[3])
    d_second_b = wide8(d_second)
    d_active = nt(d_second_b[:, 0:128], hidden_units[0])
    for i in range(1, 12):
        d_active = d_active + nt(d_second_b[:, 128 * i : 128 * i + 128], hidden_units[i])
    d_active = pltpu.roll(d_active, WIDE // 2 - 20, 1)
    slope = cdf + preact * jnp.exp(-0.5 * preact * preact) * 0.3989422804014327
    d_pre = jnp.where(unit_at, d_active * slope, 0.0).astype(BF16)
    input_part = jnp.concatenate([nn(d_pre, hidden_units[i]) for i in range(12)], axis=1)
    sums = pair_sum(8, 2, input_part)
    d_first = d_second + norm_back(sums[0] + sums[1], hat2, inv2, gains[2])
    d_first = wide8(mine_of(d_first))
    d_heads1 = nn(d_first, rows1).astype(BF16)
    d_heads3 = nn(d_first, rows3).astype(BF16)
    value0 = nt(jnp.where(val_at[0:1, 128:256], d_heads1.astype(F32), 0.0).astype(BF16), attn[1])
    value1 = nt(jnp.where(val_at[1:2, 384:512], d_heads3.astype(F32), 0.0).astype(BF16), attn[3])
    expect0 = jnp.sum(d_heads1[0:1].astype(F32) * heads1, axis=-1, keepdims=True)
    expect1 = jnp.sum(d_heads3[0:1].astype(F32) * heads3, axis=-1, keepdims=True)
    vd_out[0:1, :] = value0[0:1]
    vd_out[1:2, :] = value1[0:1]
    vd_out[2:3, :] = jnp.where(lane < 128, denominator[0:1], denominator[1:2])
    vd_out[3:4, :] = jnp.where(lane < 128, expect0, expect1)
    copies = to_all(9, vd_out, vd_in)
    vd_in[s] = vd_out[...]
    token_logits = nt(unit, dirs[0:16, :], HIGH) / ROOT
    landed_all(copies)
    head_at = iota((1, 16), 1)
    denominators = jnp.zeros((1, 16), F32)
    expects = jnp.zeros((1, 16), F32)
    for index in range(NS):
        dirs[16 + 2 * index : 18 + 2 * index, :] = vd_in[index, 0:2]
        for h in range(2):
            here = head_at == 2 * index + h
            denominators = jnp.where(here, vd_in[index, 2:3, 128 * h : 128 * h + 1], denominators)
            expects = jnp.where(here, vd_in[index, 3:4, 128 * h : 128 * h + 1], expects)
    token_weight = jnp.exp(token_logits) / denominators
    token_dots = nt(unit, dirs[16:32, :], HIGH)
    logit_grads = token_weight * (token_dots - expects)
    d_unit = nn(logit_grads / ROOT, dirs[0:16, :], HIGH) + nn(
        token_weight.astype(BF16).astype(F32), dirs[16:32, :], HIGH
    )
    d_pre_x = norm_back(d_unit, hat1, inv1, gains[1])
    d_embedded = norm_back(d_pre_x, hat0, inv0, gains[0]).astype(BF16)
    d_parts = [nn(d_embedded, patch_unit(u)) for u in range(5)]
    d_top = jnp.concatenate([part[0:16] for part in d_parts], axis=0) * img_scale
    d_bottom = jnp.concatenate([part[16:32] for part in d_parts], axis=0) * img_scale
    edge_out[1, 0] = d_bottom
    edge_out[1, 1] = d_top
    copies = to_sides(10, edge_out.at[1], edge_in.at[1])
    landed_all(copies)
    d_raw = jnp.concatenate(
        [
            jnp.concatenate(
                [d_top * corr0, d_bottom * corr1, edge_in[1, 1] * high_f, edge_in[1, 0] * low_f],
                axis=1,
            ),
            jnp.zeros((48, 512), F32),
        ],
        axis=0,
    ).astype(BF16)
    d_narrow = jnp.concatenate(
        [nt(rows_w[512 * m : 512 * m + 512, :], d_raw) for m in range(3)], axis=1
    ).astype(BF16)
    for k in range(4):
        d_pix = nn(d_narrow, columns_w[:, 256 * k : 256 * k + 256]).astype(BF16)
        for x in range(2):
            rows = slice(64 * k + 32 * x, 64 * k + 32 * x + 32)
            for r in range(16):
                cols_buf[rows, 128 * r : 128 * r + 128] = d_pix[
                    32 * r : 32 * r + 32, 128 * x : 128 * x + 128
                ]
    acc[...] = jnp.zeros_like(acc)

    def head_back(i, carry):
        at = pl.multiple_of(i * 256, 256)
        grads = nn(head_p[...], cols_buf[:, pl.ds(at, 256)])
        normed = nrm[:, pl.ds(at, 256)]
        gained = normed * gain + gshift
        gate = 1.0 / (1.0 + jnp.exp(-gained))
        grads = grads * (gate * (1.0 + gained * (1.0 - gate))) * gain
        dnrm[:, pl.ds(at, 256)] = grads
        acc[0] += grads[:, 0:128] + grads[:, 128:256]
        both = grads * normed
        acc[1] += both[:, 0:128] + both[:, 128:256]
        return carry

    lax.fori_loop(0, 8, head_back, 0)
    conv0_t = nt(eye, conv0).astype(BF16)
    tail_t = nt(eye[0:16], tail).astype(BF16)
    mean0, mean1 = group_totals(2)

    def conv_back(i, carry):
        at = pl.multiple_of(i * 256, 256)
        grads = (dnrm[:, pl.ds(at, 256)] - mean0 - nrm[:, pl.ds(at, 256)] * mean1) * inverse
        grads = grads.astype(BF16)
        dnrm[0:128, pl.ds(at, 256)] = nn(conv0_t, grads)
        dnrm[128:144, pl.ds(at, 256)] = nn(tail_t, grads)
        return carry

    lax.fori_loop(0, 8, conv_back, 0)
    total = jnp.zeros((16, 2304), F32)
    column = lax.rem(iota((16, 2304), 1), 128)
    for b in range(3):
        part = jnp.zeros((16, 2304), F32)
        for a in range(3):
            t = 3 * a + b
            pieces = [dnrm[16 * t : 16 * t + 16, :]]
            if a:
                pieces = [jnp.zeros((16, 128 * a), F32)] + pieces
            if a < 2:
                pieces = pieces + [jnp.zeros((16, 256 - 128 * a), F32)]
            part = part + jnp.concatenate(pieces, axis=1)
        if b == 0:
            part = jnp.where(column < 127, pltpu.roll(part, 2303, 1), 0.0)
        if b == 2:
            part = jnp.where(column > 0, pltpu.roll(part, 1, 1), 0.0)
        total = total + part
    rim_out[0] = total[:, 2176:2304]
    rim_out[1] = total[:, 0:128]
    copies = to_sides(11, rim_out, rim_in)
    landed_all(copies)
    rows = [total[:, 128 * r + 128 : 128 * r + 256] for r in range(16)]
    rows[0] = rows[0] + rim_in[0] * low_f
    rows[15] = rows[15] + rim_in[1] * high_f
    rows = [-sigma * (row / LAT_SCALE) for row in rows]
    stacked = jnp.concatenate(
        [
            jnp.concatenate([rows[4 * k + p], rows[4 * k + 2 + p]], axis=1)
            for k in range(4)
            for p in range(2)
        ],
        axis=0,
    ).astype(BF16)
    centre = jnp.concatenate([inter[:, 128:256], inter[:, 512:640]], axis=1)
    tok = nt(stacked, centre)
    tok_t = jnp.concatenate(
        [
            jnp.concatenate(
                [tok[32 * k : 32 * k + 32, 128 * q : 128 * q + 128] for k in range(4)], axis=1
            )
            for q in range(2)
        ],
        axis=0,
    ).astype(BF16)
    d_vel = nn(perm[...], tok_t).astype(BF16)
    for quarter in range(4):
        part = nn(d_vel, mod[:, 768 * quarter : 768 * quarter + 768])
        for w in range(2 * NS):
            gsplit[w, 4 * quarter : 4 * quarter + 4] = part[4 * w : 4 * w + 4]
    for copy in live:
        copy.wait_send()
    if weights is not None:
        weights.finish()
        mine[...] = gsplit[...].astype(BF16)
        reduce_gradient(mine, landed, terms, arrived, collected, sems[11:])
        whole = jnp.concatenate([collected[w] for w in range(2 * NS)], axis=0)
        grad_out[...] = jnp.transpose(whole)[0:96, :]
    else:
        grad_out[...] = gsplit[...]


def resize_table(out_count, in_count):
    stretch = in_count / out_count
    centers = (np.arange(out_count) + 0.5) * stretch
    places = np.arange(in_count) + 0.5
    weights = np.maximum(0.0, 1.0 - np.abs(places[None, :] - centers[:, None]) / stretch)
    return weights / weights.sum(axis=1, keepdims=True)


def constants():
    perm = np.zeros((64, 64))
    for c in range(16):
        for p in range(2):
            for q in range(2):
                perm[4 * c + 2 * p + q, q * 32 + p * 16 + c] = 1
    inter = np.zeros((2, 2, 64, 2, 3, 128))
    for q in range(2):
        for i2 in range(2):
            for j in range(64):
                for b in range(3):
                    at = 2 * j + q - b + 1
                    if 0 <= at < 128:
                        inter[q, i2, j, i2, b, at] = 1
    table = resize_table(224, 1024)
    columns = np.zeros((3, 8, 16, 8, 128))
    for m in range(3):
        for u in range(5):
            if 3 * u + m < 14:
                for pc in range(16):
                    columns[m, u, pc] = table[14 * pc + 3 * u + m].reshape(128, 8).T
    rows = np.zeros((3, 16, 4, 8, 4, 128))
    local = table[28 * 3 : 28 * 3 + 28, 128 * 3 : 128 * 3 + 128].reshape(28, 16, 8)
    to_next = table[28 * 4, 128 * 3 : 128 * 3 + 128].reshape(16, 8)
    to_prev = table[28 * 3 - 1, 128 * 3 : 128 * 3 + 128].reshape(16, 8)
    for m in range(3):
        for c in range(3):
            for a in range(14):
                at = 42 * m + 14 * c + a
                rows[m, :, c, :, 0, at] = local[a]
                rows[m, :, c, :, 1, at] = local[14 + a]
            rows[m, :, c, :, 2, 42 * m + 14 * c] = to_next
            rows[m, :, c, :, 3, 42 * m + 14 * c + 13] = to_prev
    lanes = np.zeros((8, 128))
    lanes[0:2] = 1
    for m in range(3):
        for c in range(3):
            for a in range(14):
                at = 42 * m + 14 * c + a
                lanes[2, at] = 0.5 / PIX_STD[c]
                lanes[3, at] = (0.5 - PIX_MEAN[c]) / PIX_STD[c]
            lanes[0, 42 * m + 14 * c] = table[0, 0] / table[28, 128]
            lanes[1, 42 * m + 14 * c + 13] = table[223, 1023] / table[27, 127]
    ph = np.zeros((2, 128, 8, 32))
    for c in range(3):
        for y in range(8):
            for x in range(8):
                k = 64 * c + 8 * y + x
                if k < 128:
                    ph[0, k, x, 8 * c + y] = 1
                else:
                    ph[1, 16 + k - 128, x, 8 * c + y] = 1
    one = lambda v: jnp.asarray(v.astype(jnp.bfloat16))
    ph = ph.reshape(2, 128, 256)
    order = np.zeros((3, 14, 14, 640))
    for c in range(3):
        for a in range(14):
            for b in range(14):
                order[c, a, b, 128 * (b // 3) + 42 * (b % 3) + 14 * c + a] = 1
    wide = np.zeros((16, 40, 16, 48))
    for k in range(16):
        wide[k, np.arange(40), k, np.arange(40)] = 1
    return (
        one(perm), one(perm.T), one(inter.reshape(256, 768)),
        one(columns.reshape(384, 1024)), one(rows.reshape(1536, 512)),
        one(ph[0]), one(ph[1]), jnp.asarray(lanes.astype(np.float32)),
        one(order.reshape(588, 640)), one(wide.reshape(640, 768)),
    )


def raw_shards(proj, conv, head, patch, attn_in, attn_out, mlp_in, mlp_bias, mlp_out, vit):
    conv_t = conv.reshape(144, 16).T
    tail = jnp.pad(jnp.concatenate([conv_t[:, 128:], head[:, 128:]], axis=1), ((0, 0), (0, 48)))
    back = attn_out.T
    back = jnp.concatenate(
        [jnp.pad(back[:, :80], ((0, 0), (32, 16))), jnp.pad(back[:, 80:], ((0, 0), (16, 32)))], axis=1
    )
    return (
        proj, conv_t, tail, head, patch.T, attn_in, back, mlp_in.T, mlp_bias[None], mlp_out, vit
    )


def run_step(shards, fetch, grad_shape, hidden, sigma, small, consts):
    vm, dma = pltpu.VMEM, pltpu.SemaphoreType.DMA
    scratch = [
        vm((512, 3072), BF16), vm((512, 3072), BF16),
        vm((8, 16, 128), BF16), vm((16, 16, 128), BF16), vm((176, 128), BF16), vm((6, 48, 128), BF16),
        vm((8, NF, 16, 128), BF16), vm((16, NF, 16, 128), BF16),
        vm((2, NZ, 2, 176, 128), BF16), vm((2, NZ, 6, 48, 128), BF16),
        vm((48, WIDE), F32), vm((48, WIDTH), F32),
        vm((3072, 128), BF16), vm((48, 2304), BF16), vm((2, 48, 128), BF16), vm((2, 48, 128), BF16),
        vm((512, LANES), F32), vm((512, LANES), F32), vm((2, 512, 128), F32),
        vm((2, 8, 512), F32), vm((2, NS, 8, 512), F32),
        vm((256, LANES), BF16), vm((512, 1024), BF16), vm((256, 512), BF16), vm((512, 256), BF16),
        vm((2, 2, 80, 128), F32), vm((2, 2, 80, 128), F32),
        vm((2, WIDE), F32), vm((NS, 2, WIDE), F32), vm((32, WIDE), F32),
        vm((NS, 4, WIDE), F32), vm((NS, 4, WIDE), F32),
        vm((3, 2, WIDE), F32), vm((3, 2, NS, 2, WIDE), F32), vm((2, 1, 1024), F32),
        vm((4, WIDE), F32), vm((NS, 4, WIDE), F32),
        vm((4, WIDE), F32), vm((NS, 4, WIDE), F32),
        vm((2, 16, 128), F32), vm((2, 16, 128), F32),
        vm((16, 16, 768), F32), vm((16, 16, 768), BF16), vm((16, 16, 768), BF16),
        vm((NF, 4, 128), F32), vm((NF, 4, 128), F32), vm((16, 4, 128), F32),
        dma((14, 15)), dma((14, 15)), dma((1,)),
        dma((2,)), dma((2,)), dma((2, NS - 1)), dma((2, NS - 1)), dma((2,)), dma((2,)),
        dma((4,)), dma((2,)), dma((2, 16)), dma((2, 16)), dma((2, 2)),
        dma((15,)), dma((15,)), dma((31,)), dma((31,)), dma((15,)), dma((15,)),
    ]
    count = len(shards)

    def kernel(hidden_ref, *refs):
        mods, noisy, sigma_ref = refs[count : count + 3]
        step_kernel(
            fetch, hidden_ref, refs[:count], mods, noisy, sigma_ref, *refs[count + 3 :]
        )

    return pl.pallas_call(
        kernel,
        out_shape=[jax.ShapeDtypeStruct(grad_shape, F32), jax.ShapeDtypeStruct((8, 128), F32)],
        in_specs=[ANY] + [VMEM] * (count + 2) + [SMEM] + [VMEM] * (len(small) - 2 + len(consts)),
        out_specs=[VMEM, VMEM],
        scratch_shapes=scratch,
        compiler_params=pltpu.CompilerParams(
            collective_id=0, has_side_effects=True, vmem_limit_bytes=60 * 1024 * 1024
        ),
        name="step",
    )(hidden, *shards, *small[:2], sigma, *small[2:], *consts)


def flow_sigma(step_index):
    remain = 1.0 - step_index.astype(F32) / STEPS
    return 3.0 * remain / (1.0 + 2.0 * remain)


def prepare(
    modulation, noisy, proj_bias, conv_bias, norm_gain, norm_shift, head_bias,
    position, class_token, vit_gain, vit_shift, attn_out_bias, mlp_out_bias, text_embed,
):
    padded = jnp.concatenate(
        [head_bias[:128], jnp.zeros((16,), F32), head_bias[128:], jnp.zeros((48,), F32)]
    )
    return (
        modulation[0], noisy.reshape(512, 64), proj_bias[None], class_token[None], vit_gain, vit_shift,
        attn_out_bias[None], mlp_out_bias[None], position, text_embed, conv_bias[None],
        norm_gain[None], norm_shift[None], padded[None],
    )


def local(
    hidden, modulation, noisy, step_index, proj_weight, proj_bias, conv_weight, conv_bias,
    norm_gain, norm_shift, head_weight, head_bias, patch_weight, position, class_token,
    vit_gain, vit_shift, attn_in, attn_out, attn_out_bias, mlp_in, mlp_in_bias, mlp_out,
    mlp_out_bias, vit_proj, text_embed,
):
    shards = raw_shards(
        proj_weight, conv_weight, head_weight, patch_weight, attn_in, attn_out, mlp_in,
        mlp_in_bias, mlp_out, vit_proj,
    )
    small = prepare(
        modulation, noisy, proj_bias, conv_bias, norm_gain, norm_shift, head_bias, position,
        class_token, vit_gain, vit_shift, attn_out_bias, mlp_out_bias, text_embed,
    )
    grad, score = run_step(
        shards, True, (96, 64), hidden.reshape(512, 3072), flow_sigma(step_index).reshape(1, 1),
        small, constants(),
    )
    return grad, score[0, 0:1]


def solution(mesh):
    placed = (
        P(("fsdp", "grp"), "slab", None, None),
        P(("fsdp", "grp"), None, None),
        P(("fsdp", "grp"), "slab", None, None),
        P(("fsdp", "grp")),
        P("fsdp", None),
        P(),
        P(None, None, None, "fsdp"),
        P(),
        P(),
        P(),
        P("fsdp", None),
        P(),
        P(None, "fsdp"),
        P("slab", None),
        P(),
        P(),
        P(),
        P("fsdp", "slab"),
        P("slab", "fsdp"),
        P(),
        P(None, ("fsdp", "slab")),
        P(("fsdp", "slab")),
        P(("fsdp", "slab"), None),
        P(),
        P("fsdp", None),
        P(("fsdp", "grp"), None),
    )
    return jax.shard_map(
        local,
        mesh=mesh,
        in_specs=placed,
        out_specs=(P("fsdp", None), P(("fsdp", "grp"))),
        check_vma=False,
    )
```

```python
import functools

import jax
import jax.numpy as jnp
import numpy as np
from jax import lax
from jax.experimental import pallas as pl
from jax.experimental.pallas import tpu as pltpu
from jax.sharding import PartitionSpec as P

HEAD_DIM = 80
STEPS = 28
LAT_SCALE = 0.3611
LAT_SHIFT = 0.1159
PIX_MEAN = (0.48145466, 0.4578275, 0.40821073)
PIX_STD = (0.26862954, 0.26130258, 0.27577711)
HIGH = lax.Precision.HIGHEST
MESH = pl.DeviceIdType.MESH
F32 = jnp.float32
BF16 = jnp.bfloat16
ANY = pl.BlockSpec(memory_space=pl.ANY)
VMEM = pl.BlockSpec(memory_space=pltpu.VMEM)
SMEM = pl.BlockSpec(memory_space=pltpu.SMEM)
ROOT = HEAD_DIM**0.5
WIDTH = 1280
WIDE = 1536
CELLS = 128 * 128 * 16
NF, NS, NZ = 32, 8, 16
LANES = 2048


def nn(a, b, precision=None):
    return lax.dot_general(
        a, b, (((1,), (0,)), ((), ())), precision=precision, preferred_element_type=F32
    )


def nt(a, b, precision=None):
    return lax.dot_general(
        a, b, (((1,), (1,)), ((), ())), precision=precision, preferred_element_type=F32
    )


def halves(values):
    high = values.astype(BF16)
    return high, (values - high.astype(F32)).astype(BF16)


def thirds(values):
    high, rest = halves(values)
    middle = (values - high.astype(F32) - rest.astype(F32)).astype(BF16)
    return [high, rest, middle]


def remote(source, dest, send, recv, target):
    return pltpu.make_async_remote_copy(
        src_ref=source, dst_ref=dest, send_sem=send, recv_sem=recv,
        device_id=target, device_id_type=MESH,
    )


def iota(shape, dim):
    return lax.broadcasted_iota(jnp.int32, shape, dim)


def norm_stats(values, mask, epsilon):
    average = jnp.sum(values, axis=-1, keepdims=True) * (1.0 / WIDTH)
    centered = (values - average) * mask
    square = jnp.sum(centered * centered, axis=-1, keepdims=True) * (1.0 / WIDTH)
    inverse = 1.0 / jnp.sqrt(square + epsilon)
    return centered * inverse, inverse


def norm_back(grads, scaled, inverse, gain):
    grads = grads * gain
    first = jnp.sum(grads, axis=-1, keepdims=True) * (1.0 / WIDTH)
    second = jnp.sum(grads * scaled, axis=-1, keepdims=True) * (1.0 / WIDTH)
    return (grads - first - scaled * second) * inverse


class Weights:
    def __init__(self, c_own, p_own, a_own, b_own, c_buf, p_buf, a_buf, b_buf, sems):
        self.c_own, self.p_own, self.owns = c_own, p_own, (a_own, b_own)
        self.c_buf, self.p_buf, self.bufs = c_buf, p_buf, (a_buf, b_buf)
        (self.z_send, self.z_recv, self.sh_send, self.sh_recv, self.fw_send, self.fw_recv,
         self.loc, self.pair_sem, self.ring_send, self.ring_recv, self.core_sem) = sems
        self.f = lax.axis_index("fsdp")
        self.g = lax.axis_index("grp")
        self.s = lax.axis_index("slab")
        self.w = self.g * NS + self.s
        self.z, self.half = self.f // 2, lax.rem(self.f, 2)
        self.core = {"grp": 1 - self.g}
        self.inside = self.f // 16 == self.g

    def to_fsdp(self, source, dest, k):
        def send(d, carry):
            target = {"fsdp": lax.rem(self.f + d, NF)}
            remote(source, dest, self.z_send.at[k], self.z_recv.at[k], target).start()
            return carry

        lax.fori_loop(1, NF, send, 0)

    def c_copy(self):
        return pltpu.make_async_copy(
            self.c_own.at[self.s], self.c_buf.at[self.s, self.f], self.loc.at[0]
        )

    def c_start(self):
        @pl.when(self.inside)
        def _():
            self.c_copy().start()
            self.to_fsdp(self.c_own.at[self.s], self.c_buf.at[self.s, self.f], 0)

    def c_part(self, n):
        return self.c_buf.at[n, pl.ds(16 * self.g, 16)]

    def c_share(self):
        @pl.when(self.inside)
        def _():
            self.c_copy().wait()
            many = self.c_buf.at[self.s, pl.ds(16 * self.g, 15)]
            remote(many, many, self.z_send.at[0], self.z_recv.at[0], self.core).wait_recv()

        @pl.when(jnp.logical_not(self.inside))
        def _():
            many = self.c_part(self.s)
            remote(many, many, self.z_send.at[0], self.z_recv.at[0], self.core).wait_recv()

        for d in range(1, NS):
            self.share_copy(0, d, self.c_part(self.s)).start()

    def share_copy(self, k, d, block):
        return remote(
            block, block, self.sh_send.at[k, d - 1], self.sh_recv.at[k, d - 1],
            {"slab": lax.rem(self.s + d, NS)},
        )

    def core_copy(self, k, block):
        return remote(block, block, self.fw_send.at[k], self.fw_recv.at[k], self.core)

    def c_core(self):
        for d in range(1, NS):
            self.share_copy(0, d, self.c_part(lax.rem(self.s + NS - d, NS))).wait_recv()
        self.core_copy(0, self.c_buf.at[:, pl.ds(16 * self.g, 16)]).start()

    def c_done(self):
        self.core_copy(0, self.c_buf.at[:, pl.ds(16 - 16 * self.g, 16)]).wait_recv()

    def p_copy(self):
        return pltpu.make_async_copy(
            self.p_own.at[self.w], self.p_buf.at[self.w, self.f], self.loc.at[1]
        )

    def p_start(self):
        self.p_copy().start()
        self.to_fsdp(self.p_own.at[self.w], self.p_buf.at[self.w, self.f], 1)

    def p_ready(self):
        many = self.p_buf.at[self.w, pl.ds(0, NF - 1)]
        remote(many, many, self.z_send.at[1], self.z_recv.at[1], self.core).wait_recv()
        self.p_copy().wait()

    def p_share(self, *pieces):
        for d in pieces:
            self.share_copy(1, d, self.p_buf.at[self.w]).start()

    def p_core(self):
        for d in range(1, NS):
            block = self.p_buf.at[self.g * NS + lax.rem(self.s + NS - d, NS)]
            self.share_copy(1, d, block).wait_recv()
        self.core_copy(1, self.p_buf.at[pl.ds(self.g * NS, NS)]).start()

    def p_done(self):
        self.core_copy(1, self.p_buf.at[pl.ds((1 - self.g) * NS, NS)]).wait_recv()

    def view(self, kind, z):
        return self.bufs[kind].at[self.g, lax.rem(z, NZ)]

    def own(self, kind):
        dest = self.view(kind, self.z)
        dest = dest.at[self.half] if kind == 0 else dest
        return pltpu.make_async_copy(self.owns[kind], dest, self.loc.at[2 + kind])

    def pair(self):
        return remote(
            self.owns[0], self.bufs[0].at[self.g, self.z, self.half],
            self.pair_sem.at[0], self.pair_sem.at[1], {"fsdp": self.z * 2 + 1 - self.half},
        )

    def start(self):
        self.pair().start()
        self.own(0).start()
        self.own(1).start()

    def step(self, kind, step, way):
        sign = NZ - 1 if way == 0 else 1
        block = self.view(kind, self.z + sign * step)
        hop = 1 if way == 0 else NZ - 1
        target = {"fsdp": lax.rem(self.z + hop, NZ) * 2 + self.half}
        slot = way * 8 + step
        return remote(
            block, block, self.ring_send.at[kind, slot], self.ring_recv.at[kind, slot], target
        )

    def share(self, kind, z):
        block = self.view(kind, z)
        remote(block, block, self.core_sem.at[kind, 0], self.core_sem.at[kind, 1], self.core).start()

    def pump(self, kind, step):
        steps = (NZ // 2, NZ // 2 - 1)
        if step == 0:
            self.own(kind).wait()
            if kind == 0:
                self.pair().wait_recv()
        for way in (0, 1):
            if 0 < step <= steps[way]:
                self.step(kind, step - 1, way).wait_recv()
            if step < steps[way]:
                self.step(kind, step, way).start()
        if step == 0:
            self.share(kind, self.z)
        for way in (0, 1):
            if 0 < step <= steps[way]:
                self.share(kind, self.z + (NZ - step if way == 0 else step))

    def landed(self, kind):
        theirs = self.bufs[kind].at[1 - self.g]
        remote(
            theirs, theirs, self.core_sem.at[kind, 0], self.core_sem.at[kind, 1], self.core
        ).wait_recv()

    def finish(self):
        for kind in range(2):
            mine = self.bufs[kind].at[self.g]
            remote(
                mine, mine, self.core_sem.at[kind, 0], self.core_sem.at[kind, 1], self.core
            ).wait_send()
            for way, steps in ((0, NZ // 2), (1, NZ // 2 - 1)):
                for step in range(steps):
                    self.step(kind, step, way).wait_send()
        self.pair().wait_send()

        @pl.when(self.inside)
        def _():
            many = self.c_buf.at[self.s, pl.ds(0, NF - 1)]
            remote(many, many, self.z_send.at[0], self.z_recv.at[0], self.core).wait_send()

        many = self.p_buf.at[self.w, pl.ds(0, NF - 1)]
        remote(many, many, self.z_send.at[1], self.z_recv.at[1], self.core).wait_send()
        for d in range(1, NS):
            self.share_copy(0, d, self.c_part(self.s)).wait_send()
            self.share_copy(1, d, self.p_buf.at[self.w]).wait_send()
        self.core_copy(0, self.c_buf.at[:, pl.ds(16 * self.g, 16)]).wait_send()
        self.core_copy(1, self.p_buf.at[pl.ds(self.g * NS, NS)]).wait_send()


def greet(targets):
    barrier = pltpu.get_barrier_semaphore()
    for target in targets:
        pl.semaphore_signal(barrier, inc=1, device_id=target, device_id_type=MESH)


def greeted(targets):
    pl.semaphore_wait(pltpu.get_barrier_semaphore(), len(targets))


def block_targets(g, s):
    found = []
    for d in range(1, 2 * NS):
        other_g = lax.rem(g + d // NS, 2)
        other_s = lax.rem(s + d % NS, NS)
        found.append((other_g * NS + other_s, {"grp": other_g, "slab": other_s}))
    return found


def pair_targets(f, s):
    z, half = f // 2, lax.rem(f, 2)
    found = []
    for h in range(2):
        there = z * 2 + lax.rem(half + h, 2)
        for d in range(NS):
            if h or d:
                found.append((h * NS + d - 1, {"fsdp": there, "slab": lax.rem(s + d, NS)}))
    return found


def all_targets():
    f, g, s = lax.axis_index("fsdp"), lax.axis_index("grp"), lax.axis_index("slab")
    return (
        [target for _, target in block_targets(g, s)]
        + [{"fsdp": lax.rem(f + d, NF)} for d in range(1, NF)]
        + [target for _, target in pair_targets(f, s)[NS:]]
    )


def reduce_gradient(mine, landed, terms, arrived, collected, sems):
    a_send, a_recv, b_send, b_recv, c_send, c_recv = sems
    f, g, s = lax.axis_index("fsdp"), lax.axis_index("grp"), lax.axis_index("slab")
    w = g * NS + s
    block = block_targets(g, s)
    copies = []
    for d, (index, target) in enumerate(block):
        copy = remote(mine.at[index], landed.at[w], a_send.at[d], a_recv.at[d], target)
        copy.start()
        copies.append(copy)
    landed[w] = mine[w]
    for copy in copies:
        copy.wait()
    total = landed[0].astype(F32)
    for index in range(1, 2 * NS):
        total = total + landed[index].astype(F32)
    for index in range(NF):
        rows, lanes = 4 * (index // 8), 96 * (index % 8)
        terms[index, :, 0:96] = total[rows : rows + 4, lanes : lanes + 96]
        terms[index, :, 96:128] = jnp.zeros((4, 32), F32)
    copies = []
    for d in range(1, NF):
        p = lax.rem(f + d, NF)
        copy = remote(terms.at[p], arrived.at[f], b_send.at[d - 1], b_recv.at[d - 1], {"fsdp": p})
        copy.start()
        copies.append(copy)
    arrived[f] = terms[f]
    for copy in copies:
        copy.wait()
    collected[w] = jnp.sum(arrived[...], axis=0)
    copies = []
    for d, (index, target) in enumerate(block):
        copy = remote(collected.at[w], collected.at[w], c_send.at[d], c_recv.at[d], target)
        copy.start()
        copies.append(copy)
    for copy in copies:
        copy.wait()


def pack_tiles(
    g, s, proj_in, conv_in, head_in, patch_in, attn_in, back_in, up_in, bias_in, down_in,
    vit_in, patch_perm, wide_w, back_perm, tail_perm, fill, c_own, p_own, a_own, b_own,
):
    choose = (iota((96, 96), 0) == iota((96, 96), 1)).astype(BF16)
    proj = nt(choose, proj_in[...])
    proj = jnp.concatenate([proj[0:48], proj[48:96]], axis=1).astype(BF16)
    for n in range(3):
        c_own[n] = proj[16 * n : 16 * n + 16]
    c_own[3] = conv_in[:, 0:128]
    c_own[4] = head_in[:, 0:128]
    c_own[5] = (
        nn(conv_in[:, 128:144], tail_perm[0:16, :]) + nn(head_in[:, 128:192], tail_perm[16:80, :])
    ).astype(BF16)
    patch = nn(patch_in[...], patch_perm[...])
    patch = jnp.concatenate([patch, jnp.zeros((8, 640), F32)], axis=0).astype(BF16)
    for u in range(5):
        for rb in range(3):
            n = 3 * u + rb
            block = patch[16 * rb : 16 * rb + 16, 128 * u : 128 * u + 128]
            if n < 2:
                c_own[6 + n] = block
            else:
                p_own[n - 2] = block
    for n in range(13, 16):
        p_own[n] = jnp.zeros((16, 128), BF16)

    def tall(rows, lanes):
        values = rows.astype(F32)
        more = lanes - values.shape[1]
        if more:
            values = jnp.concatenate([values, jnp.zeros((40, more), F32)], axis=1)
        return jnp.concatenate([values, jnp.zeros((8, lanes), F32)], axis=0)

    attn = tall(attn_in[...], 512)
    back = tall(nn(back_in[...], back_perm[...]), 256)
    vit = tall(vit_in[:, pl.ds(pl.multiple_of(128 * s, 128), 128)], 128)
    tiles = [attn[:, 128 * u : 128 * u + 128] for u in range(4)] + [back[:, 0:128], back[:, 128:256]]
    for u in range(3):
        a_own[48 * u : 48 * u + 48, :] = jnp.where(g == 0, tiles[u], tiles[3 + u]).astype(BF16)
    last = jnp.concatenate([vit[32:48], jnp.zeros((16, 128), F32)], axis=0)
    a_own[144:176, :] = jnp.where(g == 0, vit[0:32], last).astype(BF16)
    fill[0:20, :] = up_in[...].astype(F32)
    fill[20:40, :] = down_in[...].astype(F32)
    fill[40:48, :] = jnp.zeros((8, WIDTH), F32)
    values = fill[...].astype(BF16)
    wide = jnp.concatenate([nn(values[:, 0:640], wide_w[...]), nn(values[:, 640:1280], wide_w[...])], axis=1)
    bias = jnp.where(
        iota((48, 20), 0) == iota((48, 20), 1), jnp.broadcast_to(bias_in[...].astype(F32), (48, 20)), 0.0
    )
    bias = jnp.sum(bias, axis=1, keepdims=True)
    wide = jnp.where(iota((48, WIDE), 1) == 40, bias, wide)
    wide = jnp.where(g == 0, wide[:, 0:768], wide[:, 768:1536]).astype(BF16)
    for u in range(6):
        b_own[u] = wide[:, 128 * u : 128 * u + 128]


def step_kernel(
    fetch, hidden, shards, mods, noisy, sigma_ref, flat, gain_in, shift_in, position_in, text,
    perm, perm_t, inter, columns_w, rows_w, ph0, ph1, lane_rows, patch_perm, wide_w, back_perm, tail_perm,
    grad_out, score_out,
    hid, mod, c_own, p_own, a_own, b_own, c_buf, p_buf, a_buf, b_buf, vecs, fill,
    proj_full, ext, halo_out, halo_in, nrm, dnrm, acc, stat_out, stat_in,
    cols_buf, pix, head_t, head_p, edge_out, edge_in, kd_out, kd_in, dirs, u_out, u_in,
    ao_out, ao_in, row_out, row_in, text_in, emb_out, emb_in, vd_out, vd_in, rim_out, rim_in, gsplit, mine, landed,
    terms, arrived, collected,
    x_send, x_recv, hid_sem, *sems,
):
    s = lax.axis_index("slab")
    f = lax.axis_index("fsdp")
    half = lax.rem(f, 2)
    low, high = s > 0, s < NS - 1
    low_f, high_f = jnp.where(low, 1.0, 0.0), jnp.where(high, 1.0, 0.0)
    before, after = {"slab": lax.rem(s + NS - 1, NS)}, {"slab": lax.rem(s + 1, NS)}
    hid_copy = pltpu.make_async_copy(hidden, hid, hid_sem.at[0])
    hid_copy.start()
    sigma = sigma_ref[0, 0]
    live = []

    def to_all(kind, source, dest, swap=False):
        copies = []
        for d in range(1, NS):
            p = lax.rem(s + d, NS)
            copies.append(
                remote(
                    source.at[p] if swap else source, dest.at[s],
                    x_send.at[kind, d - 1], x_recv.at[kind, d - 1], {"slab": p},
                )
            )
        for copy in copies:
            copy.start()
        live.extend(copies)
        return copies

    def to_sides(kind, source, dest):
        copies = [
            remote(source.at[0], dest.at[0], x_send.at[kind, 0], x_recv.at[kind, 0], after),
            remote(source.at[1], dest.at[1], x_send.at[kind, 1], x_recv.at[kind, 1], before),
        ]
        for copy in copies:
            copy.start()
        live.extend(copies)
        return copies

    def landed_all(copies):
        for copy in copies:
            copy.wait_recv()

    def flat_row(first, count):
        return jnp.concatenate([flat[k : k + 1, :] for k in range(first, first + count)], axis=1)

    targets = all_targets() if fetch else [target for _, target in pair_targets(f, s)]
    greet(targets)

    scale = 1.0 + mods[1:2].astype(F32)
    shift = mods[0:1].astype(F32)

    def modulate(lo, hi):
        def body(i, carry):
            rows = pl.ds(pl.multiple_of(i * 32, 32), 32)
            values = hid[rows, :].astype(F32)
            average = jnp.mean(values, axis=-1, keepdims=True)
            centered = values - average
            square = jnp.mean(centered * centered, axis=-1, keepdims=True)
            scaled = centered * (1.0 / jnp.sqrt(square + 1e-06))
            mod[rows, :] = (scaled * scale + shift).astype(BF16)
            return carry

        lax.fori_loop(lo, hi, body, 0)

    if fetch:
        weights = Weights(c_own, p_own, a_own, b_own, c_buf, p_buf, a_buf, b_buf, sems[:11])
        pack_tiles(
            weights.g, s, *shards, patch_perm, wide_w, back_perm, tail_perm, fill, c_own, p_own, a_own, b_own
        )
    else:
        weights = None
        for ref, given in zip((c_buf, p_buf, a_buf, b_buf), shards):
            ref[...] = given[...]
    hid_copy.wait()
    modulate(0, 8)
    greeted(targets)
    if fetch:
        weights.c_start()
        weights.start()
    words_copy = remote(
        text, text_in.at[half], x_send.at[12, 0], x_recv.at[12, 0], {"fsdp": f + 1 - 2 * half}
    )
    words_copy.start()
    live.append(words_copy)
    text_in[half] = text[...]

    def pump(*steps):
        if weights is not None:
            for kind, step in enumerate(steps):
                if step is not None:
                    weights.pump(kind, step)

    fill[0:1, :] = flat_row(14, 10)
    fill[1:5, :] = gain_in[...]
    fill[5:9, :] = shift_in[...]
    fill[9:10, :] = flat_row(24, 10)
    fill[10:11, :] = flat_row(34, 10)
    fill[11:16, :] = jnp.zeros((5, WIDTH), F32)
    fill[16:48, :] = position_in[...].astype(F32)
    for k in range(2):
        parts = jnp.concatenate(thirds(fill[:, 640 * k : 640 * k + 640]), axis=0)
        parts = nn(parts, wide_w[...])
        vecs[:, 768 * k : 768 * k + 768] = parts[0:48] + (parts[48:96] + parts[96:144])
    modulate(8, 16)
    if weights is not None:
        weights.c_share()
        pump(0, 0)
        weights.p_start()
        pump(1)
        weights.c_core()
        pump(2, 1)
        weights.c_done()

    def patch_unit(u):
        parts = []
        for rb in range(3):
            n = 3 * u + rb
            parts.append(c_buf[6 + n] if n < 2 else p_buf[n - 2])
        return jnp.concatenate(parts, axis=1).reshape(WIDE, 128)

    def a_unit(index):
        k = index % 3
        return a_buf[index // 3, :, :, 48 * k : 48 * k + 48].reshape(WIDE, 128)

    for n in range(3):
        both = c_buf[n].reshape(512, 128).astype(F32)
        turned = pltpu.roll(both, 64, 1).astype(BF16)
        for k in range(NF):
            at = 96 * k + 16 * n
            proj_full[at : at + 16, :] = c_buf[n, k]
            proj_full[at + 48 : at + 64, :] = turned[16 * k : 16 * k + 16]
    velocity = nn(mod[...], proj_full[...])[:, :64] + flat[13:14, 0:64]
    pump(3)
    clean = noisy[...].astype(F32) - sigma * velocity
    lat_tok = (clean / LAT_SCALE + LAT_SHIFT).astype(BF16)
    tok_t = nt(perm_t[...], lat_tok)
    stacked = jnp.concatenate(
        [
            jnp.concatenate(
                [tok_t[0:32, 128 * k : 128 * k + 128], tok_t[32:64, 128 * k : 128 * k + 128]], axis=1
            )
            for k in range(4)
        ],
        axis=0,
    ).astype(BF16)
    latent = nn(stacked, inter[...]).astype(BF16)
    for k in range(4):
        for i2 in range(2):
            for p in range(2):
                r = 4 * k + 2 * i2 + p + 1
                for b in range(3):
                    at = (i2 * 3 + b) * 128
                    ext[16 * b : 16 * b + 16, 128 * r : 128 * r + 128] = latent[
                        32 * k + 16 * p : 32 * k + 16 * p + 16, at : at + 128
                    ]
    halo_out[0] = ext[:, 2048:2176]
    halo_out[1] = ext[:, 128:256]
    copies = to_sides(0, halo_out, halo_in)
    same = (iota((512, 512), 0) // 16 == iota((512, 512), 1) // 16).astype(BF16)

    def columns_of(rows):
        width = rows.shape[1]
        return jnp.transpose(jnp.concatenate([rows, jnp.zeros((120, width), F32)], axis=0))

    chan = jnp.concatenate(
        [flat_row(0, 4), flat_row(4, 4), flat_row(8, 4), jnp.zeros((5, 512), F32)], axis=0
    )
    chan_cols = columns_of(chan)
    conv_bias, gain, gshift = chan_cols[:, 0:1], chan_cols[:, 1:2], chan_cols[:, 2:3]
    eye = (iota((128, 128), 0) == iota((128, 128), 1)).astype(BF16)
    conv0 = c_buf[3].reshape(512, 128)
    head0 = c_buf[4].reshape(512, 128)
    tail = c_buf[5].reshape(512, 128)
    head_p[...] = (nn(head0, ph0[...]) + nn(tail, ph1[...])).astype(BF16)
    head_t[...] = (
        lax.dot_general(ph0[...], head0, (((0,), (1,)), ((), ())), preferred_element_type=F32)
        + lax.dot_general(ph1[...], tail, (((0,), (1,)), ((), ())), preferred_element_type=F32)
    ).astype(BF16)
    bias_row = nn(jnp.broadcast_to(flat[12:13, :], (8, 128)), ph0[...].astype(F32), HIGH) + nn(
        jnp.broadcast_to(flat[44:45, :], (8, 128)), ph1[...].astype(F32), HIGH
    )
    head_col = columns_of(bias_row)[:, 0:1]
    pump(4, 2)
    if weights is not None:
        weights.p_ready()
    landed_all(copies)
    if weights is not None:
        weights.p_share(1, 2, 3)
    ext[:, 0:128] = (halo_in[0].astype(F32) * low_f).astype(BF16)
    ext[:, 2176:2304] = (halo_in[1].astype(F32) * high_f).astype(BF16)
    acc[...] = jnp.zeros_like(acc)

    def conv_chunk(i, carry):
        at = pl.multiple_of(i * 256, 256)
        parts = [ext[:, pl.ds(pl.multiple_of(at + 128 * a, 128), 256)] for a in range(3)]
        columns = jnp.concatenate(parts + [jnp.zeros((112, 256), BF16)], axis=0)
        out = nn(conv0, columns[0:128]) + nn(tail, columns[128:256]) + conv_bias
        nrm[:, pl.ds(at, 256)] = out
        acc[0] += out[:, 0:128] + out[:, 128:256]
        square = out * out
        acc[1] += square[:, 0:128] + square[:, 128:256]
        return carry

    lax.fori_loop(0, 8, conv_chunk, 0)

    def group_totals(kind, step=None):
        ones = jnp.ones((8, 128), BF16)
        first, second = [
            nt(ones, part[0]) + (nt(ones, part[1]) + nt(ones, part[2]))
            for part in (thirds(acc[0]), thirds(acc[1]))
        ]
        k = kind - 1
        stat_out[k] = jnp.concatenate([first[0:1], second[0:1]], axis=0)
        copies = to_all(kind, stat_out.at[k], stat_in.at[k])
        stat_in[k, s] = stat_out[k]
        if step is not None:
            pump(*step)
        landed_all(copies)
        total = stat_in[k, 0]
        for index in range(1, NS):
            total = total + stat_in[k, index]
        total = jnp.concatenate([total, jnp.zeros((6, 512), F32)], axis=0)
        sums = nn(jnp.concatenate(thirds(total), axis=0), same)
        columns = columns_of(sums[0:8] + (sums[8:16] + sums[16:24]))
        return columns[:, 0:1] * (1.0 / CELLS), columns[:, 1:2] * (1.0 / CELLS)

    average, square = group_totals(1, (5, 3))
    inverse = 1.0 / jnp.sqrt(square - average * average + 1e-06)
    if weights is not None:
        weights.p_share(4, 5, 6, 7)

    def head_chunk(i, carry):
        at = pl.multiple_of(i * 256, 256)
        normed = (nrm[:, pl.ds(at, 256)] - average) * inverse
        nrm[:, pl.ds(at, 256)] = normed
        gained = normed * gain + gshift
        active = (gained * (1.0 / (1.0 + jnp.exp(-gained)))).astype(BF16)
        cells = (nn(head_t[...], active) + head_col).astype(BF16)
        for rr in range(2):
            rows = pl.ds(pl.multiple_of(i * 64 + 32 * rr, 32), 32)
            for x in range(8):
                pix[rows, 128 * x : 128 * x + 128] = cells[
                    32 * x : 32 * x + 32, 128 * rr : 128 * rr + 128
                ]
        return carry

    lax.fori_loop(0, 4, head_chunk, 0)
    pump(6, 4)
    lax.fori_loop(4, 8, head_chunk, 0)
    pump(7, 5)
    narrow = nt(columns_w[...], pix[...]).astype(BF16)
    raw = jnp.zeros((80, 512), F32)
    for m in range(3):
        raw = raw + nn(narrow[128 * m : 128 * m + 80], rows_w[512 * m : 512 * m + 512, :])
    edge_out[0, 0] = raw[:, 256:384]
    edge_out[0, 1] = raw[:, 384:512]
    copies = to_sides(2 + 1, edge_out.at[0], edge_in.at[0])
    pump(8, 6)
    if weights is not None:
        weights.p_core()
        weights.landed(0)
    lane = iota((1, WIDE), 1)
    mask = (lax.rem(lane, 48) < 40).astype(F32)
    gains = [vecs[1 + i : 2 + i, :] for i in range(4)]
    shifts = [vecs[5 + i : 6 + i, :] for i in range(4)]
    class_hat, _ = norm_stats(vecs[0:1, :], mask, 1e-05)
    class_pre = class_hat * gains[0] + shifts[0]
    class_hat, _ = norm_stats(class_pre, mask, 1e-05)
    class_unit = jnp.broadcast_to(class_hat * gains[1] + shifts[1], (8, WIDE)).astype(BF16)
    attn = [a_unit(i) for i in range(4)]
    class_qkv = jnp.concatenate([nn(class_unit, attn[i]) for i in range(4)], axis=1)
    class_qkv = class_qkv.astype(BF16).astype(F32)
    place512 = iota((8, 512), 1)
    row512 = iota((8, 512), 0)
    start = jnp.where(row512 == 0, 0, 240)
    in_head = row512 < 2
    key_at = in_head & (place512 >= start + 80) & (place512 < start + 160)
    val_at = in_head & (place512 >= start + 160) & (place512 < start + 240)
    query = jnp.where(key_at, pltpu.roll(class_qkv, 80, 1), 0.0)
    class_exp = jnp.exp(jnp.sum(query * class_qkv, axis=-1, keepdims=True) / ROOT)
    query_b = query.astype(BF16)
    key_dir = nt(query_b[:, 0:128], attn[0])
    for i in range(1, 4):
        key_dir = key_dir + nt(query_b[:, 128 * i : 128 * i + 128], attn[i])
    kd_out[...] = key_dir[0:2]
    kd_copies = to_all(4, kd_out, kd_in)
    kd_in[s] = key_dir[0:2]
    corr0 = jnp.where(low, 1.0, lane_rows[0:1, :])
    corr1 = jnp.where(high, 1.0, lane_rows[1:2, :])
    img_scale, img_shift = lane_rows[2:3, :], lane_rows[3:4, :]
    if weights is not None:
        weights.p_done()
    landed_all(copies)
    top = (raw[:, 0:128] * corr0 + edge_in[0, 0] * low_f) * img_scale + img_shift
    bottom = (raw[:, 128:256] * corr1 + edge_in[0, 1] * high_f) * img_scale + img_shift
    patches = jnp.concatenate(
        [
            jnp.concatenate([part[16 * u : 16 * u + 16] for u in range(5)], axis=1)
            for part in (top, bottom)
        ],
        axis=0,
    ).astype(BF16)
    embedded = vecs[16:48, :]
    for u in range(5):
        embedded = embedded + nt(patches[:, 128 * u : 128 * u + 128], patch_unit(u))
    hat0, inv0 = norm_stats(embedded, mask, 1e-05)
    hat1, inv1 = norm_stats(hat0 * gains[0] + shifts[0], mask, 1e-05)
    unit = hat1 * gains[1] + shifts[1]
    unit_b = unit.astype(BF16)
    unit = unit_b.astype(F32)
    pump(None, 7)
    landed_all(kd_copies)
    for index in range(NS):
        dirs[2 * index : 2 * index + 2, :] = kd_in[index]
    token_exp = jnp.exp(nt(dirs[0:16, :], unit, HIGH) / ROOT)
    gathered = nn(token_exp, unit, HIGH)
    gathered = jnp.where(lane == 40, jnp.sum(token_exp, axis=1, keepdims=True), gathered)
    for index in range(NS):
        u_out[index] = gathered[2 * index : 2 * index + 2]
    copies = to_all(5, u_out, u_in, swap=True)
    u_in[s] = u_out[s]
    pump(None, 8)
    landed_all(copies)
    total = u_in[0]
    for index in range(1, NS):
        total = total + u_in[index]
    denominator = class_exp[0:2] + total[:, 40:41]
    mixed = halves(jnp.concatenate([total[0:2], jnp.zeros((6, WIDE), F32)], axis=0))
    first = nn(mixed[0], attn[1]) + nn(mixed[1], attn[1])
    second = nn(mixed[0], attn[3]) + nn(mixed[1], attn[3])
    heads1 = jnp.where(val_at[0:1, 128:256], first[0:1] + class_exp[0:1] * class_qkv[0:1, 128:256], 0.0)
    heads3 = jnp.where(val_at[1:2, 384:512], second[1:2] + class_exp[1:2] * class_qkv[0:1, 384:512], 0.0)
    heads1 = heads1 / denominator[0:1]
    heads3 = heads3 / denominator[1:2]
    rows1 = a_unit(4)
    rows3 = a_unit(5)

    def wide8(row):
        if row.shape[0] == 1:
            return jnp.broadcast_to(row, (8, row.shape[1])).astype(BF16)
        return jnp.concatenate([row, jnp.zeros((6, row.shape[1]), F32)], axis=0).astype(BF16)

    def mine_of(rows):
        return jnp.where(half == 0, rows[0:1], rows[1:2])

    attn_part = nt(wide8(heads1), rows1) + nt(wide8(heads3), rows3)

    def pair_sum(kind, k, rows):
        row_out[k] = rows[0:2]
        copies = [
            remote(
                row_out.at[k], row_in.at[k, half, s], x_send.at[kind, index], x_recv.at[kind, index],
                target,
            )
            for index, target in pair_targets(f, s)
        ]
        for copy in copies:
            copy.start()
        live.extend(copies)
        row_in[k, half, s] = row_out[k]
        landed_all(copies)
        sums = []
        for h in range(2):
            total = row_in[k, h, 0]
            for index in range(1, NS):
                total = total + row_in[k, h, index]
            sums.append(total)
        return sums

    ao_out[...] = attn_part[0:1]
    copies = [
        remote(ao_out, ao_in.at[half, s], x_send.at[6, index], x_recv.at[6, index], target)
        for index, target in pair_targets(f, s)
    ]
    for copy in copies:
        copy.start()
    live.extend(copies)
    ao_in[half, s] = attn_part[0:1]
    landed_all(copies)
    sums = []
    for h in range(2):
        total = ao_in[h, 0]
        for index in range(1, NS):
            total = total + ao_in[h, index]
        sums.append(total)
    block_mid = class_pre + jnp.concatenate(sums, axis=0) + vecs[9:10, :]
    hat2, inv2 = norm_stats(block_mid, mask, 1e-05)
    mlp_input = hat2 * gains[2] + shifts[2]
    mlp_input = wide8(jnp.where(lane == 40, 1.0, mlp_input))
    if weights is not None:
        weights.landed(1)
    hidden_units = [b_buf[i // 6, :, i % 6].reshape(WIDE // 2, 128) for i in range(12)]
    unit_at = lax.rem(iota((1, WIDE // 2), 1), 48) < 20
    preact = nt(mlp_input[:, 0:128], hidden_units[0])
    for i in range(1, 12):
        preact = preact + nt(mlp_input[:, 128 * i : 128 * i + 128], hidden_units[i])
    preact = jnp.where(unit_at, preact, 0.0)
    cdf = 0.5 * (1.0 + lax.erf(preact * 0.7071067811865476))
    active = preact * cdf
    active = pltpu.roll(active, 20, 1).astype(BF16)
    mlp_part = jnp.concatenate([nn(active, hidden_units[i]) for i in range(12)], axis=1)
    sums = pair_sum(7, 1, mlp_part)
    block_out = block_mid + (sums[0] + sums[1]) + vecs[10:11, :]
    hat3, inv3 = norm_stats(block_out, mask, 1e-05)
    post = wide8(hat3 * gains[3] + shifts[3])
    vit = jnp.concatenate([a_buf[0, :, :, 144:176], a_buf[1, :, :, 144:160]], axis=2).reshape(WIDE, 128)
    embed = nn(post, vit)[0:2]
    words_copy.wait_recv()
    words = jnp.concatenate([text_in[0], text_in[1]], axis=0)
    own_words = jnp.concatenate(
        [text_in[k, :, pl.ds(pl.multiple_of(128 * s, 128), 128)] for k in range(2)], axis=0
    )
    four = jnp.concatenate([own_words, embed], axis=0)
    exact = four.astype(BF16).astype(F32)
    eight = nt(jnp.concatenate([exact, four - exact], axis=0).astype(BF16), vit)
    four = eight[0:4] + eight[4:8]
    dots = jnp.sum(embed * own_words, axis=-1, keepdims=True)
    squares = jnp.sum(embed * embed, axis=-1, keepdims=True)
    emb_out[0:2, :] = four[0:2]
    emb_out[2:4, :] = jnp.where(lane == 40, dots, jnp.where(lane == 41, squares, four[2:4]))
    copies = to_all(13, emb_out, emb_in)
    emb_in[s] = emb_out[...]
    landed_all(copies)
    total = emb_in[0]
    for index in range(1, NS):
        total = total + emb_in[index]
    dots, size_e = total[2:4, 40:41], total[2:4, 41:42] + 1e-06
    size_t = jnp.sum(words * words, axis=-1, keepdims=True) + 1e-06
    sizes = jnp.sqrt(size_e) * jnp.sqrt(size_t)
    score = 100.0 * dots / sizes
    score_out[...] = jnp.broadcast_to(mine_of(score), (8, 128))
    d_post = (-1.0 / 64.0) * ((100.0 / sizes) * total[0:2] - (score / size_e) * total[2:4])
    d_second = norm_back(d_post[0:2], hat3, inv3, gains[3])
    d_second_b = wide8(d_second)
    d_active = nt(d_second_b[:, 0:128], hidden_units[0])
    for i in range(1, 12):
        d_active = d_active + nt(d_second_b[:, 128 * i : 128 * i + 128], hidden_units[i])
    d_active = pltpu.roll(d_active, WIDE // 2 - 20, 1)
    slope = cdf + preact * jnp.exp(-0.5 * preact * preact) * 0.3989422804014327
    d_pre = jnp.where(unit_at, d_active * slope, 0.0).astype(BF16)
    input_part = jnp.concatenate([nn(d_pre, hidden_units[i]) for i in range(12)], axis=1)
    sums = pair_sum(8, 2, input_part)
    d_first = d_second + norm_back(sums[0] + sums[1], hat2, inv2, gains[2])
    d_first = wide8(mine_of(d_first))
    d_heads1 = nn(d_first, rows1).astype(BF16)
    d_heads3 = nn(d_first, rows3).astype(BF16)
    value0 = nt(jnp.where(val_at[0:1, 128:256], d_heads1.astype(F32), 0.0).astype(BF16), attn[1])
    value1 = nt(jnp.where(val_at[1:2, 384:512], d_heads3.astype(F32), 0.0).astype(BF16), attn[3])
    expect0 = jnp.sum(d_heads1[0:1].astype(F32) * heads1, axis=-1, keepdims=True)
    expect1 = jnp.sum(d_heads3[0:1].astype(F32) * heads3, axis=-1, keepdims=True)
    values = jnp.concatenate([value0[0:1], value1[0:1]], axis=0)
    expects = jnp.concatenate([expect0, expect1], axis=0)
    vd_out[...] = jnp.where(lane == 40, denominator, jnp.where(lane == 41, expects, values))
    copies = to_all(9, vd_out, vd_in)
    vd_in[s] = vd_out[...]
    token_logits = nt(unit, dirs[0:16, :], HIGH) / ROOT
    landed_all(copies)
    head_at = iota((1, 16), 1)
    denominators = jnp.zeros((1, 16), F32)
    expects = jnp.zeros((1, 16), F32)
    for index in range(NS):
        dirs[16 + 2 * index : 18 + 2 * index, :] = vd_in[index]
        for h in range(2):
            here = head_at == 2 * index + h
            denominators = jnp.where(here, vd_in[index, h : h + 1, 40:41], denominators)
            expects = jnp.where(here, vd_in[index, h : h + 1, 41:42], expects)
    token_weight = jnp.exp(token_logits) / denominators
    token_dots = nt(unit, dirs[16:32, :], HIGH)
    logit_grads = token_weight * (token_dots - expects)
    d_unit = nn(logit_grads / ROOT, dirs[0:16, :], HIGH) + nn(
        token_weight.astype(BF16).astype(F32), dirs[16:32, :], HIGH
    )
    d_pre_x = norm_back(d_unit, hat1, inv1, gains[1])
    d_embedded = norm_back(d_pre_x, hat0, inv0, gains[0]).astype(BF16)
    d_parts = [nn(d_embedded, patch_unit(u)) for u in range(5)]
    d_top = jnp.concatenate([part[0:16] for part in d_parts], axis=0) * img_scale
    d_bottom = jnp.concatenate([part[16:32] for part in d_parts], axis=0) * img_scale
    edge_out[1, 0] = d_bottom
    edge_out[1, 1] = d_top
    copies = to_sides(10, edge_out.at[1], edge_in.at[1])
    landed_all(copies)
    d_raw = jnp.concatenate(
        [
            jnp.concatenate(
                [d_top * corr0, d_bottom * corr1, edge_in[1, 1] * high_f, edge_in[1, 0] * low_f],
                axis=1,
            ),
            jnp.zeros((48, 512), F32),
        ],
        axis=0,
    ).astype(BF16)
    d_narrow = jnp.concatenate(
        [nt(rows_w[512 * m : 512 * m + 512, :], d_raw) for m in range(3)], axis=1
    ).astype(BF16)
    for k in range(4):
        d_pix = nn(d_narrow, columns_w[:, 256 * k : 256 * k + 256]).astype(BF16)
        for x in range(2):
            rows = slice(64 * k + 32 * x, 64 * k + 32 * x + 32)
            for r in range(16):
                cols_buf[rows, 128 * r : 128 * r + 128] = d_pix[
                    32 * r : 32 * r + 32, 128 * x : 128 * x + 128
                ]
    acc[...] = jnp.zeros_like(acc)

    def head_back(i, carry):
        at = pl.multiple_of(i * 256, 256)
        grads = nn(head_p[...], cols_buf[:, pl.ds(at, 256)])
        normed = nrm[:, pl.ds(at, 256)]
        gained = normed * gain + gshift
        gate = 1.0 / (1.0 + jnp.exp(-gained))
        grads = grads * (gate * (1.0 + gained * (1.0 - gate))) * gain
        dnrm[:, pl.ds(at, 256)] = grads
        acc[0] += grads[:, 0:128] + grads[:, 128:256]
        both = grads * normed
        acc[1] += both[:, 0:128] + both[:, 128:256]
        return carry

    lax.fori_loop(0, 8, head_back, 0)
    conv0_t = nt(eye, conv0).astype(BF16)
    tail_t = nt(eye[0:16], tail).astype(BF16)
    mean0, mean1 = group_totals(2)

    def conv_back(i, carry):
        at = pl.multiple_of(i * 256, 256)
        grads = (dnrm[:, pl.ds(at, 256)] - mean0 - nrm[:, pl.ds(at, 256)] * mean1) * inverse
        grads = grads.astype(BF16)
        dnrm[0:128, pl.ds(at, 256)] = nn(conv0_t, grads)
        dnrm[128:144, pl.ds(at, 256)] = nn(tail_t, grads)
        return carry

    lax.fori_loop(0, 8, conv_back, 0)
    total = jnp.zeros((16, 2304), F32)
    column = lax.rem(iota((16, 2304), 1), 128)
    for b in range(3):
        part = jnp.zeros((16, 2304), F32)
        for a in range(3):
            t = 3 * a + b
            pieces = [dnrm[16 * t : 16 * t + 16, :]]
            if a:
                pieces = [jnp.zeros((16, 128 * a), F32)] + pieces
            if a < 2:
                pieces = pieces + [jnp.zeros((16, 256 - 128 * a), F32)]
            part = part + jnp.concatenate(pieces, axis=1)
        if b == 0:
            part = jnp.where(column < 127, pltpu.roll(part, 2303, 1), 0.0)
        if b == 2:
            part = jnp.where(column > 0, pltpu.roll(part, 1, 1), 0.0)
        total = total + part
    rim_out[0] = total[:, 2176:2304]
    rim_out[1] = total[:, 0:128]
    copies = to_sides(11, rim_out, rim_in)
    landed_all(copies)
    rows = [total[:, 128 * r + 128 : 128 * r + 256] for r in range(16)]
    rows[0] = rows[0] + rim_in[0] * low_f
    rows[15] = rows[15] + rim_in[1] * high_f
    rows = [-sigma * (row / LAT_SCALE) for row in rows]
    stacked = jnp.concatenate(
        [
            jnp.concatenate([rows[4 * k + p], rows[4 * k + 2 + p]], axis=1)
            for k in range(4)
            for p in range(2)
        ],
        axis=0,
    ).astype(BF16)
    centre = jnp.concatenate([inter[:, 128:256], inter[:, 512:640]], axis=1)
    tok = nt(stacked, centre)
    tok_t = jnp.concatenate(
        [
            jnp.concatenate(
                [tok[32 * k : 32 * k + 32, 128 * q : 128 * q + 128] for k in range(4)], axis=1
            )
            for q in range(2)
        ],
        axis=0,
    ).astype(BF16)
    d_vel = nn(perm[...], tok_t).astype(BF16)
    for quarter in range(4):
        part = nn(d_vel, mod[:, 768 * quarter : 768 * quarter + 768])
        for w in range(2 * NS):
            gsplit[w, 4 * quarter : 4 * quarter + 4] = part[4 * w : 4 * w + 4]
    for copy in live:
        copy.wait_send()
    if weights is not None:
        weights.finish()
        mine[...] = gsplit[...].astype(BF16)
        reduce_gradient(mine, landed, terms, arrived, collected, sems[11:])
        whole = jnp.concatenate([collected[w] for w in range(2 * NS)], axis=0)
        grad_out[...] = jnp.transpose(whole)[0:96, :]
    else:
        grad_out[...] = gsplit[...]


def resize_table(out_count, in_count):
    stretch = in_count / out_count
    centers = (np.arange(out_count) + 0.5) * stretch
    places = np.arange(in_count) + 0.5
    weights = np.maximum(0.0, 1.0 - np.abs(places[None, :] - centers[:, None]) / stretch)
    return weights / weights.sum(axis=1, keepdims=True)


def constants():
    perm = np.zeros((64, 64))
    for c in range(16):
        for p in range(2):
            for q in range(2):
                perm[4 * c + 2 * p + q, q * 32 + p * 16 + c] = 1
    inter = np.zeros((2, 2, 64, 2, 3, 128))
    for q in range(2):
        for i2 in range(2):
            for j in range(64):
                for b in range(3):
                    at = 2 * j + q - b + 1
                    if 0 <= at < 128:
                        inter[q, i2, j, i2, b, at] = 1
    table = resize_table(224, 1024)
    columns = np.zeros((3, 8, 16, 8, 128))
    for m in range(3):
        for u in range(5):
            if 3 * u + m < 14:
                for pc in range(16):
                    columns[m, u, pc] = table[14 * pc + 3 * u + m].reshape(128, 8).T
    rows = np.zeros((3, 16, 4, 8, 4, 128))
    local = table[28 * 3 : 28 * 3 + 28, 128 * 3 : 128 * 3 + 128].reshape(28, 16, 8)
    to_next = table[28 * 4, 128 * 3 : 128 * 3 + 128].reshape(16, 8)
    to_prev = table[28 * 3 - 1, 128 * 3 : 128 * 3 + 128].reshape(16, 8)
    for m in range(3):
        for c in range(3):
            for a in range(14):
                at = 42 * m + 14 * c + a
                rows[m, :, c, :, 0, at] = local[a]
                rows[m, :, c, :, 1, at] = local[14 + a]
            rows[m, :, c, :, 2, 42 * m + 14 * c] = to_next
            rows[m, :, c, :, 3, 42 * m + 14 * c + 13] = to_prev
    lanes = np.zeros((8, 128))
    lanes[0:2] = 1
    for m in range(3):
        for c in range(3):
            for a in range(14):
                at = 42 * m + 14 * c + a
                lanes[2, at] = 0.5 / PIX_STD[c]
                lanes[3, at] = (0.5 - PIX_MEAN[c]) / PIX_STD[c]
            lanes[0, 42 * m + 14 * c] = table[0, 0] / table[28, 128]
            lanes[1, 42 * m + 14 * c + 13] = table[223, 1023] / table[27, 127]
    ph = np.zeros((2, 128, 8, 32))
    for c in range(3):
        for y in range(8):
            for x in range(8):
                k = 64 * c + 8 * y + x
                if k < 128:
                    ph[0, k, x, 8 * c + y] = 1
                else:
                    ph[1, 16 + k - 128, x, 8 * c + y] = 1
    one = lambda v: jnp.asarray(v.astype(jnp.bfloat16))
    ph = ph.reshape(2, 128, 256)
    order = np.zeros((3, 14, 14, 640))
    for c in range(3):
        for a in range(14):
            for b in range(14):
                order[c, a, b, 128 * (b // 3) + 42 * (b % 3) + 14 * c + a] = 1
    back = np.zeros((160, 256))
    back[np.arange(80), 32 + np.arange(80)] = 1
    back[80 + np.arange(80), 128 + 16 + np.arange(80)] = 1
    tail = np.zeros((80, 128))
    tail[np.arange(80), np.arange(80)] = 1
    wide = np.zeros((16, 40, 16, 48))
    for k in range(16):
        wide[k, np.arange(40), k, np.arange(40)] = 1
    return (
        one(perm), one(perm.T), one(inter.reshape(256, 768)),
        one(columns.reshape(384, 1024)), one(rows.reshape(1536, 512)),
        one(ph[0]), one(ph[1]), jnp.asarray(lanes.astype(np.float32)),
        one(order.reshape(588, 640)), one(wide.reshape(640, 768)), one(back), one(tail),
    )


def raw_shards(proj, conv, head, patch, attn_in, attn_out, mlp_in, mlp_bias, mlp_out, vit):
    conv_t = conv.reshape(144, 16).T
    return (
        proj.T, conv_t, head, patch.T, attn_in, attn_out.T, mlp_in.T, mlp_bias[None], mlp_out, vit
    )


def run_step(shards, fetch, grad_shape, hidden, sigma, small, consts):
    vm, dma = pltpu.VMEM, pltpu.SemaphoreType.DMA
    scratch = [
        vm((512, 3072), BF16), vm((512, 3072), BF16),
        vm((8, 16, 128), BF16), vm((16, 16, 128), BF16), vm((176, 128), BF16), vm((6, 48, 128), BF16),
        vm((8, NF, 16, 128), BF16), vm((16, NF, 16, 128), BF16),
        vm((2, NZ, 2, 176, 128), BF16), vm((2, NZ, 6, 48, 128), BF16),
        vm((48, WIDE), F32), vm((48, WIDTH), F32),
        vm((3072, 128), BF16), vm((48, 2304), BF16), vm((2, 48, 128), BF16), vm((2, 48, 128), BF16),
        vm((512, LANES), F32), vm((512, LANES), F32), vm((2, 512, 128), F32),
        vm((2, 2, 512), F32), vm((2, NS, 2, 512), F32),
        vm((256, LANES), BF16), vm((512, 1024), BF16), vm((256, 512), BF16), vm((512, 256), BF16),
        vm((2, 2, 80, 128), F32), vm((2, 2, 80, 128), F32),
        vm((2, WIDE), F32), vm((NS, 2, WIDE), F32), vm((32, WIDE), F32),
        vm((NS, 2, WIDE), F32), vm((NS, 2, WIDE), F32),
        vm((1, WIDE), F32), vm((2, NS, 1, WIDE), F32),
        vm((3, 2, WIDE), F32), vm((3, 2, NS, 2, WIDE), F32), vm((2, 1, 1024), F32),
        vm((4, WIDE), F32), vm((NS, 4, WIDE), F32),
        vm((2, WIDE), F32), vm((NS, 2, WIDE), F32),
        vm((2, 16, 128), F32), vm((2, 16, 128), F32),
        vm((16, 16, 768), F32), vm((16, 16, 768), BF16), vm((16, 16, 768), BF16),
        vm((NF, 4, 128), F32), vm((NF, 4, 128), F32), vm((16, 4, 128), F32),
        dma((14, 15)), dma((14, 15)), dma((1,)),
        dma((2,)), dma((2,)), dma((2, NS - 1)), dma((2, NS - 1)), dma((2,)), dma((2,)),
        dma((4,)), dma((2,)), dma((2, 16)), dma((2, 16)), dma((2, 2)),
        dma((15,)), dma((15,)), dma((31,)), dma((31,)), dma((15,)), dma((15,)),
    ]
    count = len(shards)

    def kernel(hidden_ref, *refs):
        mods, noisy, sigma_ref = refs[count : count + 3]
        step_kernel(
            fetch, hidden_ref, refs[:count], mods, noisy, sigma_ref, *refs[count + 3 :]
        )

    return pl.pallas_call(
        kernel,
        out_shape=[jax.ShapeDtypeStruct(grad_shape, F32), jax.ShapeDtypeStruct((8, 128), F32)],
        in_specs=[ANY] + [VMEM] * (count + 2) + [SMEM] + [VMEM] * (len(small) - 2 + len(consts)),
        out_specs=[VMEM, VMEM],
        scratch_shapes=scratch,
        compiler_params=pltpu.CompilerParams(
            collective_id=0, has_side_effects=True, vmem_limit_bytes=60 * 1024 * 1024
        ),
        name="step",
    )(hidden, *shards, *small[:2], sigma, *small[2:], *consts)


def flow_sigma(step_index):
    remain = 1.0 - step_index.astype(F32) / STEPS
    return 3.0 * remain / (1.0 + 2.0 * remain)


def prepare(
    modulation, noisy, proj_bias, conv_bias, norm_gain, norm_shift, head_bias,
    position, class_token, vit_gain, vit_shift, attn_out_bias, mlp_out_bias, text_embed,
):
    flat = jnp.concatenate(
        [
            conv_bias, norm_gain, norm_shift, head_bias[:128], proj_bias, jnp.zeros((64,), F32),
            class_token, attn_out_bias, mlp_out_bias, jnp.zeros((16,), F32), head_bias[128:],
            jnp.zeros((432,), F32),
        ]
    )
    return (
        modulation[0], noisy.reshape(512, 64), flat.reshape(48, 128), vit_gain, vit_shift, position,
        text_embed,
    )


def local(
    hidden, modulation, noisy, step_index, proj_weight, proj_bias, conv_weight, conv_bias,
    norm_gain, norm_shift, head_weight, head_bias, patch_weight, position, class_token,
    vit_gain, vit_shift, attn_in, attn_out, attn_out_bias, mlp_in, mlp_in_bias, mlp_out,
    mlp_out_bias, vit_proj, text_embed,
):
    shards = raw_shards(
        proj_weight, conv_weight, head_weight, patch_weight, attn_in, attn_out, mlp_in,
        mlp_in_bias, mlp_out, vit_proj,
    )
    small = prepare(
        modulation, noisy, proj_bias, conv_bias, norm_gain, norm_shift, head_bias, position,
        class_token, vit_gain, vit_shift, attn_out_bias, mlp_out_bias, text_embed,
    )
    grad, score = run_step(
        shards, True, (96, 64), hidden.reshape(512, 3072), flow_sigma(step_index).reshape(1, 1),
        small, constants(),
    )
    return grad, score[0, 0:1]


def solution(mesh):
    placed = (
        P(("fsdp", "grp"), "slab", None, None),
        P(("fsdp", "grp"), None, None),
        P(("fsdp", "grp"), "slab", None, None),
        P(("fsdp", "grp")),
        P("fsdp", None),
        P(),
        P(None, None, None, "fsdp"),
        P(),
        P(),
        P(),
        P("fsdp", None),
        P(),
        P(None, "fsdp"),
        P("slab", None),
        P(),
        P(),
        P(),
        P("fsdp", "slab"),
        P("slab", "fsdp"),
        P(),
        P(None, ("fsdp", "slab")),
        P(("fsdp", "slab")),
        P(("fsdp", "slab"), None),
        P(),
        P("fsdp", None),
        P(("fsdp", "grp"), None),
    )
    return jax.shard_map(
        local,
        mesh=mesh,
        in_specs=placed,
        out_specs=(P("fsdp", None), P(("fsdp", "grp"))),
        check_vma=False,
    )
```

```python
import functools

import jax
import jax.numpy as jnp
import numpy as np
from jax import lax
from jax.experimental import pallas as pl
from jax.experimental.pallas import tpu as pltpu
from jax.sharding import PartitionSpec as P

HEAD_DIM = 80
STEPS = 28
LAT_SCALE = 0.3611
LAT_SHIFT = 0.1159
PIX_MEAN = (0.48145466, 0.4578275, 0.40821073)
PIX_STD = (0.26862954, 0.26130258, 0.27577711)
HIGH = lax.Precision.HIGHEST
MESH = pl.DeviceIdType.MESH
F32 = jnp.float32
BF16 = jnp.bfloat16
ANY = pl.BlockSpec(memory_space=pl.ANY)
VMEM = pl.BlockSpec(memory_space=pltpu.VMEM)
SMEM = pl.BlockSpec(memory_space=pltpu.SMEM)
ROOT = HEAD_DIM**0.5
WIDTH = 1280
WIDE = 1536
CELLS = 128 * 128 * 16
NF, NS, NZ = 32, 8, 16
LANES = 2048


def nn(a, b, precision=None):
    return lax.dot_general(
        a, b, (((1,), (0,)), ((), ())), precision=precision, preferred_element_type=F32
    )


def nt(a, b, precision=None):
    return lax.dot_general(
        a, b, (((1,), (1,)), ((), ())), precision=precision, preferred_element_type=F32
    )


def sigmoid(values):
    return 0.5 + 0.5 * jnp.tanh(0.5 * values)


def halves(values):
    high = values.astype(BF16)
    return high, (values - high.astype(F32)).astype(BF16)


def thirds(values):
    high, rest = halves(values)
    middle = (values - high.astype(F32) - rest.astype(F32)).astype(BF16)
    return [high, rest, middle]


def remote(source, dest, send, recv, target):
    return pltpu.make_async_remote_copy(
        src_ref=source, dst_ref=dest, send_sem=send, recv_sem=recv,
        device_id=target, device_id_type=MESH,
    )


def iota(shape, dim):
    return lax.broadcasted_iota(jnp.int32, shape, dim)


def norm_stats(values, mask, epsilon):
    average = jnp.sum(values, axis=-1, keepdims=True) * (1.0 / WIDTH)
    centered = (values - average) * mask
    square = jnp.sum(centered * centered, axis=-1, keepdims=True) * (1.0 / WIDTH)
    inverse = 1.0 / jnp.sqrt(square + epsilon)
    return centered * inverse, inverse


def norm_back(grads, scaled, inverse, gain):
    grads = grads * gain
    first = jnp.sum(grads, axis=-1, keepdims=True) * (1.0 / WIDTH)
    second = jnp.sum(grads * scaled, axis=-1, keepdims=True) * (1.0 / WIDTH)
    return (grads - first - scaled * second) * inverse


class Weights:
    def __init__(self, c_own, p_own, a_own, b_own, c_buf, p_buf, a_buf, b_buf, sems):
        self.c_own, self.p_own, self.owns = c_own, p_own, (a_own, b_own)
        self.c_buf, self.p_buf, self.bufs = c_buf, p_buf, (a_buf, b_buf)
        (self.z_send, self.z_recv, self.sh_send, self.sh_recv, self.fw_send, self.fw_recv,
         self.loc, self.pair_sem, self.ring_send, self.ring_recv, self.core_sem) = sems
        self.f = lax.axis_index("fsdp")
        self.g = lax.axis_index("grp")
        self.s = lax.axis_index("slab")
        self.w = self.g * NS + self.s
        self.z, self.half = self.f // 2, lax.rem(self.f, 2)
        self.core = {"grp": 1 - self.g}
        self.inside = self.f // 16 == self.g

    def to_fsdp(self, source, dest, k):
        def send(d, carry):
            target = {"fsdp": lax.rem(self.f + d, NF)}
            remote(source, dest, self.z_send.at[k], self.z_recv.at[k], target).start()
            return carry

        lax.fori_loop(1, NF, send, 0)

    def c_copy(self):
        return pltpu.make_async_copy(
            self.c_own.at[self.s], self.c_buf.at[self.s, self.f], self.loc.at[0]
        )

    def c_start(self):
        @pl.when(self.inside)
        def _():
            self.c_copy().start()
            self.to_fsdp(self.c_own.at[self.s], self.c_buf.at[self.s, self.f], 0)

    def c_part(self, n):
        return self.c_buf.at[n, pl.ds(16 * self.g, 16)]

    def c_share(self):
        @pl.when(self.inside)
        def _():
            self.c_copy().wait()
            many = self.c_buf.at[self.s, pl.ds(16 * self.g, 15)]
            remote(many, many, self.z_send.at[0], self.z_recv.at[0], self.core).wait_recv()

        @pl.when(jnp.logical_not(self.inside))
        def _():
            many = self.c_part(self.s)
            remote(many, many, self.z_send.at[0], self.z_recv.at[0], self.core).wait_recv()

        for d in range(1, NS):
            self.share_copy(0, d, self.c_part(self.s)).start()

    def share_copy(self, k, d, block):
        return remote(
            block, block, self.sh_send.at[k, d - 1], self.sh_recv.at[k, d - 1],
            {"slab": lax.rem(self.s + d, NS)},
        )

    def core_copy(self, k, block):
        return remote(block, block, self.fw_send.at[k], self.fw_recv.at[k], self.core)

    def c_core(self):
        for d in range(1, NS):
            self.share_copy(0, d, self.c_part(lax.rem(self.s + NS - d, NS))).wait_recv()
        self.core_copy(0, self.c_buf.at[:, pl.ds(16 * self.g, 16)]).start()

    def c_done(self):
        self.core_copy(0, self.c_buf.at[:, pl.ds(16 - 16 * self.g, 16)]).wait_recv()

    def p_copy(self):
        return pltpu.make_async_copy(
            self.p_own.at[self.w], self.p_buf.at[self.w, self.f], self.loc.at[1]
        )

    def p_start(self):
        self.p_copy().start()
        self.to_fsdp(self.p_own.at[self.w], self.p_buf.at[self.w, self.f], 1)

    def p_ready(self):
        many = self.p_buf.at[self.w, pl.ds(0, NF - 1)]
        remote(many, many, self.z_send.at[1], self.z_recv.at[1], self.core).wait_recv()
        self.p_copy().wait()

    def p_share(self, *pieces):
        for d in pieces:
            self.share_copy(1, d, self.p_buf.at[self.w]).start()

    def p_core(self):
        for d in range(1, NS):
            block = self.p_buf.at[self.g * NS + lax.rem(self.s + NS - d, NS)]
            self.share_copy(1, d, block).wait_recv()
        self.core_copy(1, self.p_buf.at[pl.ds(self.g * NS, NS)]).start()

    def p_done(self):
        self.core_copy(1, self.p_buf.at[pl.ds((1 - self.g) * NS, NS)]).wait_recv()

    def view(self, kind, z):
        return self.bufs[kind].at[self.g, lax.rem(z, NZ)]

    def own(self, kind):
        dest = self.view(kind, self.z)
        dest = dest.at[self.half] if kind == 0 else dest
        return pltpu.make_async_copy(self.owns[kind], dest, self.loc.at[2 + kind])

    def pair(self):
        return remote(
            self.owns[0], self.bufs[0].at[self.g, self.z, self.half],
            self.pair_sem.at[0], self.pair_sem.at[1], {"fsdp": self.z * 2 + 1 - self.half},
        )

    def start(self):
        self.pair().start()
        self.own(0).start()
        self.own(1).start()

    def step(self, kind, step, way):
        sign = NZ - 1 if way == 0 else 1
        block = self.view(kind, self.z + sign * step)
        hop = 1 if way == 0 else NZ - 1
        target = {"fsdp": lax.rem(self.z + hop, NZ) * 2 + self.half}
        slot = way * 8 + step
        return remote(
            block, block, self.ring_send.at[kind, slot], self.ring_recv.at[kind, slot], target
        )

    def share(self, kind, z):
        block = self.view(kind, z)
        remote(block, block, self.core_sem.at[kind, 0], self.core_sem.at[kind, 1], self.core).start()

    def pump(self, kind, step):
        steps = (NZ // 2, NZ // 2 - 1)
        if step == 0:
            self.own(kind).wait()
            if kind == 0:
                self.pair().wait_recv()
        for way in (0, 1):
            if 0 < step <= steps[way]:
                self.step(kind, step - 1, way).wait_recv()
            if step < steps[way]:
                self.step(kind, step, way).start()
        if step == 0:
            self.share(kind, self.z)
        for way in (0, 1):
            if 0 < step <= steps[way]:
                self.share(kind, self.z + (NZ - step if way == 0 else step))

    def landed(self, kind):
        theirs = self.bufs[kind].at[1 - self.g]
        remote(
            theirs, theirs, self.core_sem.at[kind, 0], self.core_sem.at[kind, 1], self.core
        ).wait_recv()

    def finish(self):
        for kind in range(2):
            mine = self.bufs[kind].at[self.g]
            remote(
                mine, mine, self.core_sem.at[kind, 0], self.core_sem.at[kind, 1], self.core
            ).wait_send()
            for way, steps in ((0, NZ // 2), (1, NZ // 2 - 1)):
                for step in range(steps):
                    self.step(kind, step, way).wait_send()
        self.pair().wait_send()

        @pl.when(self.inside)
        def _():
            many = self.c_buf.at[self.s, pl.ds(0, NF - 1)]
            remote(many, many, self.z_send.at[0], self.z_recv.at[0], self.core).wait_send()

        many = self.p_buf.at[self.w, pl.ds(0, NF - 1)]
        remote(many, many, self.z_send.at[1], self.z_recv.at[1], self.core).wait_send()
        for d in range(1, NS):
            self.share_copy(0, d, self.c_part(self.s)).wait_send()
            self.share_copy(1, d, self.p_buf.at[self.w]).wait_send()
        self.core_copy(0, self.c_buf.at[:, pl.ds(16 * self.g, 16)]).wait_send()
        self.core_copy(1, self.p_buf.at[pl.ds(self.g * NS, NS)]).wait_send()


def greet(targets):
    barrier = pltpu.get_barrier_semaphore()
    for target in targets:
        pl.semaphore_signal(barrier, inc=1, device_id=target, device_id_type=MESH)


def greeted(targets):
    pl.semaphore_wait(pltpu.get_barrier_semaphore(), len(targets))


def block_targets(g, s):
    found = []
    for d in range(1, 2 * NS):
        other_g = lax.rem(g + d // NS, 2)
        other_s = lax.rem(s + d % NS, NS)
        found.append((other_g * NS + other_s, {"grp": other_g, "slab": other_s}))
    return found


def pair_targets(f, s):
    z, half = f // 2, lax.rem(f, 2)
    found = []
    for h in range(2):
        there = z * 2 + lax.rem(half + h, 2)
        for d in range(NS):
            if h or d:
                found.append((h * NS + d - 1, {"fsdp": there, "slab": lax.rem(s + d, NS)}))
    return found


def all_targets():
    f, g, s = lax.axis_index("fsdp"), lax.axis_index("grp"), lax.axis_index("slab")
    return (
        [target for _, target in block_targets(g, s)]
        + [{"fsdp": lax.rem(f + d, NF)} for d in range(1, NF)]
        + [target for _, target in pair_targets(f, s)[NS:]]
    )


def reduce_gradient(mine, landed, terms, arrived, collected, sems, meanwhile):
    a_send, a_recv, b_send, b_recv, c_send, c_recv = sems
    f, g, s = lax.axis_index("fsdp"), lax.axis_index("grp"), lax.axis_index("slab")
    w = g * NS + s
    block = block_targets(g, s)
    copies = []
    for d, (index, target) in enumerate(block):
        copy = remote(mine.at[index], landed.at[w], a_send.at[d], a_recv.at[d], target)
        copy.start()
        copies.append(copy)
    landed[w] = mine[w]
    meanwhile()
    for copy in copies:
        copy.wait()
    total = landed[0].astype(F32)
    for index in range(1, 2 * NS):
        total = total + landed[index].astype(F32)
    for index in range(NF):
        rows, lanes = 4 * (index // 8), 96 * (index % 8)
        terms[index, :, 0:96] = total[rows : rows + 4, lanes : lanes + 96]
        terms[index, :, 96:128] = jnp.zeros((4, 32), F32)
    copies = []
    for d in range(1, NF):
        p = lax.rem(f + d, NF)
        copy = remote(terms.at[p], arrived.at[f], b_send.at[d - 1], b_recv.at[d - 1], {"fsdp": p})
        copy.start()
        copies.append(copy)
    arrived[f] = terms[f]
    for copy in copies:
        copy.wait()
    collected[w] = jnp.sum(arrived[...], axis=0)
    copies = []
    for d, (index, target) in enumerate(block):
        copy = remote(collected.at[w], collected.at[w], c_send.at[d], c_recv.at[d], target)
        copy.start()
        copies.append(copy)
    for copy in copies:
        copy.wait()


def pack_tiles(
    g, s, proj_in, conv_in, head_in, patch_in, attn_in, back_in, up_in, bias_in, down_in,
    vit_in, patch_perm, wide_w, back_perm, tail_perm, fill, c_own, p_own, a_own, b_own,
):
    choose = (iota((96, 96), 0) == iota((96, 96), 1)).astype(BF16)
    proj = nt(choose, proj_in[...])
    proj = jnp.concatenate([proj[0:48], proj[48:96]], axis=1).astype(BF16)
    for n in range(3):
        c_own[n] = proj[16 * n : 16 * n + 16]
    c_own[3] = conv_in[:, 0:128]
    c_own[4] = head_in[:, 0:128]
    c_own[5] = (
        nn(conv_in[:, 128:144], tail_perm[0:16, :]) + nn(head_in[:, 128:192], tail_perm[16:80, :])
    ).astype(BF16)
    patch = nn(patch_in[...], patch_perm[...])
    patch = jnp.concatenate([patch, jnp.zeros((8, 640), F32)], axis=0).astype(BF16)
    for u in range(5):
        for rb in range(3):
            n = 3 * u + rb
            block = patch[16 * rb : 16 * rb + 16, 128 * u : 128 * u + 128]
            if n < 2:
                c_own[6 + n] = block
            else:
                p_own[n - 2] = block
    for n in range(13, 16):
        p_own[n] = jnp.zeros((16, 128), BF16)

    def tall(rows, lanes):
        values = rows.astype(F32)
        more = lanes - values.shape[1]
        if more:
            values = jnp.concatenate([values, jnp.zeros((40, more), F32)], axis=1)
        return jnp.concatenate([values, jnp.zeros((8, lanes), F32)], axis=0)

    attn = tall(attn_in[...], 512)
    back = tall(nn(back_in[...], back_perm[...]), 256)
    vit = tall(vit_in[:, pl.ds(pl.multiple_of(128 * s, 128), 128)], 128)
    tiles = [attn[:, 128 * u : 128 * u + 128] for u in range(4)] + [back[:, 0:128], back[:, 128:256]]
    for u in range(3):
        a_own[48 * u : 48 * u + 48, :] = jnp.where(g == 0, tiles[u], tiles[3 + u]).astype(BF16)
    last = jnp.concatenate([vit[32:48], jnp.zeros((16, 128), F32)], axis=0)
    a_own[144:176, :] = jnp.where(g == 0, vit[0:32], last).astype(BF16)
    fill[0:20, :] = up_in[...].astype(F32)
    fill[20:40, :] = down_in[...].astype(F32)
    fill[40:48, :] = jnp.zeros((8, WIDTH), F32)
    values = fill[...].astype(BF16)
    wide = jnp.concatenate([nn(values[:, 0:640], wide_w[...]), nn(values[:, 640:1280], wide_w[...])], axis=1)
    bias = jnp.where(
        iota((48, 20), 0) == iota((48, 20), 1), jnp.broadcast_to(bias_in[...].astype(F32), (48, 20)), 0.0
    )
    bias = jnp.sum(bias, axis=1, keepdims=True)
    wide = jnp.where(iota((48, WIDE), 1) == 40, bias, wide)
    wide = jnp.where(g == 0, wide[:, 0:768], wide[:, 768:1536]).astype(BF16)
    for u in range(6):
        b_own[u] = wide[:, 128 * u : 128 * u + 128]


def step_kernel(
    fetch, hidden, shards, mods, noisy, sigma_ref, flat, gain_in, shift_in, position_in, text,
    perm, perm_t, inter, columns_w, rows_w, ph0, ph1, lane_rows, patch_perm, wide_w, back_perm, tail_perm,
    grad_out, score_out,
    hid, mod, c_own, p_own, a_own, b_own, c_buf, p_buf, a_buf, b_buf, vecs, fill,
    proj_full, ext, halo_out, halo_in, nrm, dnrm, acc, stat_out, stat_in,
    cols_buf, pix, head_t, head_p, edge_out, edge_in, kd_out, kd_in, dirs, u_out, u_in,
    ao_out, ao_in, row_out, row_in, text_in, emb_out, emb_in, vd_out, vd_in, rim_out, rim_in, gsplit, mine, landed,
    terms, arrived, collected,
    x_send, x_recv, hid_sem, *sems,
):
    s = lax.axis_index("slab")
    f = lax.axis_index("fsdp")
    half = lax.rem(f, 2)
    low, high = s > 0, s < NS - 1
    low_f, high_f = jnp.where(low, 1.0, 0.0), jnp.where(high, 1.0, 0.0)
    before, after = {"slab": lax.rem(s + NS - 1, NS)}, {"slab": lax.rem(s + 1, NS)}
    hid_copy = pltpu.make_async_copy(hidden, hid, hid_sem.at[0])
    hid_copy.start()
    sigma = sigma_ref[0, 0]
    live = []

    def to_all(kind, source, dest, swap=False):
        copies = []
        for d in range(1, NS):
            p = lax.rem(s + d, NS)
            copies.append(
                remote(
                    source.at[p] if swap else source, dest.at[s],
                    x_send.at[kind, d - 1], x_recv.at[kind, d - 1], {"slab": p},
                )
            )
        for copy in copies:
            copy.start()
        live.extend(copies)
        return copies

    def to_sides(kind, source, dest):
        copies = [
            remote(source.at[0], dest.at[0], x_send.at[kind, 0], x_recv.at[kind, 0], after),
            remote(source.at[1], dest.at[1], x_send.at[kind, 1], x_recv.at[kind, 1], before),
        ]
        for copy in copies:
            copy.start()
        live.extend(copies)
        return copies

    def landed_all(copies):
        for copy in copies:
            copy.wait_recv()

    def flat_row(first, count):
        return jnp.concatenate([flat[k : k + 1, :] for k in range(first, first + count)], axis=1)

    targets = all_targets() if fetch else [target for _, target in pair_targets(f, s)]
    greet(targets)

    scale = 1.0 + mods[1:2].astype(F32)
    shift = mods[0:1].astype(F32)

    def modulate(lo, hi):
        def body(i, carry):
            rows = pl.ds(pl.multiple_of(i * 32, 32), 32)
            values = hid[rows, :].astype(F32)
            average = jnp.mean(values, axis=-1, keepdims=True)
            centered = values - average
            square = jnp.mean(centered * centered, axis=-1, keepdims=True)
            scaled = centered * (1.0 / jnp.sqrt(square + 1e-06))
            mod[rows, :] = (scaled * scale + shift).astype(BF16)
            return carry

        lax.fori_loop(lo, hi, body, 0)

    if fetch:
        weights = Weights(c_own, p_own, a_own, b_own, c_buf, p_buf, a_buf, b_buf, sems[:11])
        pack_tiles(
            weights.g, s, *shards, patch_perm, wide_w, back_perm, tail_perm, fill, c_own, p_own, a_own, b_own
        )
    else:
        weights = None
        for ref, given in zip((c_buf, p_buf, a_buf, b_buf), shards):
            ref[...] = given[...]
    greeted(targets)
    if fetch:
        weights.c_start()
        weights.start()
    words_copy = remote(
        text, text_in.at[half], x_send.at[12, 0], x_recv.at[12, 0], {"fsdp": f + 1 - 2 * half}
    )
    words_copy.start()
    live.append(words_copy)
    text_in[half] = text[...]

    def pump(*steps):
        if weights is not None:
            for kind, step in enumerate(steps):
                if step is not None:
                    weights.pump(kind, step)

    fill[0:1, :] = flat_row(14, 10)
    fill[1:5, :] = gain_in[...]
    fill[5:9, :] = shift_in[...]
    fill[9:10, :] = flat_row(24, 10)
    fill[10:11, :] = flat_row(34, 10)
    fill[11:16, :] = jnp.zeros((5, WIDTH), F32)
    fill[16:48, :] = position_in[...].astype(F32)
    for k in range(2):
        parts = jnp.concatenate(thirds(fill[:, 640 * k : 640 * k + 640]), axis=0)
        parts = nn(parts, wide_w[...])
        vecs[:, 768 * k : 768 * k + 768] = parts[0:48] + (parts[48:96] + parts[96:144])
    hid_copy.wait()
    modulate(0, 16)
    if weights is not None:
        weights.c_share()
        pump(0, 0)
        weights.p_start()
        pump(1)
        weights.c_core()
        pump(2, 1)
        weights.c_done()

    def patch_unit(u):
        parts = []
        for rb in range(3):
            n = 3 * u + rb
            parts.append(c_buf[6 + n] if n < 2 else p_buf[n - 2])
        return jnp.concatenate(parts, axis=1).reshape(WIDE, 128)

    def a_unit(index):
        k = index % 3
        return a_buf[index // 3, :, :, 48 * k : 48 * k + 48].reshape(WIDE, 128)

    for n in range(3):
        both = c_buf[n].reshape(512, 128).astype(F32)
        turned = pltpu.roll(both, 64, 1).astype(BF16)
        for k in range(NF):
            at = 96 * k + 16 * n
            proj_full[at : at + 16, :] = c_buf[n, k]
            proj_full[at + 48 : at + 64, :] = turned[16 * k : 16 * k + 16]
    velocity = nn(mod[...], proj_full[...])[:, :64] + flat[13:14, 64:128]
    pump(3)
    clean = noisy[...].astype(F32) - sigma * velocity
    lat_tok = (clean / LAT_SCALE + LAT_SHIFT).astype(BF16)
    tok_t = nt(perm_t[...], lat_tok)
    stacked = jnp.concatenate(
        [
            jnp.concatenate(
                [tok_t[0:32, 128 * k : 128 * k + 128], tok_t[32:64, 128 * k : 128 * k + 128]], axis=1
            )
            for k in range(4)
        ],
        axis=0,
    ).astype(BF16)
    latent = nn(stacked, inter[...]).astype(BF16)
    for k in range(4):
        for i2 in range(2):
            for p in range(2):
                r = 4 * k + 2 * i2 + p + 1
                for b in range(3):
                    at = (i2 * 3 + b) * 128
                    ext[16 * b : 16 * b + 16, 128 * r : 128 * r + 128] = latent[
                        32 * k + 16 * p : 32 * k + 16 * p + 16, at : at + 128
                    ]
    halo_out[0] = ext[:, 2048:2176]
    halo_out[1] = ext[:, 128:256]
    copies = to_sides(0, halo_out, halo_in)
    same = (iota((512, 512), 0) // 16 == iota((512, 512), 1) // 16).astype(BF16)

    def columns_of(rows):
        width = rows.shape[1]
        return jnp.transpose(jnp.concatenate([rows, jnp.zeros((120, width), F32)], axis=0))

    chan = jnp.concatenate(
        [flat_row(0, 4), flat_row(4, 4), flat_row(8, 4), jnp.zeros((5, 512), F32)], axis=0
    )
    chan_cols = columns_of(chan)
    conv_bias, gain, gshift = chan_cols[:, 0:1], chan_cols[:, 1:2], chan_cols[:, 2:3]
    eye = (iota((128, 128), 0) == iota((128, 128), 1)).astype(BF16)
    conv0 = c_buf[3].reshape(512, 128)
    head0 = c_buf[4].reshape(512, 128)
    tail = c_buf[5].reshape(512, 128)
    head_p[...] = (nn(head0, ph0[...]) + nn(tail, ph1[...])).astype(BF16)
    head_t[...] = (
        lax.dot_general(ph0[...], head0, (((0,), (1,)), ((), ())), preferred_element_type=F32)
        + lax.dot_general(ph1[...], tail, (((0,), (1,)), ((), ())), preferred_element_type=F32)
    ).astype(BF16)
    bias_row = nn(jnp.broadcast_to(flat[12:13, :], (8, 128)), ph0[...].astype(F32), HIGH) + nn(
        jnp.broadcast_to(flat[13:14, 0:64], (8, 64)), ph1[16:80, :].astype(F32), HIGH
    )
    head_col = columns_of(bias_row)[:, 0:1]
    pump(4, 2)
    if weights is not None:
        weights.p_ready()
    landed_all(copies)
    if weights is not None:
        weights.p_share(1, 2, 3)
    ext[:, 0:128] = (halo_in[0].astype(F32) * low_f).astype(BF16)
    ext[:, 2176:2304] = (halo_in[1].astype(F32) * high_f).astype(BF16)
    acc[...] = jnp.zeros_like(acc)

    def conv_chunk(i, carry):
        at = pl.multiple_of(i * 256, 256)
        parts = [ext[:, pl.ds(pl.multiple_of(at + 128 * a, 128), 256)] for a in range(3)]
        columns = jnp.concatenate(parts + [jnp.zeros((112, 256), BF16)], axis=0)
        out = nn(conv0, columns[0:128]) + nn(tail, columns[128:256]) + conv_bias
        nrm[:, pl.ds(at, 256)] = out
        acc[0] += out[:, 0:128] + out[:, 128:256]
        square = out * out
        acc[1] += square[:, 0:128] + square[:, 128:256]
        return carry

    lax.fori_loop(0, 8, conv_chunk, 0)

    def group_totals(kind, step=None):
        ones = jnp.ones((8, 128), BF16)
        first, second = [
            nt(ones, part[0]) + (nt(ones, part[1]) + nt(ones, part[2]))
            for part in (thirds(acc[0]), thirds(acc[1]))
        ]
        k = kind - 1
        stat_out[k] = jnp.concatenate([first[0:1], second[0:1]], axis=0)
        copies = to_all(kind, stat_out.at[k], stat_in.at[k])
        stat_in[k, s] = stat_out[k]
        if step is not None:
            pump(*step)
        landed_all(copies)
        total = stat_in[k, 0]
        for index in range(1, NS):
            total = total + stat_in[k, index]
        total = jnp.concatenate([total, jnp.zeros((6, 512), F32)], axis=0)
        sums = nn(jnp.concatenate(thirds(total), axis=0), same)
        columns = columns_of(sums[0:8] + (sums[8:16] + sums[16:24]))
        return columns[:, 0:1] * (1.0 / CELLS), columns[:, 1:2] * (1.0 / CELLS)

    average, square = group_totals(1, (5, 3))
    inverse = 1.0 / jnp.sqrt(square - average * average + 1e-06)
    if weights is not None:
        weights.p_share(4, 5, 6, 7)

    def head_chunk(i, carry):
        at = pl.multiple_of(i * 256, 256)
        normed = (nrm[:, pl.ds(at, 256)] - average) * inverse
        nrm[:, pl.ds(at, 256)] = normed
        gained = normed * gain + gshift
        active = (gained * sigmoid(gained)).astype(BF16)
        cells = (nn(head_t[...], active) + head_col).astype(BF16)
        for rr in range(2):
            rows = pl.ds(pl.multiple_of(i * 64 + 32 * rr, 32), 32)
            for x in range(8):
                pix[rows, 128 * x : 128 * x + 128] = cells[
                    32 * x : 32 * x + 32, 128 * rr : 128 * rr + 128
                ]
        return carry

    lax.fori_loop(0, 4, head_chunk, 0)
    pump(6, 4)
    lax.fori_loop(4, 8, head_chunk, 0)
    pump(7, 5)
    narrow = nt(columns_w[...], pix[...]).astype(BF16)
    raw = jnp.zeros((80, 512), F32)
    for m in range(3):
        raw = raw + nn(narrow[128 * m : 128 * m + 80], rows_w[512 * m : 512 * m + 512, :])
    edge_out[0, 0] = raw[:, 256:384]
    edge_out[0, 1] = raw[:, 384:512]
    copies = to_sides(2 + 1, edge_out.at[0], edge_in.at[0])
    pump(8, 6)
    if weights is not None:
        weights.p_core()
        weights.landed(0)
    lane = iota((1, WIDE), 1)
    mask = (lax.rem(lane, 48) < 40).astype(F32)
    gains = [vecs[1 + i : 2 + i, :] for i in range(4)]
    shifts = [vecs[5 + i : 6 + i, :] for i in range(4)]
    class_hat, _ = norm_stats(vecs[0:1, :], mask, 1e-05)
    class_pre = class_hat * gains[0] + shifts[0]
    class_hat, _ = norm_stats(class_pre, mask, 1e-05)
    class_unit = jnp.broadcast_to(class_hat * gains[1] + shifts[1], (8, WIDE)).astype(BF16)
    attn = [a_unit(i) for i in range(4)]
    class_qkv = jnp.concatenate([nn(class_unit, attn[i]) for i in range(4)], axis=1)
    class_qkv = class_qkv.astype(BF16).astype(F32)
    place512 = iota((8, 512), 1)
    row512 = iota((8, 512), 0)
    start = jnp.where(row512 == 0, 0, 240)
    in_head = row512 < 2
    key_at = in_head & (place512 >= start + 80) & (place512 < start + 160)
    val_at = in_head & (place512 >= start + 160) & (place512 < start + 240)
    query = jnp.where(key_at, pltpu.roll(class_qkv, 80, 1), 0.0)
    class_exp = jnp.exp(jnp.sum(query * class_qkv, axis=-1, keepdims=True) / ROOT)
    query_b = query.astype(BF16)
    key_dir = nt(query_b[:, 0:128], attn[0])
    for i in range(1, 4):
        key_dir = key_dir + nt(query_b[:, 128 * i : 128 * i + 128], attn[i])
    kd_out[...] = key_dir[0:2]
    kd_copies = to_all(4, kd_out, kd_in)
    kd_in[s] = key_dir[0:2]
    corr0 = jnp.where(low, 1.0, lane_rows[0:1, :])
    corr1 = jnp.where(high, 1.0, lane_rows[1:2, :])
    img_scale, img_shift = lane_rows[2:3, :], lane_rows[3:4, :]
    if weights is not None:
        weights.p_done()
    landed_all(copies)
    top = (raw[:, 0:128] * corr0 + edge_in[0, 0] * low_f) * img_scale + img_shift
    bottom = (raw[:, 128:256] * corr1 + edge_in[0, 1] * high_f) * img_scale + img_shift
    patches = jnp.concatenate(
        [
            jnp.concatenate([part[16 * u : 16 * u + 16] for u in range(5)], axis=1)
            for part in (top, bottom)
        ],
        axis=0,
    ).astype(BF16)
    embedded = vecs[16:48, :]
    for u in range(5):
        embedded = embedded + nt(patches[:, 128 * u : 128 * u + 128], patch_unit(u))
    hat0, inv0 = norm_stats(embedded, mask, 1e-05)
    hat1, inv1 = norm_stats(hat0 * gains[0] + shifts[0], mask, 1e-05)
    unit = hat1 * gains[1] + shifts[1]
    unit_b = unit.astype(BF16)
    unit = unit_b.astype(F32)
    pump(None, 7)
    landed_all(kd_copies)
    for index in range(NS):
        dirs[2 * index : 2 * index + 2, :] = kd_in[index]
    token_exp = jnp.exp(nt(dirs[0:16, :], unit, HIGH) / ROOT)
    gathered = nn(token_exp, unit, HIGH)
    gathered = jnp.where(lane == 40, jnp.sum(token_exp, axis=1, keepdims=True), gathered)
    for index in range(NS):
        u_out[index] = gathered[2 * index : 2 * index + 2]
    copies = to_all(5, u_out, u_in, swap=True)
    u_in[s] = u_out[s]
    pump(None, 8)
    landed_all(copies)
    total = u_in[0]
    for index in range(1, NS):
        total = total + u_in[index]
    denominator = class_exp[0:2] + total[:, 40:41]
    mixed = halves(jnp.concatenate([total[0:2], jnp.zeros((6, WIDE), F32)], axis=0))
    first = nn(mixed[0], attn[1]) + nn(mixed[1], attn[1])
    second = nn(mixed[0], attn[3]) + nn(mixed[1], attn[3])
    heads1 = jnp.where(val_at[0:1, 128:256], first[0:1] + class_exp[0:1] * class_qkv[0:1, 128:256], 0.0)
    heads3 = jnp.where(val_at[1:2, 384:512], second[1:2] + class_exp[1:2] * class_qkv[0:1, 384:512], 0.0)
    heads1 = heads1 / denominator[0:1]
    heads3 = heads3 / denominator[1:2]
    rows1 = a_unit(4)
    rows3 = a_unit(5)

    def wide8(row):
        if row.shape[0] == 1:
            return jnp.broadcast_to(row, (8, row.shape[1])).astype(BF16)
        return jnp.concatenate([row, jnp.zeros((6, row.shape[1]), F32)], axis=0).astype(BF16)

    def mine_of(rows):
        return jnp.where(half == 0, rows[0:1], rows[1:2])

    attn_part = nt(wide8(heads1), rows1) + nt(wide8(heads3), rows3)

    def pair_sum(kind, k, rows):
        row_out[k] = rows[0:2]
        copies = [
            remote(
                row_out.at[k], row_in.at[k, half, s], x_send.at[kind, index], x_recv.at[kind, index],
                target,
            )
            for index, target in pair_targets(f, s)
        ]
        for copy in copies:
            copy.start()
        live.extend(copies)
        row_in[k, half, s] = row_out[k]
        landed_all(copies)
        sums = []
        for h in range(2):
            total = row_in[k, h, 0]
            for index in range(1, NS):
                total = total + row_in[k, h, index]
            sums.append(total)
        return sums

    ao_out[...] = attn_part[0:1]
    copies = [
        remote(ao_out, ao_in.at[half, s], x_send.at[6, index], x_recv.at[6, index], target)
        for index, target in pair_targets(f, s)
    ]
    for copy in copies:
        copy.start()
    live.extend(copies)
    ao_in[half, s] = attn_part[0:1]
    landed_all(copies)
    sums = []
    for h in range(2):
        total = ao_in[h, 0]
        for index in range(1, NS):
            total = total + ao_in[h, index]
        sums.append(total)
    block_mid = class_pre + jnp.concatenate(sums, axis=0) + vecs[9:10, :]
    hat2, inv2 = norm_stats(block_mid, mask, 1e-05)
    mlp_input = hat2 * gains[2] + shifts[2]
    mlp_input = wide8(jnp.where(lane == 40, 1.0, mlp_input))
    if weights is not None:
        weights.landed(1)
    hidden_units = [b_buf[i // 6, :, i % 6].reshape(WIDE // 2, 128) for i in range(12)]
    unit_at = lax.rem(iota((1, WIDE // 2), 1), 48) < 20
    preact = nt(mlp_input[:, 0:128], hidden_units[0])
    for i in range(1, 12):
        preact = preact + nt(mlp_input[:, 128 * i : 128 * i + 128], hidden_units[i])
    preact = jnp.where(unit_at, preact, 0.0)
    cdf = 0.5 * (1.0 + lax.erf(preact * 0.7071067811865476))
    active = preact * cdf
    active = pltpu.roll(active, 20, 1).astype(BF16)
    mlp_part = jnp.concatenate([nn(active, hidden_units[i]) for i in range(12)], axis=1)
    sums = pair_sum(7, 1, mlp_part)
    block_out = block_mid + (sums[0] + sums[1]) + vecs[10:11, :]
    hat3, inv3 = norm_stats(block_out, mask, 1e-05)
    post = wide8(hat3 * gains[3] + shifts[3])
    vit = jnp.concatenate([a_buf[0, :, :, 144:176], a_buf[1, :, :, 144:160]], axis=2).reshape(WIDE, 128)
    embed = nn(post, vit)[0:2]
    words_copy.wait_recv()
    words = jnp.concatenate([text_in[0], text_in[1]], axis=0)
    own_words = jnp.concatenate(
        [text_in[k, :, pl.ds(pl.multiple_of(128 * s, 128), 128)] for k in range(2)], axis=0
    )
    four = jnp.concatenate([own_words, embed], axis=0)
    exact = four.astype(BF16).astype(F32)
    eight = nt(jnp.concatenate([exact, four - exact], axis=0).astype(BF16), vit)
    four = eight[0:4] + eight[4:8]
    dots = jnp.sum(embed * own_words, axis=-1, keepdims=True)
    squares = jnp.sum(embed * embed, axis=-1, keepdims=True)
    emb_out[0:2, :] = four[0:2]
    emb_out[2:4, :] = jnp.where(lane == 40, dots, jnp.where(lane == 41, squares, four[2:4]))
    copies = to_all(13, emb_out, emb_in)
    emb_in[s] = emb_out[...]
    landed_all(copies)
    total = emb_in[0]
    for index in range(1, NS):
        total = total + emb_in[index]
    dots, size_e = total[2:4, 40:41], total[2:4, 41:42] + 1e-06
    size_t = jnp.sum(words * words, axis=-1, keepdims=True) + 1e-06
    sizes = jnp.sqrt(size_e) * jnp.sqrt(size_t)
    score = 100.0 * dots / sizes
    score_out[...] = jnp.broadcast_to(mine_of(score), (8, 128))
    d_post = (-1.0 / 64.0) * ((100.0 / sizes) * total[0:2] - (score / size_e) * total[2:4])
    d_second = norm_back(d_post[0:2], hat3, inv3, gains[3])
    d_second_b = wide8(d_second)
    d_active = nt(d_second_b[:, 0:128], hidden_units[0])
    for i in range(1, 12):
        d_active = d_active + nt(d_second_b[:, 128 * i : 128 * i + 128], hidden_units[i])
    d_active = pltpu.roll(d_active, WIDE // 2 - 20, 1)
    slope = cdf + preact * jnp.exp(-0.5 * preact * preact) * 0.3989422804014327
    d_pre = jnp.where(unit_at, d_active * slope, 0.0).astype(BF16)
    input_part = jnp.concatenate([nn(d_pre, hidden_units[i]) for i in range(12)], axis=1)
    sums = pair_sum(8, 2, input_part)
    d_first = d_second + norm_back(sums[0] + sums[1], hat2, inv2, gains[2])
    d_first = wide8(mine_of(d_first))
    d_heads1 = nn(d_first, rows1).astype(BF16)
    d_heads3 = nn(d_first, rows3).astype(BF16)
    value0 = nt(jnp.where(val_at[0:1, 128:256], d_heads1.astype(F32), 0.0).astype(BF16), attn[1])
    value1 = nt(jnp.where(val_at[1:2, 384:512], d_heads3.astype(F32), 0.0).astype(BF16), attn[3])
    expect0 = jnp.sum(d_heads1[0:1].astype(F32) * heads1, axis=-1, keepdims=True)
    expect1 = jnp.sum(d_heads3[0:1].astype(F32) * heads3, axis=-1, keepdims=True)
    values = jnp.concatenate([value0[0:1], value1[0:1]], axis=0)
    expects = jnp.concatenate([expect0, expect1], axis=0)
    vd_out[...] = jnp.where(lane == 40, denominator, jnp.where(lane == 41, expects, values))
    copies = to_all(9, vd_out, vd_in)
    vd_in[s] = vd_out[...]
    token_logits = nt(unit, dirs[0:16, :], HIGH) / ROOT
    landed_all(copies)
    head_at = iota((1, 16), 1)
    denominators = jnp.zeros((1, 16), F32)
    expects = jnp.zeros((1, 16), F32)
    for index in range(NS):
        dirs[16 + 2 * index : 18 + 2 * index, :] = vd_in[index]
        for h in range(2):
            here = head_at == 2 * index + h
            denominators = jnp.where(here, vd_in[index, h : h + 1, 40:41], denominators)
            expects = jnp.where(here, vd_in[index, h : h + 1, 41:42], expects)
    token_weight = jnp.exp(token_logits) / denominators
    token_dots = nt(unit, dirs[16:32, :], HIGH)
    logit_grads = token_weight * (token_dots - expects)
    d_unit = nn(logit_grads / ROOT, dirs[0:16, :], HIGH) + nn(
        token_weight.astype(BF16).astype(F32), dirs[16:32, :], HIGH
    )
    d_pre_x = norm_back(d_unit, hat1, inv1, gains[1])
    d_embedded = norm_back(d_pre_x, hat0, inv0, gains[0]).astype(BF16)
    d_parts = [nn(d_embedded, patch_unit(u)) for u in range(5)]
    d_top = jnp.concatenate([part[0:16] for part in d_parts], axis=0) * img_scale
    d_bottom = jnp.concatenate([part[16:32] for part in d_parts], axis=0) * img_scale
    edge_out[1, 0] = d_bottom
    edge_out[1, 1] = d_top
    copies = to_sides(10, edge_out.at[1], edge_in.at[1])
    landed_all(copies)
    d_raw = jnp.concatenate(
        [
            jnp.concatenate(
                [d_top * corr0, d_bottom * corr1, edge_in[1, 1] * high_f, edge_in[1, 0] * low_f],
                axis=1,
            ),
            jnp.zeros((48, 512), F32),
        ],
        axis=0,
    ).astype(BF16)
    d_narrow = jnp.concatenate(
        [nt(rows_w[512 * m : 512 * m + 512, :], d_raw) for m in range(3)], axis=1
    ).astype(BF16)
    for k in range(4):
        d_pix = nn(d_narrow, columns_w[:, 256 * k : 256 * k + 256]).astype(BF16)
        for x in range(2):
            rows = slice(64 * k + 32 * x, 64 * k + 32 * x + 32)
            for r in range(16):
                cols_buf[rows, 128 * r : 128 * r + 128] = d_pix[
                    32 * r : 32 * r + 32, 128 * x : 128 * x + 128
                ]
    acc[...] = jnp.zeros_like(acc)

    def head_back(i, carry):
        at = pl.multiple_of(i * 256, 256)
        grads = nn(head_p[...], cols_buf[:, pl.ds(at, 256)])
        normed = nrm[:, pl.ds(at, 256)]
        gained = normed * gain + gshift
        gate = sigmoid(gained)
        grads = grads * (gate * (1.0 + gained * (1.0 - gate))) * gain
        dnrm[:, pl.ds(at, 256)] = grads
        acc[0] += grads[:, 0:128] + grads[:, 128:256]
        both = grads * normed
        acc[1] += both[:, 0:128] + both[:, 128:256]
        return carry

    lax.fori_loop(0, 8, head_back, 0)
    conv0_t = nt(eye, conv0).astype(BF16)
    tail_t = nt(eye[0:16], tail).astype(BF16)
    mean0, mean1 = group_totals(2)

    def conv_back(i, carry):
        at = pl.multiple_of(i * 256, 256)
        grads = (dnrm[:, pl.ds(at, 256)] - mean0 - nrm[:, pl.ds(at, 256)] * mean1) * inverse
        grads = grads.astype(BF16)
        dnrm[0:128, pl.ds(at, 256)] = nn(conv0_t, grads)
        dnrm[128:144, pl.ds(at, 256)] = nn(tail_t, grads)
        return carry

    lax.fori_loop(0, 8, conv_back, 0)
    total = jnp.zeros((16, 2304), F32)
    column = lax.rem(iota((16, 2304), 1), 128)
    for b in range(3):
        part = jnp.zeros((16, 2304), F32)
        for a in range(3):
            t = 3 * a + b
            pieces = [dnrm[16 * t : 16 * t + 16, :]]
            if a:
                pieces = [jnp.zeros((16, 128 * a), F32)] + pieces
            if a < 2:
                pieces = pieces + [jnp.zeros((16, 256 - 128 * a), F32)]
            part = part + jnp.concatenate(pieces, axis=1)
        if b == 0:
            part = jnp.where(column < 127, pltpu.roll(part, 2303, 1), 0.0)
        if b == 2:
            part = jnp.where(column > 0, pltpu.roll(part, 1, 1), 0.0)
        total = total + part
    rim_out[0] = total[:, 2176:2304]
    rim_out[1] = total[:, 0:128]
    copies = to_sides(11, rim_out, rim_in)
    landed_all(copies)
    rows = [total[:, 128 * r + 128 : 128 * r + 256] for r in range(16)]
    rows[0] = rows[0] + rim_in[0] * low_f
    rows[15] = rows[15] + rim_in[1] * high_f
    rows = [-sigma * (row / LAT_SCALE) for row in rows]
    stacked = jnp.concatenate(
        [
            jnp.concatenate([rows[4 * k + p], rows[4 * k + 2 + p]], axis=1)
            for k in range(4)
            for p in range(2)
        ],
        axis=0,
    ).astype(BF16)
    centre = jnp.concatenate([inter[:, 128:256], inter[:, 512:640]], axis=1)
    tok = nt(stacked, centre)
    tok_t = jnp.concatenate(
        [
            jnp.concatenate(
                [tok[32 * k : 32 * k + 32, 128 * q : 128 * q + 128] for k in range(4)], axis=1
            )
            for q in range(2)
        ],
        axis=0,
    ).astype(BF16)
    d_vel = nn(perm[...], tok_t).astype(BF16)
    for quarter in range(4):
        part = nn(d_vel, mod[:, 768 * quarter : 768 * quarter + 768])
        for w in range(2 * NS):
            gsplit[w, 4 * quarter : 4 * quarter + 4] = part[4 * w : 4 * w + 4]
    def sent_all():
        for copy in live:
            copy.wait_send()
        if weights is not None:
            weights.finish()

    if weights is not None:
        mine[...] = gsplit[...].astype(BF16)
        reduce_gradient(mine, landed, terms, arrived, collected, sems[11:], sent_all)
        whole = jnp.concatenate([collected[w] for w in range(2 * NS)], axis=0)
        grad_out[...] = jnp.transpose(whole)[0:96, :]
    else:
        sent_all()
        grad_out[...] = gsplit[...]


def resize_table(out_count, in_count):
    stretch = in_count / out_count
    centers = (np.arange(out_count) + 0.5) * stretch
    places = np.arange(in_count) + 0.5
    weights = np.maximum(0.0, 1.0 - np.abs(places[None, :] - centers[:, None]) / stretch)
    return weights / weights.sum(axis=1, keepdims=True)


def constants():
    perm = np.zeros((64, 64))
    for c in range(16):
        for p in range(2):
            for q in range(2):
                perm[4 * c + 2 * p + q, q * 32 + p * 16 + c] = 1
    inter = np.zeros((2, 2, 64, 2, 3, 128))
    for q in range(2):
        for i2 in range(2):
            for j in range(64):
                for b in range(3):
                    at = 2 * j + q - b + 1
                    if 0 <= at < 128:
                        inter[q, i2, j, i2, b, at] = 1
    table = resize_table(224, 1024)
    columns = np.zeros((3, 8, 16, 8, 128))
    for m in range(3):
        for u in range(5):
            if 3 * u + m < 14:
                for pc in range(16):
                    columns[m, u, pc] = table[14 * pc + 3 * u + m].reshape(128, 8).T
    rows = np.zeros((3, 16, 4, 8, 4, 128))
    local = table[28 * 3 : 28 * 3 + 28, 128 * 3 : 128 * 3 + 128].reshape(28, 16, 8)
    to_next = table[28 * 4, 128 * 3 : 128 * 3 + 128].reshape(16, 8)
    to_prev = table[28 * 3 - 1, 128 * 3 : 128 * 3 + 128].reshape(16, 8)
    for m in range(3):
        for c in range(3):
            for a in range(14):
                at = 42 * m + 14 * c + a
                rows[m, :, c, :, 0, at] = local[a]
                rows[m, :, c, :, 1, at] = local[14 + a]
            rows[m, :, c, :, 2, 42 * m + 14 * c] = to_next
            rows[m, :, c, :, 3, 42 * m + 14 * c + 13] = to_prev
    lanes = np.zeros((8, 128))
    lanes[0:2] = 1
    for m in range(3):
        for c in range(3):
            for a in range(14):
                at = 42 * m + 14 * c + a
                lanes[2, at] = 0.5 / PIX_STD[c]
                lanes[3, at] = (0.5 - PIX_MEAN[c]) / PIX_STD[c]
            lanes[0, 42 * m + 14 * c] = table[0, 0] / table[28, 128]
            lanes[1, 42 * m + 14 * c + 13] = table[223, 1023] / table[27, 127]
    ph = np.zeros((2, 128, 8, 32))
    for c in range(3):
        for y in range(8):
            for x in range(8):
                k = 64 * c + 8 * y + x
                if k < 128:
                    ph[0, k, x, 8 * c + y] = 1
                else:
                    ph[1, 16 + k - 128, x, 8 * c + y] = 1
    one = lambda v: jnp.asarray(v.astype(jnp.bfloat16))
    ph = ph.reshape(2, 128, 256)
    order = np.zeros((3, 14, 14, 640))
    for c in range(3):
        for a in range(14):
            for b in range(14):
                order[c, a, b, 128 * (b // 3) + 42 * (b % 3) + 14 * c + a] = 1
    back = np.zeros((160, 256))
    back[np.arange(80), 32 + np.arange(80)] = 1
    back[80 + np.arange(80), 128 + 16 + np.arange(80)] = 1
    tail = np.zeros((80, 128))
    tail[np.arange(80), np.arange(80)] = 1
    wide = np.zeros((16, 40, 16, 48))
    for k in range(16):
        wide[k, np.arange(40), k, np.arange(40)] = 1
    return (
        one(perm), one(perm.T), one(inter.reshape(256, 768)),
        one(columns.reshape(384, 1024)), one(rows.reshape(1536, 512)),
        one(ph[0]), one(ph[1]), jnp.asarray(lanes.astype(np.float32)),
        one(order.reshape(588, 640)), one(wide.reshape(640, 768)), one(back), one(tail),
    )


def raw_shards(proj, conv, head, patch, attn_in, attn_out, mlp_in, mlp_bias, mlp_out, vit):
    conv_t = conv.reshape(144, 16).T
    return (
        proj.T, conv_t, head, patch.T, attn_in, attn_out.T, mlp_in.T, mlp_bias[None], mlp_out, vit
    )


def run_step(shards, fetch, grad_shape, hidden, sigma, small, consts):
    vm, dma = pltpu.VMEM, pltpu.SemaphoreType.DMA
    scratch = [
        vm((512, 3072), BF16), vm((512, 3072), BF16),
        vm((8, 16, 128), BF16), vm((16, 16, 128), BF16), vm((176, 128), BF16), vm((6, 48, 128), BF16),
        vm((8, NF, 16, 128), BF16), vm((16, NF, 16, 128), BF16),
        vm((2, NZ, 2, 176, 128), BF16), vm((2, NZ, 6, 48, 128), BF16),
        vm((48, WIDE), F32), vm((48, WIDTH), F32),
        vm((3072, 128), BF16), vm((48, 2304), BF16), vm((2, 48, 128), BF16), vm((2, 48, 128), BF16),
        vm((512, LANES), F32), vm((512, LANES), F32), vm((2, 512, 128), F32),
        vm((2, 2, 512), F32), vm((2, NS, 2, 512), F32),
        vm((256, LANES), BF16), vm((512, 1024), BF16), vm((256, 512), BF16), vm((512, 256), BF16),
        vm((2, 2, 80, 128), F32), vm((2, 2, 80, 128), F32),
        vm((2, WIDE), F32), vm((NS, 2, WIDE), F32), vm((32, WIDE), F32),
        vm((NS, 2, WIDE), F32), vm((NS, 2, WIDE), F32),
        vm((1, WIDE), F32), vm((2, NS, 1, WIDE), F32),
        vm((3, 2, WIDE), F32), vm((3, 2, NS, 2, WIDE), F32), vm((2, 1, 1024), F32),
        vm((4, WIDE), F32), vm((NS, 4, WIDE), F32),
        vm((2, WIDE), F32), vm((NS, 2, WIDE), F32),
        vm((2, 16, 128), F32), vm((2, 16, 128), F32),
        vm((16, 16, 768), F32), vm((16, 16, 768), BF16), vm((16, 16, 768), BF16),
        vm((NF, 4, 128), F32), vm((NF, 4, 128), F32), vm((16, 4, 128), F32),
        dma((14, 15)), dma((14, 15)), dma((1,)),
        dma((2,)), dma((2,)), dma((2, NS - 1)), dma((2, NS - 1)), dma((2,)), dma((2,)),
        dma((4,)), dma((2,)), dma((2, 16)), dma((2, 16)), dma((2, 2)),
        dma((15,)), dma((15,)), dma((31,)), dma((31,)), dma((15,)), dma((15,)),
    ]
    count = len(shards)

    def kernel(hidden_ref, *refs):
        mods, noisy, sigma_ref = refs[count : count + 3]
        step_kernel(
            fetch, hidden_ref, refs[:count], mods, noisy, sigma_ref, *refs[count + 3 :]
        )

    return pl.pallas_call(
        kernel,
        out_shape=[jax.ShapeDtypeStruct(grad_shape, F32), jax.ShapeDtypeStruct((8, 128), F32)],
        in_specs=[ANY] + [VMEM] * (count + 2) + [SMEM] + [VMEM] * (len(small) - 2 + len(consts)),
        out_specs=[VMEM, VMEM],
        scratch_shapes=scratch,
        compiler_params=pltpu.CompilerParams(
            collective_id=0, has_side_effects=True, vmem_limit_bytes=60 * 1024 * 1024
        ),
        name="step",
    )(hidden, *shards, *small[:2], sigma, *small[2:], *consts)


def flow_sigma(step_index):
    remain = 1.0 - step_index.astype(F32) / STEPS
    return 3.0 * remain / (1.0 + 2.0 * remain)


def prepare(
    modulation, noisy, proj_bias, conv_bias, norm_gain, norm_shift, head_bias,
    position, class_token, vit_gain, vit_shift, attn_out_bias, mlp_out_bias, text_embed,
):
    flat = jnp.concatenate(
        [
            conv_bias, norm_gain, norm_shift, head_bias, proj_bias,
            class_token, attn_out_bias, mlp_out_bias, jnp.zeros((512,), F32),
        ]
    )
    return (
        modulation[0], noisy.reshape(512, 64), flat.reshape(48, 128), vit_gain, vit_shift, position,
        text_embed,
    )


def local(
    hidden, modulation, noisy, step_index, proj_weight, proj_bias, conv_weight, conv_bias,
    norm_gain, norm_shift, head_weight, head_bias, patch_weight, position, class_token,
    vit_gain, vit_shift, attn_in, attn_out, attn_out_bias, mlp_in, mlp_in_bias, mlp_out,
    mlp_out_bias, vit_proj, text_embed,
):
    shards = raw_shards(
        proj_weight, conv_weight, head_weight, patch_weight, attn_in, attn_out, mlp_in,
        mlp_in_bias, mlp_out, vit_proj,
    )
    small = prepare(
        modulation, noisy, proj_bias, conv_bias, norm_gain, norm_shift, head_bias, position,
        class_token, vit_gain, vit_shift, attn_out_bias, mlp_out_bias, text_embed,
    )
    grad, score = run_step(
        shards, True, (96, 64), hidden.reshape(512, 3072), flow_sigma(step_index).reshape(1, 1),
        small, constants(),
    )
    return grad, score[0, 0:1]


def solution(mesh):
    placed = (
        P(("fsdp", "grp"), "slab", None, None),
        P(("fsdp", "grp"), None, None),
        P(("fsdp", "grp"), "slab", None, None),
        P(("fsdp", "grp")),
        P("fsdp", None),
        P(),
        P(None, None, None, "fsdp"),
        P(),
        P(),
        P(),
        P("fsdp", None),
        P(),
        P(None, "fsdp"),
        P("slab", None),
        P(),
        P(),
        P(),
        P("fsdp", "slab"),
        P("slab", "fsdp"),
        P(),
        P(None, ("fsdp", "slab")),
        P(("fsdp", "slab")),
        P(("fsdp", "slab"), None),
        P(),
        P("fsdp", None),
        P(("fsdp", "grp"), None),
    )
    return jax.shard_map(
        local,
        mesh=mesh,
        in_specs=placed,
        out_specs=(P("fsdp", None), P(("fsdp", "grp"))),
        check_vma=False,
    )
```
